128 devices in a mesh: ty: 8 (over z, core), tx: 16 (over y, x).
Axes of the slice: x: 4, y: 4, z: 4, core: 2. Of those that a mesh axis runs over, the one named last changes fastest.
Arguments:
- lam_tracer: float32 [16, 256, 4096], P(None, 'ty', 'tx'), may hold values from -6 to 6
- lam_eta: float32 [256, 4096], P('ty', 'tx'), may hold values from -60 to 60
- land: int32 [256, 4096], P('ty', 'tx'), may hold values 0 or 1
- zonal_flow: float32 [2, 16, 256, 4096], P(None, None, 'ty', 'tx'), may hold values from -1.5 to 1.5
- merid_flow: float32 [2, 16, 256, 4096], P(None, None, 'ty', 'tx'), may hold values from -1.5 to 1.5
- zonal_mixing: float32 [16, 256, 4096], P(None, 'ty', 'tx'), may hold values from 0.02 to 0.12
- merid_mixing: float32 [16, 256, 4096], P(None, 'ty', 'tx'), may hold values from 0.02 to 0.12
- surface_east: float32 [256, 4096], P('ty', 'tx'), may hold values from 1 to 8
- surface_north: float32 [256, 4096], P('ty', 'tx'), may hold values from 1 to 8
- surface_diag: float32 [256, 4096], P('ty', 'tx'), may hold values from 0.2 to 1
- steric: float32 [16], replicated, may hold values from 0.2 to 1
- eta_saved: float32 [256, 4096], P('ty', 'tx'), may hold values from -6 to 6
- obs_sla: float32 [131072, 128], P(('ty', 'tx')), may hold values from -6 to 6
- obs_weight: float32 [131072, 128], P(('ty', 'tx')), may hold values from 0.05 to 0.5
- obs_tile: int32 [131072, 1], P(('ty', 'tx')), may hold values from 0 to 127; in each aligned block of 1024 rows (0 to 1023, 1024 to 2047, ...) at most 16 rows name the same one
- obs_start: int32 [131072], P(('ty', 'tx')), may hold values from 0 to 8064, as said below
- obs_count: int32 [131072], P(('ty', 'tx')), may hold values from 1 to 128
Outputs:
- lam_tracer_start: float32 [16, 256, 4096], P(None, 'ty', 'tx')
- lam_eta_start: float32 [256, 4096], P('ty', 'tx')
The draws below stay inside these ranges and needn't reach their ends.
Inputs may be any that keep to these rules, and one draw needn't show every extreme that they name: `obs_tile`: in the rows of one device no tile is named by more than 16 segments, a bound that some block reaches; every tile is named somewhere. `obs_start`: A segment's 128 cells lie in one row of its tile.
All inputs are finite; a program needn't handle non-finite values. No bound on the sum of `land` on one device may be relied on, other than what follows from the above.
Results may differ from the reference program's by a relative error of at most 0.0003.
Values sent between devices are 32-bit elements; how exact they have to be, the bound alone decides.
No kernel may reach another device: no remote copies, remote signals or barrier semaphores. Data moves between devices by JAX's collectives and lax.ppermute only.
A program may use at most 64 MiB of HBM per device.

```python
import math
import jax
import jax.numpy as jnp
import numpy as np

LAT_DEV = 32
LON_DEV = 256
LEVELS = 16
ITERS = 3
SEG_POINTS = 128
SEG_DEV = 1024
NY = 256
NX = 4096
SEGMENTS = 131072
CAP = 16
N_TX = 16
DEVICES = 128


def draw_lam_eta(key, part):
    key = jax.random.fold_in(key, 11)
    lat = jnp.arange(NY, dtype=jnp.float32)[:, None] / NY
    lon = jnp.arange(NX, dtype=jnp.float32)[None, :] / NX
    base = jnp.clip(jax.random.normal(key, (NY, NX), jnp.float32), -4.0, 4.0)
    ramp = 3.0 ** lat * 3.0 ** lon
    return base * ramp


def draw_obs_start(key, part):
    key = jax.random.fold_in(key, 23)
    keys = jax.random.split(key, 4)
    rows = jax.random.randint(keys[0], (SEGMENTS,), 0, LAT_DEV)
    cols = jax.random.randint(keys[1], (SEGMENTS,), 0, LON_DEV - SEG_POINTS + 1)
    start = rows * LON_DEV + cols
    top_pos = jax.random.randint(keys[2], (), 0, SEGMENTS)
    low_pos = jax.random.randint(keys[3], (), 0, SEGMENTS)
    start = start.at[top_pos].set(LAT_DEV * LON_DEV - SEG_POINTS)
    start = start.at[low_pos].set(0)
    return start.astype(jnp.int32)


def draw_obs_count(key, part):
    key = jax.random.fold_in(key, 37)
    keys = jax.random.split(key, 3)
    count = jax.random.randint(keys[0], (SEGMENTS,), 1, SEG_POINTS + 1)
    top_pos = jax.random.randint(keys[1], (), 0, SEGMENTS)
    low_pos = jax.random.randint(keys[2], (), 0, SEGMENTS)
    count = count.at[top_pos].set(SEG_POINTS)
    count = count.at[low_pos].set(1)
    return count.astype(jnp.int32)


def place_ends(drawn, key, low, top_value):
    longest = drawn.shape.index(max(drawn.shape))
    spots = []
    for shift in (0, 1):
        where = [jax.random.randint(jax.random.fold_in(key, axis), (), 0, length) for axis, length in enumerate(drawn.shape)]
        where[longest] = (where[longest] + shift) % drawn.shape[longest]
        spots.append(tuple(where))
    return drawn.at[spots[0]].set(low).at[spots[1]].set(top_value)


def block_levels(rng, dims, cuts, smallest, largest):
    gain, own = 1.0, jax.random.fold_in(rng, 6)
    for axis_at, blocks in cuts:
        heights = jnp.exp(jax.random.uniform(jax.random.fold_in(own, axis_at), (blocks,), jnp.float32, smallest / len(cuts), largest / len(cuts)))
        gain = gain * jnp.repeat(heights, dims[axis_at] // blocks).reshape([-1 if axis == axis_at else 1 for axis in range(len(dims))])
    return gain


def assign_block(rng, own, number, rows, count, top, limit, slope):
    ranking = jax.random.permutation(rng, count)
    heavy_load, ordinary = shares(count, rows * top, limit, slope, True), shares(count, rows * top, limit, slope, False)
    places = jnp.arange(count)

    def named(sizes, offset_by):
        used = int((sizes > 0).sum())
        fixed = max(1, used // 4)
        passed = fixed + (places - fixed + offset_by * (used - fixed)) % max(1, count - fixed)
        return jnp.zeros((count,), jnp.int32).at[ranking[jnp.where(places < fixed, places, passed)]].set(jnp.asarray(sizes, jnp.int32))

    sizes = jnp.where(number % 4 == 0, named(heavy_load, number // 4), named(ordinary, number - number // 4 - 1))
    mixed = jax.random.permutation(jax.random.fold_in(own, 3), count)
    source_of, taker = mixed[0:count // 2 * 2:2], mixed[1:count // 2 * 2:2]
    slack = jnp.minimum(sizes[source_of] - 1, limit - sizes[taker]) // 2
    slack = jnp.where((source_of == ranking[0]) | (taker == ranking[0]) | (sizes[taker] == 0), 0, jnp.maximum(slack, 0))
    passed = jax.random.randint(jax.random.fold_in(own, 4), (count // 2,), 0, 1 << 20) % (slack + 1)
    sizes = sizes.at[source_of].add(-passed).at[taker].add(passed)
    labels = jnp.searchsorted(jnp.cumsum(sizes), jnp.arange(rows * top), side="right").astype(jnp.int32)
    listing = labels.reshape(top, rows).T
    listing = listing[jax.random.permutation(jax.random.fold_in(own, 1), rows)]
    offset_by = jax.random.randint(jax.random.fold_in(own, 2), (rows, 1), 0, top)
    return jnp.take_along_axis(listing, (jnp.arange(top)[None, :] + offset_by) % top, axis=1)


def shares(number_of, total, bound, skew, full):
    weights = [(1 << 20) // math.isqrt(standing ** skew) + 1 for standing in range(1, number_of + 1)]
    largest = bound if full else min(bound, max(-(-total // number_of), total * weights[0] // sum(weights)))
    least = 1 if total - largest >= number_of - 1 else 0
    counts, spare = [largest] + [least] * (number_of - 1), total - largest - least * (number_of - 1)
    while spare > 0:
        free = [i for i in range(1, number_of) if counts[i] < largest] or [i for i in range(1, number_of) if counts[i] < bound]
        pool, budget = sum([weights[i] for i in free]), spare
        for i in free:
            more = min(bound - counts[i], max(1, budget * weights[i] // pool), spare)
            counts[i] = counts[i] + more
            spare = spare - more
    return np.array(counts)


def bell_draw(rng, dims, spread, most, cuts=(), kind=jnp.bfloat16):
    array = jax.random.normal(rng, dims, jnp.float32) * spread
    if len(cuts) > 0:
        array = block_levels(rng, dims, cuts, -0.22, 0.18) * array
    return jnp.clip(array, min=-most, max=most).astype(kind)


def setup_inputs(seed: int = 0) -> dict:
    streams_of = jax.random.split(jax.random.key(seed), 18)
    lam_tracer = bell_draw(streams_of[0], (LEVELS, NY, NX), 1.0, 6.0, ((1, 8), (2, 16)), jnp.float32)
    lam_eta = draw_lam_eta(jax.random.fold_in(streams_of[17], 71), 0)
    land = place_ends((jax.random.randint(streams_of[2], (NY, NX), 0, 8) < 7).astype(jnp.int32), jax.random.fold_in(streams_of[2], 1), 0, 1)
    zonal_flow = bell_draw(streams_of[3], (2, LEVELS, NY, NX), 0.1, 1.5, ((2, 8), (3, 16)), jnp.float32)
    merid_flow = bell_draw(streams_of[4], (2, LEVELS, NY, NX), 0.1, 1.5, ((2, 8), (3, 16)), jnp.float32)
    zonal_mixing = jnp.clip(0.02 + 0.09999999776482582 * jax.random.uniform(streams_of[5], (LEVELS, NY, NX), jnp.float32) ** block_levels(streams_of[5], (LEVELS, NY, NX), ((1, 8), (2, 16)), -0.2, 0.2), 0.02, 0.12)
    merid_mixing = jnp.clip(0.02 + 0.09999999776482582 * jax.random.uniform(streams_of[6], (LEVELS, NY, NX), jnp.float32) ** block_levels(streams_of[6], (LEVELS, NY, NX), ((1, 8), (2, 16)), -0.2, 0.2), 0.02, 0.12)
    surface_east = jnp.clip(jnp.exp(math.log(8.0) - 2.0794415 * jax.random.uniform(streams_of[7], (NY, NX), jnp.float32) ** block_levels(streams_of[7], (NY, NX), ((0, 8), (1, 16)), -0.2, 0.2)), 1.0, 8.0)
    surface_north = jnp.clip(jnp.exp(math.log(8.0) - 2.0794415 * jax.random.uniform(streams_of[8], (NY, NX), jnp.float32) ** block_levels(streams_of[8], (NY, NX), ((0, 8), (1, 16)), -0.2, 0.2)), 1.0, 8.0)
    surface_diag = jnp.clip(jnp.exp(math.log(1.0) - 1.609438 * jax.random.uniform(streams_of[9], (NY, NX), jnp.float32) ** block_levels(streams_of[9], (NY, NX), ((0, 8), (1, 16)), -0.2, 0.2)), 0.2, 1.0)
    steric = jnp.clip(jnp.exp(jax.random.uniform(streams_of[10], (LEVELS,), jnp.float32, math.log(0.2), math.log(1.0))), 0.2, 1.0)
    eta_saved = bell_draw(streams_of[11], (NY, NX), 1.0, 6.0, ((0, 8), (1, 16)), jnp.float32)
    obs_sla = bell_draw(streams_of[12], (SEGMENTS, SEG_POINTS), 1.0, 6.0, ((0, 128),), jnp.float32)
    obs_weight = jnp.clip(jnp.exp(math.log(0.5) - 2.3025851 * jax.random.uniform(streams_of[13], (SEGMENTS, SEG_POINTS), jnp.float32) ** block_levels(streams_of[13], (SEGMENTS, SEG_POINTS), ((0, 128),), -0.2, 0.2)), 0.05, 0.5)
    obs_tile_keys = jax.random.split(jax.random.fold_in(streams_of[14], 1), SEGMENTS // SEG_DEV)
    obs_tile_turns = jax.random.permutation(jax.random.fold_in(streams_of[14], 3), SEGMENTS // SEG_DEV)
    obs_tile = jax.vmap(lambda own, number: assign_block(jax.random.fold_in(streams_of[14], 2), own, number, SEG_DEV, DEVICES, 1, CAP, 2))(obs_tile_keys, obs_tile_turns).reshape((SEGMENTS, 1))
    obs_start = draw_obs_start(jax.random.fold_in(streams_of[17], 71), 0)
    obs_count = draw_obs_count(jax.random.fold_in(streams_of[17], 71), 0)
    return {"lam_tracer": lam_tracer, "lam_eta": lam_eta, "land": land, "zonal_flow": zonal_flow, "merid_flow": merid_flow, "zonal_mixing": zonal_mixing, "merid_mixing": merid_mixing, "surface_east": surface_east, "surface_north": surface_north, "surface_diag": surface_diag, "steric": steric, "eta_saved": eta_saved, "obs_sla": obs_sla, "obs_weight": obs_weight, "obs_tile": obs_tile, "obs_start": obs_start, "obs_count": obs_count}


def east(v):
    return jnp.roll(v, -1, axis=-1)


def west(v):
    return jnp.roll(v, 1, axis=-1)


def north(v):
    return jnp.roll(v, -1, axis=-2)


def south(v):
    return jnp.roll(v, 1, axis=-2)


def surface_apply(v, surface_diag, surface_east, surface_north):
    total = (1.0 + surface_diag) * v + surface_east * (v - east(v)) + west(surface_east) * (v - west(v))
    return total + surface_north * (v - north(v)) + south(surface_north) * (v - south(v))


def conjugate(rhs, surface_diag, surface_east, surface_north):
    solved = jnp.zeros_like(rhs)
    resid = rhs
    direction = rhs
    norm_now = jnp.sum(resid * resid)
    for step in range(ITERS):
        image = surface_apply(direction, surface_diag, surface_east, surface_north)
        alpha = norm_now / jnp.sum(direction * image)
        solved = solved + alpha * direction
        resid = resid - alpha * image
        norm_next = jnp.sum(resid * resid)
        direction = resid + (norm_next / norm_now) * direction
        norm_now = norm_next
    return solved


def tracer_back(masked, zonal, merid, zonal_mix, merid_mix):
    diff_x = masked - east(masked)
    diff_y = masked - north(masked)
    result = (0.5 * zonal + zonal_mix) * diff_x + west((0.5 * zonal - zonal_mix) * diff_x)
    result = result + (0.5 * merid + merid_mix) * diff_y + south((0.5 * merid - merid_mix) * diff_y)
    return masked - result


def reference(lam_tracer, lam_eta, land, zonal_flow, merid_flow, zonal_mixing, merid_mixing, surface_east, surface_north, surface_diag, steric, eta_saved, obs_sla, obs_weight, obs_tile, obs_start, obs_count):
    rows_all = jnp.arange(NY, dtype=jnp.int32)[:, None]
    open_rows = (rows_all < NY - 1).astype(jnp.float32)
    merid_flow = merid_flow * open_rows
    merid_mixing = merid_mixing * open_rows
    surface_north = surface_north * open_rows
    ocean = land.astype(jnp.float32)
    target = obs_tile[:, 0]
    row_first = (target // N_TX) * LAT_DEV + obs_start // LON_DEV
    col_first = (target % N_TX) * LON_DEV + obs_start % LON_DEV
    offsets = jnp.arange(SEG_POINTS, dtype=jnp.int32)
    cells = (row_first * NX + col_first)[:, None] + offsets[None, :]
    live = offsets[None, :] < obs_count[:, None]
    eta_at = eta_saved.reshape(-1)[cells]
    term = jnp.where(live, obs_weight * (eta_at - obs_sla), jnp.float32(0.0))
    forcing = jnp.zeros((NY * NX,), jnp.float32).at[cells.reshape(-1)].add(term.reshape(-1)).reshape(NY, NX)
    mu_eta = lam_eta + forcing
    mu_tracer = lam_tracer
    for step in (1, 0):
        rho = conjugate(ocean * mu_eta, surface_diag, surface_east, surface_north)
        mu_eta = rho
        masked = ocean[None] * (mu_tracer + steric[:, None, None] * rho[None])
        mu_tracer = tracer_back(masked, zonal_flow[step], merid_flow[step], zonal_mixing, merid_mixing)
    return mu_tracer, mu_eta
```

```python
import jax
import jax.numpy as jnp
from jax import lax
from jax.sharding import PartitionSpec as P

AXES = ("ty", "tx")
SHIFT_0 = 1.6
SHIFT_1 = 35.0
SCALE_0 = 1.0 / 32.0
SCALE_1 = 1.0 / 16.0


def beside(cells, axis, step):
    count = lax.axis_size(axis)
    return lax.ppermute(cells, axis, [((i + step) % count, i) for i in range(count)])


def ringed(field, rows, cols):
    north = beside(field[..., :rows, :], "ty", 1)
    south = beside(field[..., -rows:, :], "ty", -1)
    field = jnp.concatenate([field, north, south], axis=-2)
    east = beside(field[..., :cols], "tx", 1)
    west = beside(field[..., -cols:], "tx", -1)
    return jnp.concatenate([field, east, west], axis=-1)


def east(v):
    return jnp.roll(v, -1, axis=-1)


def west(v):
    return jnp.roll(v, 1, axis=-1)


def north(v):
    return jnp.roll(v, -1, axis=-2)


def south(v):
    return jnp.roll(v, 1, axis=-2)


def krylov(apply, start):
    first = apply(start)
    one = SCALE_0 * (first - SHIFT_0 * start)
    second = apply(one)
    two = SCALE_1 * (second - SHIFT_1 * one)
    return (start, one, two), (first, second, apply(two))


def small_solve(g, b):
    d0 = g[0][0]
    l1 = g[1][0] / d0
    l2 = g[2][0] / d0
    d1 = g[1][1] - l1 * g[1][0]
    t = g[2][1] - l1 * g[2][0]
    d1_ok = d1 > 1e-6 * g[1][1]
    m2 = jnp.where(d1_ok, t / d1, 0.0)
    d2 = g[2][2] - l2 * g[2][0] - m2 * t
    y1 = b[1] - l1 * b[0]
    y2 = b[2] - l2 * b[0] - m2 * y1
    x2 = jnp.where(d2 > 1e-6 * g[2][2], y2 / d2, 0.0)
    x1 = jnp.where(d1_ok, y1 / d1, 0.0) - m2 * x2
    x0 = b[0] / d0 - l1 * x1 - l2 * x2
    return (x0, x1, x2)


def pack(obs_sla, obs_weight, obs_tile, obs_start, obs_count, devices, capacity):
    seg_dev, points = obs_sla.shape
    slots = devices * capacity
    target = obs_tile[:, 0]
    tile_hit = target[:, None] == jnp.arange(devices, dtype=jnp.int32)[None, :]
    seg_ids = jnp.arange(seg_dev, dtype=jnp.int32)
    earlier = (seg_ids[None, :] < seg_ids[:, None]).astype(jnp.bfloat16)
    before = jnp.dot(earlier, tile_hit.astype(jnp.bfloat16), preferred_element_type=jnp.float32)
    slot = jnp.sum(jnp.where(tile_hit, before, 0.0), axis=1).astype(jnp.int32)
    where_to = target * capacity + slot
    placed = where_to[None, :] == jnp.arange(slots, dtype=jnp.int32)[:, None]
    lane = jnp.arange(points, dtype=jnp.int32)[None, :]
    weight = jnp.where(lane < obs_count[:, None], obs_weight, 0.0)
    stacked = jnp.concatenate([weight, weight * obs_sla], axis=1)
    packed = jnp.dot(placed.astype(jnp.float32), stacked, precision=lax.Precision.HIGHEST)
    start = jnp.sum(jnp.where(placed, obs_start[None, :], 0), axis=1).astype(jnp.float32)
    packed = packed.reshape(devices, capacity, 2, points).transpose(0, 2, 1, 3)
    start = jnp.pad(start.reshape(devices, 1, capacity), ((0, 0), (0, 0), (0, points - capacity)))
    return jnp.concatenate(
        [packed.reshape(devices, 2 * capacity, points), start], axis=1
    ).reshape(devices, 1, (2 * capacity + 1) * points)


def unpack(got, rows, cols, capacity):
    devices = got.shape[0]
    got = got.reshape(devices, 2 * capacity + 1, -1)
    points = got.shape[2]
    slots = devices * capacity
    start = got[:, 2 * capacity, :capacity].reshape(slots).astype(jnp.int32)
    row_of = start // cols
    col_of = start % cols
    row_pick = (row_of[:, None] == jnp.arange(rows, dtype=jnp.int32)[None, :]).astype(jnp.float32)
    pair = got[:, : 2 * capacity].reshape(devices, 2, capacity, points).transpose(1, 0, 2, 3)
    pair = jnp.pad(pair.reshape(2, slots, points), ((0, 0), (0, 0), (0, cols - points)))
    for bit in range((cols - 1).bit_length()):
        flag = ((col_of >> bit) % 2 == 1)[None, :, None]
        pair = jnp.where(flag, jnp.roll(pair, 1 << bit, axis=2), pair)
    total = jnp.dot(
        row_pick.T,
        pair.transpose(1, 0, 2).reshape(slots, 2 * cols),
        precision=lax.Precision.HIGHEST,
    )
    return total[:, :cols], total[:, cols:]


def on_device(
    lam_tracer,
    lam_eta,
    land,
    zonal_flow,
    merid_flow,
    zonal_mixing,
    merid_mixing,
    surface_east,
    surface_north,
    surface_diag,
    steric,
    eta_saved,
    obs_sla,
    obs_weight,
    obs_tile,
    obs_start,
    obs_count,
):
    levels, rows, cols = lam_tracer.shape
    n_rows = lax.axis_size("ty")
    devices = n_rows * lax.axis_size("tx")
    capacity = 2 * obs_sla.shape[0] // devices
    row_ids = lax.broadcasted_iota(jnp.int32, (rows, 1), 0) + lax.axis_index("ty") * rows
    open_rows = (row_ids < rows * n_rows - 1).astype(jnp.float32)
    merid_flow = merid_flow * open_rows
    merid_mixing = merid_mixing * open_rows
    surface_north = surface_north * open_rows
    ocean = land.astype(jnp.float32)

    sent = pack(obs_sla, obs_weight, obs_tile, obs_start, obs_count, devices, capacity)
    got = lax.all_to_all(sent, AXES, split_axis=0, concat_axis=0, tiled=True)

    faces = ringed(jnp.stack([surface_diag, surface_east, surface_north, ocean]), 6, 6)
    diag, f_east, f_north, ocean_5 = faces[0], faces[1], faces[2], faces[3]
    f_west, f_south = west(f_east), south(f_north)
    centre = (1.0 + diag) + f_east + f_west + f_north + f_south

    def apply(v):
        return centre * v - f_east * east(v) - f_west * west(v) - f_north * north(v) - f_south * south(v)

    half_x, half_y = 0.5 * zonal_flow, 0.5 * merid_flow
    tracers = ringed(
        jnp.concatenate(
            [
                lam_tracer,
                half_x[1] + zonal_mixing,
                half_x[1] - zonal_mixing,
                half_y[1] + merid_mixing,
                half_y[1] - merid_mixing,
                half_x[0] - zonal_mixing,
                half_y[0] - merid_mixing,
            ]
        ),
        2,
        2,
    ).reshape(7, levels, rows + 4, cols + 4)

    weight_sum, value_sum = unpack(got, rows, cols, capacity)
    rhs = ocean * (lam_eta + (weight_sum * eta_saved - value_sum))
    rhs = ringed(rhs, 6, 6)
    w, aw = krylov(apply, rhs)
    y, ay = zip(*[krylov(apply, ocean_5 * v) for v in w])
    inner = lambda a, b: jnp.sum(a[:rows, :cols] * b[:rows, :cols])
    sums = [inner(w[i], aw[j]) for i in range(3) for j in range(i + 1)]
    sums += [inner(w[i], rhs) for i in range(3)]
    pairs = [(i, k) for k in range(3) for i in range(3)]
    sums += [inner(y[i][k], ay[j][l]) for (i, k) in pairs for (j, l) in pairs if l <= k]
    sums += [inner(y[i][k], y[j][0]) for (i, k) in pairs for j in range(3)]
    mine = jnp.pad(jnp.stack(sums), (0, 128 - len(sums)))
    every = lax.all_to_all(
        jnp.broadcast_to(mine, (devices, 1, 128)), AXES, split_axis=0, concat_axis=0, tiled=True
    )
    total = jnp.sum(every.reshape(devices, 128), axis=0)
    at = iter(range(128))
    g1 = [[total[next(at)] for j in range(i + 1)] for i in range(3)]
    b1 = [total[next(at)] for i in range(3)]
    c = small_solve(g1, b1)
    g2 = [[0.0] * 3 for k in range(3)]
    b2 = [0.0] * 3
    for i, k in pairs:
        for j, l in pairs:
            if l <= k:
                g2[k][l] = g2[k][l] + c[i] * c[j] * total[next(at)]
    for i, k in pairs:
        for j in range(3):
            b2[k] = b2[k] + c[i] * c[j] * total[next(at)]
    e = small_solve(g2, b2)
    rho_1 = c[0] * w[0] + c[1] * w[1] + c[2] * w[2]
    v = [c[0] * y[0][k] + c[1] * y[1][k] + c[2] * y[2][k] for k in range(3)]
    rho_0 = e[0] * v[0] + e[1] * v[1] + e[2] * v[2]

    def cut(field):
        field = jnp.concatenate([field[: rows + 2], field[-2:]], axis=0)
        return jnp.concatenate([field[:, : cols + 2], field[:, -2:]], axis=1)

    ocean_2 = cut(ocean_5)

    def step(tracer, rho, plus_x, minus_x, plus_y, minus_y, mask):
        g = mask * (tracer + steric[:, None, None] * rho)
        dx, dy = g - east(g), g - north(g)
        return g - (plus_x * dx + west(minus_x * dx) + plus_y * dy + south(minus_y * dy))

    mu = step(tracers[0], cut(rho_1), *tracers[1:5], ocean_2)
    out_pad = lambda f: jnp.pad(f, ((0, 0), (0, 4), (0, 4)))
    plus_x0 = out_pad(half_x[0] + zonal_mixing)
    plus_y0 = out_pad(half_y[0] + merid_mixing)
    mu = step(mu, cut(rho_0), plus_x0, tracers[5], plus_y0, tracers[6], ocean_2)
    return mu[:, :rows, :cols], rho_0[:rows, :cols]


def solution(mesh):
    in_specs = (
        P(None, "ty", "tx"),
        P("ty", "tx"),
        P("ty", "tx"),
        P(None, None, "ty", "tx"),
        P(None, None, "ty", "tx"),
        P(None, "ty", "tx"),
        P(None, "ty", "tx"),
        P("ty", "tx"),
        P("ty", "tx"),
        P("ty", "tx"),
        P(),
        P("ty", "tx"),
        P(AXES, None),
        P(AXES, None),
        P(AXES, None),
        P(AXES),
        P(AXES),
    )
    out_specs = (P(None, "ty", "tx"), P("ty", "tx"))
    return jax.shard_map(
        on_device, mesh=mesh, in_specs=in_specs, out_specs=out_specs, check_vma=False
    )
```

```python
import functools

import jax
import jax.numpy as jnp
from jax import lax
from jax.experimental import pallas as pl
from jax.experimental.pallas import tpu as pltpu
from jax.sharding import PartitionSpec as P

AXES = ("ty", "tx")
SHIFT_0 = 1.6
SHIFT_1 = 35.0
SCALE_0 = 1.0 / 32.0
SCALE_1 = 1.0 / 16.0
LANES = 128
VMEM = pl.BlockSpec(memory_space=pltpu.VMEM)
F32 = jnp.float32
BF16 = jnp.bfloat16
PARAMS = pltpu.CompilerParams(vmem_limit_bytes=40 * 1024 * 1024)


def iota(shape, axis):
    return lax.broadcasted_iota(jnp.int32, shape, axis)


def split(x):
    hi = x.astype(BF16)
    return hi, (x - hi.astype(F32)).astype(BF16)


def pack_kernel(capacity, sla_ref, weight_ref, tile_ref, start_ref, count_ref, out_ref, data_ref):
    blocks = tile_ref.shape[0]
    devices = LANES
    chunk = 2 * capacity + 1
    square = (LANES, LANES)
    sub, lane = iota(square, 0), iota(square, 1)
    prefix = jnp.concatenate([(sub < lane).astype(BF16), jnp.ones(square, BF16)], axis=1)
    tile, start, count = tile_ref[...], start_ref[...], count_ref[...]
    col_t = jnp.transpose((start & (LANES - 1)).astype(F32)).astype(jnp.int32)
    count_t = jnp.transpose(count.astype(F32)).astype(jnp.int32)
    carry = jnp.zeros(square, F32)
    places, hits, firsts, lasts = [], [], [], []
    for k in range(blocks):
        target = tile[k : k + 1]
        hit = sub == target
        hits.append(hit.astype(F32).astype(BF16))
        both = jnp.dot(hits[-1], prefix, preferred_element_type=F32)
        slot = jnp.sum(jnp.where(hit, both[:, :LANES] + carry, 0.0), axis=0, keepdims=True)
        carry = carry + both[:, LANES:]
        slot = slot.astype(jnp.int32)
        places.append(target * capacity + slot)
        begin = start[k : k + 1]
        block_of = jnp.where(sub == slot, begin // LANES, 0)
        lane_of = jnp.where(sub == slot + 64, begin & (LANES - 1), 0)
        firsts.append((block_of + lane_of).astype(F32).astype(BF16))
        rows = slice(k * LANES, (k + 1) * LANES)
        weight = jnp.where(lane < count_t[:, k : k + 1], weight_ref[rows, :], 0.0)
        value = weight * sla_ref[rows, :]
        index = (lane - col_t[:, k : k + 1]) & (LANES - 1)
        weight = jnp.take_along_axis(weight, index, axis=1)
        value = jnp.take_along_axis(value, index, axis=1)
        data_ref[rows, :] = jnp.concatenate([*split(weight), *split(value)], axis=1)
    place = jnp.concatenate(places, axis=1)
    meta = lax.dot_general(
        jnp.concatenate(hits, axis=1),
        jnp.concatenate(firsts, axis=1),
        (((1,), (1,)), ((), ())),
        preferred_element_type=F32,
    )
    out_ref[pl.ds(2 * capacity, devices, stride=chunk), :] = meta
    group = 16
    height = group * capacity
    slots = iota((height, blocks * LANES), 0)
    for g in range(devices // group):
        pick = (slots == place - g * height).astype(F32).astype(BF16)
        moved = jnp.dot(pick, data_ref[...], preferred_element_type=F32)
        weight = moved[:, :LANES] + moved[:, LANES : 2 * LANES]
        value = moved[:, 2 * LANES : 3 * LANES] + moved[:, 3 * LANES :]
        for t in range(group):
            base = (g * group + t) * chunk
            rows = slice(t * capacity, (t + 1) * capacity)
            out_ref[base : base + capacity, :] = weight[rows]
            out_ref[base + capacity : base + 2 * capacity, :] = value[rows]


def pack(obs_sla, obs_weight, obs_tile, obs_start, obs_count, capacity):
    blocks = obs_sla.shape[0] // LANES
    chunk = 2 * capacity + 1
    return pl.pallas_call(
        functools.partial(pack_kernel, capacity),
        out_shape=jax.ShapeDtypeStruct((LANES * chunk, LANES), F32),
        in_specs=[VMEM] * 5,
        out_specs=VMEM,
        scratch_shapes=[pltpu.VMEM((blocks * LANES, 4 * LANES), BF16)],
        compiler_params=PARAMS,
        name="pack_segments",
    )(
        obs_sla,
        obs_weight,
        obs_tile.reshape(blocks, LANES),
        obs_start.reshape(blocks, LANES),
        obs_count.reshape(blocks, LANES),
    )


def unpack_kernel(capacity, got_ref, eta_ref, lam_ref, land_ref, q_ref, sum_ref):
    chunk = 2 * capacity + 1
    square = (LANES, LANES)
    lane = iota(square, 1)
    meta = got_ref[pl.ds(2 * capacity, LANES, stride=chunk), :]
    meta_t = jnp.transpose(meta)
    rows, cols = q_ref.shape
    cells = rows * cols // LANES
    blocks = iota((cells, LANES), 0).astype(F32)
    lane_f = lane.astype(F32)
    acc = jnp.zeros((cells, 4 * LANES), F32)
    for j in range(capacity):
        weight = got_ref[pl.ds(j, LANES, stride=chunk), :]
        value = got_ref[pl.ds(capacity + j, LANES, stride=chunk), :]
        here = lane_f >= meta[:, 64 + j : 65 + j]
        hit = (blocks == meta_t[j : j + 1]).astype(F32).astype(BF16)
        his, los = [], []
        for x in (weight, value):
            hi = x.astype(BF16).astype(F32)
            lo = x - hi
            for keep in (here, ~here):
                his.append(jnp.where(keep, hi, 0.0).astype(BF16))
                los.append(jnp.where(keep, lo, 0.0).astype(BF16))
        data = jnp.concatenate(
            [jnp.concatenate(his, axis=1), jnp.concatenate(los, axis=1)], axis=0
        )
        acc = acc + jnp.dot(
            jnp.concatenate([hit, hit], axis=1), data, preferred_element_type=F32
        )
    for i in range(2):
        here, after = acc[:, 2 * i * LANES : (2 * i + 1) * LANES], acc[:, (2 * i + 1) * LANES : (2 * i + 2) * LANES]
        sum_ref[i, :, :] = here + pltpu.roll(after, 1, 0)
    for half in range(2):
        at = slice(half * LANES, (half + 1) * LANES)
        weight = sum_ref[0, pl.ds(half, rows, stride=2), :]
        value = sum_ref[1, pl.ds(half, rows, stride=2), :]
        mu = lam_ref[:, at] + (weight * eta_ref[:, at] - value)
        q_ref[:, at] = land_ref[:, at].astype(F32) * mu


def unpack(got, eta, lam, land, capacity):
    return pl.pallas_call(
        functools.partial(unpack_kernel, capacity),
        out_shape=jax.ShapeDtypeStruct(eta.shape, F32),
        in_specs=[VMEM] * 4,
        out_specs=VMEM,
        scratch_shapes=[pltpu.VMEM((2, eta.size // LANES, LANES), F32)],
        compiler_params=PARAMS,
        name="forcing",
    )(got, eta, lam, land)


def two_sum(a, b):
    s = a + b
    t = s - a
    return s, (a - (s - t)) + (b - t)


def pair_sum(x, y):
    s, e = two_sum(x[0], y[0])
    e = e + (x[1] + y[1])
    return s, e


def tree(parts):
    while len(parts) > 1:
        odd = parts[len(parts) // 2 * 2 :]
        parts = [pair_sum(parts[i], parts[i + 1]) for i in range(0, len(parts) - 1, 2)] + odd
    return parts[0]


def rows_sum(hi):
    zero = jnp.zeros((8, LANES), F32)
    total = tree([(hi[8 * i : 8 * i + 8], zero) for i in range(16)])
    for step in (4, 2, 1):
        total = pair_sum(total, (pltpu.roll(total[0], step, 0), pltpu.roll(total[1], step, 0)))
    return total


def krylov(apply, start):
    first = apply(start)
    one = SCALE_0 * (first - SHIFT_0 * start)
    second = apply(one)
    two = SCALE_1 * (second - SHIFT_1 * one)
    return (start, one, two), (first, second, apply(two))


def sums_kernel(q_ref, north_ref, south_ref, east_ref, west_ref, face_ref, row_ref, field_ref, part_ref):
    rows, cols = q_ref.shape
    high, wide = rows + 16, cols + LANES
    side = jnp.where(iota((high, LANES), 1) < LANES // 2, east_ref[...], west_ref[...])
    q = jnp.concatenate(
        [jnp.concatenate([q_ref[...], north_ref[...], south_ref[...]], axis=0), side], axis=1
    )

    def apply(v):
        return (
            face_ref[0] * v
            - face_ref[1] * pltpu.roll(v, wide - 1, 1)
            - face_ref[2] * pltpu.roll(v, 1, 1)
            - face_ref[3] * pltpu.roll(v, high - 1, 0)
            - face_ref[4] * pltpu.roll(v, 1, 0)
        )

    def inner(at, a, b):
        p = a[:rows, :cols] * b[:rows, :cols]
        p = (p[0:8] + p[8:16]) + (p[16:24] + p[24:32])
        part_ref[8 * at : 8 * at + 8, :] = p[:, :LANES] + p[:, LANES:]

    w, aw = krylov(apply, q)
    y, ay = zip(*[krylov(apply, face_ref[5] * v) for v in w])
    for i in range(3):
        field_ref[i] = w[i]
        field_ref[3 + 2 * i] = y[i][1]
        field_ref[4 + 2 * i] = y[i][2]
    orders = [(k, l) for k in range(3) for l in range(k + 1)]
    at = 0
    for i in range(3):
        for j in range(3):
            for k, l in orders:
                inner(at, y[i][k], ay[j][l])
                at += 1
            for k in range(3):
                inner(at, y[i][k], y[j][0])
                at += 1
    for k, l in orders:
        inner(at, w[k], aw[l])
        at += 1
    for k in range(3):
        inner(at, w[k], q)
        at += 1
    part_ref[8 * at :, :] = jnp.zeros((8 * (LANES - at), LANES), F32)
    zero = jnp.zeros((LANES, LANES), F32)
    pieces = [(part_ref[pl.ds(s, LANES, stride=8), :], zero) for s in range(8)]
    hi, lo = tree(pieces)
    hi, lo = jnp.transpose(hi), jnp.transpose(lo)
    total = rows_sum(hi)
    row = total[0] + (total[1] + rows_sum(lo)[0])
    row_ref[...] = jnp.broadcast_to(row[0:1], row_ref.shape)


def sums(q, north, south, east, west, faces):
    rows, cols = q.shape
    high, wide = rows + 16, cols + LANES
    return pl.pallas_call(
        sums_kernel,
        out_shape=(
            jax.ShapeDtypeStruct((LANES, LANES), F32),
            jax.ShapeDtypeStruct((9, high, wide), F32),
        ),
        in_specs=[VMEM] * 6,
        out_specs=(VMEM, VMEM),
        scratch_shapes=[pltpu.VMEM((8 * LANES, LANES), F32)],
        compiler_params=PARAMS,
        name="krylov_sums",
    )(q, north, south, east, west, faces)


def two_prod(a, b):
    p = a * b
    t = 4097.0 * a
    ah = t - (t - a)
    al = a - ah
    t = 4097.0 * b
    bh = t - (t - b)
    bl = b - bh
    return p, ((ah * bh - p) + (ah * bl + al * bh)) + al * bl


def quick(s, e):
    t = s + e
    return t, e - (t - s)


def pair_add(x, y):
    s, e = two_sum(x[0], y[0])
    return quick(s, e + (x[1] + y[1]))


def pair_neg(x):
    return -x[0], -x[1]


def pair_mul(x, y):
    p, e = two_prod(x[0], y[0])
    return quick(p, e + (x[0] * y[1] + x[1] * y[0]))


def pair_div(x, y):
    first = x[0] / y[0]
    p, e = two_prod(first, y[0])
    rest = ((x[0] - p) - e) + (x[1] - first * y[1])
    return quick(first, rest / y[0])


def pair_where(ok, x):
    return jnp.where(ok, x[0], 0.0), jnp.where(ok, x[1], 0.0)


def small_solve(g, b):
    sub = lambda x, y: pair_add(x, pair_neg(y))
    l1 = pair_div(g[1], g[0])
    l2 = pair_div(g[3], g[0])
    d1 = sub(g[2], pair_mul(l1, g[1]))
    t = sub(g[4], pair_mul(l1, g[3]))
    ok1 = d1[0] > 1e-10 * g[2][0]
    m2 = pair_where(ok1, pair_div(t, d1))
    d2 = sub(sub(g[5], pair_mul(l2, g[3])), pair_mul(m2, t))
    y1 = sub(b[1], pair_mul(l1, b[0]))
    y2 = sub(sub(b[2], pair_mul(l2, b[0])), pair_mul(m2, y1))
    x2 = pair_where(d2[0] > 1e-10 * g[5][0], pair_div(y2, d2))
    x1 = sub(pair_where(ok1, pair_div(y1, d1)), pair_mul(m2, x2))
    x0 = sub(sub(pair_div(b[0], g[0]), pair_mul(l1, x1)), pair_mul(l2, x2))
    return x0, x1, x2


def coefficients(every_ref):
    total = rows_sum(every_ref[...])
    total = quick(*total)
    lane = iota((8, LANES), 1)

    def pick(x, at):
        return tuple(jnp.sum(jnp.where(lane == at, v, 0.0), axis=1, keepdims=True) for v in x)

    wide = lambda x: tuple(jnp.broadcast_to(v, (8, LANES)) for v in x)
    first = [wide(pick(total, 81 + m)) for m in range(9)]
    c = small_solve(first[:6], first[6:])
    system = None
    for i in range(3):
        for j in range(3):
            shift = (LANES - 9 * (3 * i + j)) % LANES
            row = tuple(pltpu.roll(v, shift, 1) if shift else v for v in total)
            term = pair_mul(row, pair_mul(c[i], c[j]))
            system = term if system is None else pair_add(system, term)
    second = [wide(pick(system, m)) for m in range(9)]
    e = small_solve(second[:6], second[6:])
    return [v[0] for v in c], [v[0] for v in e]


def tracer_kernel(steric_ref, every_ref, field_ref, ocean_ref, lam_ref, one_ref, zero_ref, mu_ref, rho_ref, scratch_ref):
    rows, cols = rho_ref.shape
    high, wide = rows + 8, cols + LANES
    level = pl.program_id(0)

    def trim(v):
        edge = jnp.where(iota((8, wide), 0) < 4, v[rows : rows + 8], v[rows + 8 :])
        return jnp.concatenate([v[:rows], edge], axis=0)

    @pl.when(level == 0)
    def _():
        c, e = coefficients(every_ref)
        c, e = [v[0:1, 0:1] for v in c], [v[0:1, 0:1] for v in e]
        w = [field_ref[i] for i in range(3)]
        rho_1 = c[0] * w[0] + c[1] * w[1] + c[2] * w[2]
        rho_0 = e[0] * (ocean_ref[...] * rho_1)
        for k in (1, 2):
            v = c[0] * field_ref[2 + k] + c[1] * field_ref[4 + k] + c[2] * field_ref[6 + k]
            rho_0 = rho_0 + e[k] * v
        rho_ref[...] = rho_0[:rows, :cols]
        scratch_ref[0] = trim(rho_1)
        scratch_ref[1] = trim(rho_0)
        scratch_ref[2] = trim(ocean_ref[...])

    height = steric_ref[level]
    ocean = scratch_ref[2]

    def near(g):
        return (
            pltpu.roll(g, wide - 1, 1),
            pltpu.roll(g, 1, 1),
            pltpu.roll(g, high - 1, 0),
            pltpu.roll(g, 1, 0),
        )

    g = ocean * (lam_ref[0] + height * scratch_ref[0])
    e, w, n, s = near(g)
    mu = g - (
        one_ref[0, 0] * (g - e) + one_ref[1, 0] * (w - g) + one_ref[2, 0] * (g - n) + one_ref[3, 0] * (s - g)
    )
    g = ocean * (mu + height * scratch_ref[1])
    e, w, n, s = [v[:rows, :cols] for v in near(g)]
    g = g[:rows, :cols]
    mu_ref[0] = g - (
        zero_ref[0, 0] * (g - e) + zero_ref[1, 0] * (w - g) + zero_ref[2, 0] * (g - n) + zero_ref[3, 0] * (s - g)
    )


def tracers(steric, every, fields, ocean, lam, one, zero):
    levels, high, wide = lam.shape
    rows, cols = high - 8, wide - LANES
    whole = lambda shape: pl.BlockSpec(shape, lambda k: (0,) * len(shape))
    return pl.pallas_call(
        tracer_kernel,
        grid=(levels,),
        out_shape=(
            jax.ShapeDtypeStruct((levels, rows, cols), F32),
            jax.ShapeDtypeStruct((rows, cols), F32),
        ),
        in_specs=[
            pl.BlockSpec(memory_space=pltpu.SMEM),
            whole(every.shape),
            whole(fields.shape),
            whole(ocean.shape),
            pl.BlockSpec((1, high, wide), lambda k: (k, 0, 0)),
            pl.BlockSpec((4, 1, high, wide), lambda k: (0, k, 0, 0)),
            pl.BlockSpec((4, 1, rows, cols), lambda k: (0, k, 0, 0)),
        ],
        out_specs=(pl.BlockSpec((1, rows, cols), lambda k: (k, 0, 0)), whole((rows, cols))),
        scratch_shapes=[pltpu.VMEM((3, high, wide), F32)],
        compiler_params=PARAMS,
        name="tracer_steps",
    )(steric, every, fields, ocean, lam, one, zero)


def beside(cells, axis, step):
    count = lax.axis_size(axis)
    return lax.ppermute(cells, axis, [((i + step) % count, i) for i in range(count)])


def stretched(field, width, rows_to, cols_to):
    top, bottom = field[..., :width, :], field[..., -width:, :]
    north, south = beside(top, "ty", 1), beside(bottom, "ty", -1)
    gap = jnp.zeros(field.shape[:-2] + (rows_to - 2 * width, field.shape[-1]), F32)
    field = jnp.concatenate([field, north, gap, south], axis=-2)

    def strip(cells, step):
        flat = jnp.moveaxis(cells, -1, 0)
        sent = beside(flat.reshape(-1, LANES) if flat.size % LANES == 0 else flat.reshape(-1), "tx", step)
        return jnp.moveaxis(sent.reshape(flat.shape), 0, -1)

    east, west = strip(field[..., :width], 1), strip(field[..., -width:], -1)
    gap = jnp.zeros(field.shape[:-1] + (cols_to - 2 * width,), F32)
    return jnp.concatenate([field, east, gap, west], axis=-1)


def west_of(v):
    return jnp.roll(v, 1, axis=-1)


def south_of(v):
    return jnp.roll(v, 1, axis=-2)


def on_device(
    lam_tracer,
    lam_eta,
    land,
    zonal_flow,
    merid_flow,
    zonal_mixing,
    merid_mixing,
    surface_east,
    surface_north,
    surface_diag,
    steric,
    eta_saved,
    obs_sla,
    obs_weight,
    obs_tile,
    obs_start,
    obs_count,
):
    levels, rows, cols = lam_tracer.shape
    n_rows = lax.axis_size("ty")
    devices = n_rows * lax.axis_size("tx")
    capacity = 2 * obs_sla.shape[0] // devices
    row_ids = lax.broadcasted_iota(jnp.int32, (rows, 1), 0) + lax.axis_index("ty") * rows
    open_rows = (row_ids < rows * n_rows - 1).astype(jnp.float32)

    sent = pack(obs_sla, obs_weight, obs_tile, obs_start, obs_count, capacity)
    got = lax.all_to_all(
        sent.reshape(devices, 1, -1), AXES, split_axis=0, concat_axis=0, tiled=True
    ).reshape(sent.shape)

    merid_flow = merid_flow * open_rows
    merid_mixing = merid_mixing * open_rows
    surface_north = surface_north * open_rows
    ocean = land.astype(jnp.float32)
    faces = stretched(jnp.stack([surface_diag, surface_east, surface_north, ocean]), 6, 16, LANES)
    diag, f_east, f_north, ocean_6 = faces[0], faces[1], faces[2], faces[3]
    f_west, f_south = west_of(f_east), south_of(f_north)
    centre = (1.0 + diag) + f_east + f_west + f_north + f_south
    faces = jnp.stack([centre, f_east, f_west, f_north, f_south, ocean_6])

    half_x, half_y = 0.5 * zonal_flow, 0.5 * merid_flow
    fields = stretched(
        jnp.concatenate(
            [
                lam_tracer,
                half_x[1] + zonal_mixing,
                half_x[1] - zonal_mixing,
                half_y[1] + merid_mixing,
                half_y[1] - merid_mixing,
                half_x[0] - zonal_mixing,
                half_y[0] - merid_mixing,
            ]
        ),
        2,
        8,
        LANES,
    ).reshape(7, levels, rows + 8, cols + LANES)
    lam = fields[0]
    one = jnp.stack([fields[1], west_of(fields[2]), fields[3], south_of(fields[4])])
    zero = jnp.stack(
        [
            half_x[0] + zonal_mixing,
            west_of(fields[5])[:, :rows, :cols],
            half_y[0] + merid_mixing,
            south_of(fields[6])[:, :rows, :cols],
        ]
    )

    rhs = unpack(got, eta_saved, lam_eta, land, capacity)
    north, south = beside(rhs[:8], "ty", 1), beside(rhs[-8:], "ty", -1)
    tall = jnp.concatenate([rhs, north, south], axis=0)
    east, west = beside(tall[:, :LANES], "tx", 1), beside(tall[:, -LANES:], "tx", -1)
    mine, krylov_fields = sums(rhs, north, south, east, west, faces)
    every = lax.all_to_all(
        mine.reshape(devices, 1, LANES), AXES, split_axis=0, concat_axis=0, tiled=True
    ).reshape(devices, LANES)
    return tracers(steric, every, krylov_fields, ocean_6, lam, one, zero)


def solution(mesh):
    in_specs = (
        P(None, "ty", "tx"),
        P("ty", "tx"),
        P("ty", "tx"),
        P(None, None, "ty", "tx"),
        P(None, None, "ty", "tx"),
        P(None, "ty", "tx"),
        P(None, "ty", "tx"),
        P("ty", "tx"),
        P("ty", "tx"),
        P("ty", "tx"),
        P(),
        P("ty", "tx"),
        P(AXES, None),
        P(AXES, None),
        P(AXES, None),
        P(AXES),
        P(AXES),
    )
    out_specs = (P(None, "ty", "tx"), P("ty", "tx"))
    return jax.shard_map(
        on_device, mesh=mesh, in_specs=in_specs, out_specs=out_specs, check_vma=False
    )
```

```python
import functools

import jax
import jax.numpy as jnp
from jax import lax
from jax.experimental import pallas as pl
from jax.experimental.pallas import tpu as pltpu
from jax.sharding import PartitionSpec as P

AXES = ("ty", "tx")
SHIFT_0 = 1.6
SHIFT_1 = 35.0
SCALE_0 = 1.0 / 32.0
SCALE_1 = 1.0 / 16.0
LANES = 128
VMEM = pl.BlockSpec(memory_space=pltpu.VMEM)
SCALAR = pl.BlockSpec(memory_space=pltpu.SMEM)
HBM = pl.BlockSpec(memory_space=pltpu.HBM)
F32 = jnp.float32
BF16 = jnp.bfloat16


def params(mib):
    return pltpu.CompilerParams(vmem_limit_bytes=mib * 1024 * 1024)


def iota(dims, axis):
    return lax.broadcasted_iota(jnp.int32, dims, axis)


def shape(*dims):
    return jax.ShapeDtypeStruct(dims, F32)


def far_shape(*dims):
    return pltpu.HBM(dims, F32)


def far(arrays):
    return tuple(pltpu.with_memory_space_constraint(x, pltpu.HBM) for x in arrays)


def split(x):
    hi = x.astype(BF16)
    return hi, (x - hi.astype(F32)).astype(BF16)


def rank_kernel(capacity, sla_ref, weight_ref, tile_ref, start_ref, count_ref, token_ref, data_ref, place_ref, meta_ref):
    blocks = tile_ref.shape[0]
    square = (LANES, LANES)
    sub, lane = iota(square, 0), iota(square, 1)
    prefix = jnp.concatenate([(sub < lane).astype(BF16), jnp.ones(square, BF16)], axis=1)
    tile, start, count = tile_ref[...], start_ref[...], count_ref[...]
    col_t = jnp.transpose((start & (LANES - 1)).astype(F32)).astype(jnp.int32)
    count_t = jnp.transpose(count.astype(F32)).astype(jnp.int32)
    carry = jnp.zeros(square, F32)
    hits, firsts = [], []
    for k in range(blocks):
        target = tile[k : k + 1]
        hit = sub == target
        hits.append(hit.astype(F32).astype(BF16))
        both = jnp.dot(hits[-1], prefix, preferred_element_type=F32)
        slot = jnp.sum(jnp.where(hit, both[:, :LANES] + carry, 0.0), axis=0, keepdims=True)
        carry = carry + both[:, LANES:]
        slot = slot.astype(jnp.int32)
        place_ref[k : k + 1, :] = target * capacity + slot
        begin = start[k : k + 1]
        block_of = jnp.where(sub == slot, begin // LANES, 0)
        lane_of = jnp.where(sub == slot + 64, begin & (LANES - 1), 0)
        firsts.append((block_of + lane_of).astype(F32).astype(BF16))
        rows = slice(k * LANES, (k + 1) * LANES)
        weight = jnp.where(lane < count_t[:, k : k + 1], weight_ref[rows, :], 0.0)
        value = weight * sla_ref[rows, :]
        index = (lane - col_t[:, k : k + 1]) & (LANES - 1)
        weight = jnp.take_along_axis(weight, index, axis=1)
        value = jnp.take_along_axis(value, index, axis=1)
        data_ref[rows, :] = jnp.concatenate([*split(weight), *split(value)], axis=1)
    meta_ref[...] = lax.dot_general(
        jnp.concatenate(hits, axis=1),
        jnp.concatenate(firsts, axis=1),
        (((1,), (1,)), ((), ())),
        preferred_element_type=F32,
    )


def place_kernel(capacity, data_ref, place_ref, meta_ref, token_ref, north_ref, south_ref, out_ref, next_ref, made_ref, sems):
    next_ref[...] = token_ref[...]
    blocks = place_ref.shape[0]
    devices = LANES
    chunk = 2 * capacity + 1
    made_ref[pl.ds(2 * capacity, devices, stride=chunk), :] = meta_ref[...]
    place = jnp.concatenate([place_ref[k : k + 1, :] for k in range(blocks)], axis=1)
    group = 16
    height = group * capacity
    slots = iota((height, blocks * LANES), 0)
    copies = []
    for g in range(devices // group):
        pick = (slots == place - g * height).astype(F32).astype(BF16)
        moved = jnp.dot(pick, data_ref[...], preferred_element_type=F32)
        weight = moved[:, :LANES] + moved[:, LANES : 2 * LANES]
        value = moved[:, 2 * LANES : 3 * LANES] + moved[:, 3 * LANES :]
        for t in range(group):
            base = (g * group + t) * chunk
            rows = slice(t * capacity, (t + 1) * capacity)
            made_ref[base : base + capacity, :] = weight[rows]
            made_ref[base + capacity : base + 2 * capacity, :] = value[rows]
        ready = pl.ds(g * group * chunk, group * chunk)
        copies.append(pltpu.make_async_copy(made_ref.at[ready, :], out_ref.at[ready, :], sems.at[g]))
        copies[-1].start()
    for copy in copies:
        copy.wait()


def pack(obs_sla, obs_weight, obs_tile, obs_start, obs_count, token, capacity):
    blocks = obs_sla.shape[0] // LANES
    return pl.pallas_call(
        functools.partial(rank_kernel, capacity),
        out_shape=(
            jax.ShapeDtypeStruct((blocks * LANES, 4 * LANES), BF16),
            jax.ShapeDtypeStruct((blocks, LANES), jnp.int32),
            shape(LANES, LANES),
        ),
        in_specs=[VMEM] * 6,
        out_specs=(VMEM,) * 3,
        compiler_params=params(8),
        name="rank_segments",
    )(
        obs_sla,
        obs_weight,
        obs_tile.reshape(blocks, LANES),
        obs_start.reshape(blocks, LANES),
        obs_count.reshape(blocks, LANES),
        token,
    )


def placed(data, place, meta, token, around, capacity):
    chunk = 2 * capacity + 1
    return pl.pallas_call(
        functools.partial(place_kernel, capacity),
        out_shape=(far_shape(LANES * chunk, LANES), shape(*token.shape)),
        in_specs=[VMEM] * 4 + [pl.BlockSpec(memory_space=pl.ANY)] * 2,
        out_specs=(HBM, VMEM),
        scratch_shapes=[
            pltpu.VMEM((LANES * chunk, LANES), F32),
            pltpu.SemaphoreType.DMA((LANES // 16,)),
        ],
        compiler_params=params(12),
        name="place_segments",
    )(data, place, meta, token, *around)


def unpack_kernel(capacity, got_ref, height_ref, face_ref, token_ref, q_ref, next_ref, sum_ref):
    next_ref[...] = token_ref[...]
    chunk = 2 * capacity + 1
    square = (LANES, LANES)
    lane = iota(square, 1)
    meta = got_ref[pl.ds(2 * capacity, LANES, stride=chunk), :]
    meta_t = jnp.transpose(meta)
    rows, cols = q_ref.shape
    cells = rows * cols // LANES
    blocks = iota((cells, LANES), 0).astype(F32)
    lane_f = lane.astype(F32)
    acc = jnp.zeros((cells, 4 * LANES), F32)
    for j in range(capacity):
        weight = got_ref[pl.ds(j, LANES, stride=chunk), :]
        value = got_ref[pl.ds(capacity + j, LANES, stride=chunk), :]
        here = lane_f >= meta[:, 64 + j : 65 + j]
        hit = (blocks == meta_t[j : j + 1]).astype(F32).astype(BF16)
        his, los = [], []
        for x in (weight, value):
            hi = x.astype(BF16).astype(F32)
            lo = x - hi
            for keep in (here, ~here):
                his.append(jnp.where(keep, hi, 0.0).astype(BF16))
                los.append(jnp.where(keep, lo, 0.0).astype(BF16))
        data = jnp.concatenate(
            [jnp.concatenate(his, axis=1), jnp.concatenate(los, axis=1)], axis=0
        )
        acc = acc + jnp.dot(
            jnp.concatenate([hit, hit], axis=1), data, preferred_element_type=F32
        )
    for i in range(2):
        here, after = acc[:, 2 * i * LANES : (2 * i + 1) * LANES], acc[:, (2 * i + 1) * LANES : (2 * i + 2) * LANES]
        sum_ref[i, :, :] = here + pltpu.roll(after, 1, 0)
    for half in range(2):
        at = slice(half * LANES, (half + 1) * LANES)
        weight = sum_ref[0, pl.ds(half, rows, stride=2), :]
        value = sum_ref[1, pl.ds(half, rows, stride=2), :]
        mu = height_ref[0, :, at] + (weight * height_ref[1, :, at] - value)
        q_ref[:, at] = face_ref[3, 0:rows, at] * mu


def unpack(got, heights, faces, token, capacity):
    rows, cols = heights.shape[1:]
    return pl.pallas_call(
        functools.partial(unpack_kernel, capacity),
        out_shape=(shape(rows, cols), shape(*token.shape)),
        in_specs=[VMEM] * 4,
        out_specs=(VMEM, VMEM),
        scratch_shapes=[pltpu.VMEM((2, rows * cols // LANES, LANES), F32)],
        compiler_params=params(10),
        name="forcing",
    )(got, heights, faces, token)


def two_sum(a, b):
    s = a + b
    t = s - a
    return s, (a - (s - t)) + (b - t)


def pair_sum(x, y):
    s, e = two_sum(x[0], y[0])
    e = e + (x[1] + y[1])
    return s, e


def tree(parts):
    while len(parts) > 1:
        odd = parts[len(parts) // 2 * 2 :]
        parts = [pair_sum(parts[i], parts[i + 1]) for i in range(0, len(parts) - 1, 2)] + odd
    return parts[0]


def rows_sum(hi):
    zero = jnp.zeros((8, LANES), F32)
    total = tree([(hi[8 * i : 8 * i + 8], zero) for i in range(16)])
    for step in (4, 2, 1):
        total = pair_sum(total, (pltpu.roll(total[0], step, 0), pltpu.roll(total[1], step, 0)))
    return total


def krylov(apply, start):
    first = apply(start)
    one = SCALE_0 * (first - SHIFT_0 * start)
    second = apply(one)
    two = SCALE_1 * (second - SHIFT_1 * one)
    return (start, one, two), (first, second, apply(two))


def sums_kernel(q_ref, north_ref, south_ref, east_ref, west_ref, face_ref, token_ref, row_ref, field_ref, next_ref, part_ref):
    next_ref[...] = token_ref[...]
    rows, cols = q_ref.shape
    high, wide = rows + 16, cols + LANES
    side = jnp.where(iota((high, LANES), 1) < LANES // 2, east_ref[...], west_ref[...])
    q = jnp.concatenate(
        [jnp.concatenate([q_ref[...], north_ref[...], south_ref[...]], axis=0), side], axis=1
    )

    def apply(v):
        return (
            face_ref[0] * v
            - face_ref[1] * pltpu.roll(v, wide - 1, 1)
            - face_ref[2] * pltpu.roll(v, 1, 1)
            - face_ref[3] * pltpu.roll(v, high - 1, 0)
            - face_ref[4] * pltpu.roll(v, 1, 0)
        )

    def inner(at, a, b):
        p = a[:rows, :cols] * b[:rows, :cols]
        p = (p[0:8] + p[8:16]) + (p[16:24] + p[24:32])
        part_ref[8 * at : 8 * at + 8, :] = p[:, :LANES] + p[:, LANES:]

    w, aw = krylov(apply, q)
    y, ay = zip(*[krylov(apply, face_ref[5] * v) for v in w])
    for i in range(3):
        field_ref[i] = w[i]
        field_ref[3 + 2 * i] = y[i][1]
        field_ref[4 + 2 * i] = y[i][2]
    orders = [(k, l) for k in range(3) for l in range(k + 1)]
    at = 0
    for i in range(3):
        for j in range(3):
            for k, l in orders:
                inner(at, y[i][k], ay[j][l])
                at += 1
            for k in range(3):
                inner(at, y[i][k], y[j][0])
                at += 1
    for k, l in orders:
        inner(at, w[k], aw[l])
        at += 1
    for k in range(3):
        inner(at, w[k], q)
        at += 1
    part_ref[8 * at :, :] = jnp.zeros((8 * (LANES - at), LANES), F32)
    zero = jnp.zeros((LANES, LANES), F32)
    pieces = [(part_ref[pl.ds(s, LANES, stride=8), :], zero) for s in range(8)]
    hi, lo = tree(pieces)
    hi, lo = jnp.transpose(hi), jnp.transpose(lo)
    total = rows_sum(hi)
    row = total[0] + (total[1] + rows_sum(lo)[0])
    row_ref[...] = jnp.broadcast_to(row[0:1], row_ref.shape)


def sums(q, north, south, east, west, faces, token):
    rows, cols = q.shape
    return pl.pallas_call(
        sums_kernel,
        out_shape=(shape(LANES, LANES), shape(9, rows + 16, cols + LANES), shape(*token.shape)),
        in_specs=[VMEM] * 7,
        out_specs=(VMEM,) * 3,
        scratch_shapes=[pltpu.VMEM((8 * LANES, LANES), F32)],
        compiler_params=params(8),
        name="krylov_sums",
    )(q, north, south, east, west, faces, token)


def two_prod(a, b):
    p = a * b
    t = 4097.0 * a
    ah = t - (t - a)
    al = a - ah
    t = 4097.0 * b
    bh = t - (t - b)
    bl = b - bh
    return p, ((ah * bh - p) + (ah * bl + al * bh)) + al * bl


def quick(s, e):
    t = s + e
    return t, e - (t - s)


def pair_add(x, y):
    s, e = two_sum(x[0], y[0])
    return quick(s, e + (x[1] + y[1]))


def pair_neg(x):
    return -x[0], -x[1]


def pair_mul(x, y):
    p, e = two_prod(x[0], y[0])
    return quick(p, e + (x[0] * y[1] + x[1] * y[0]))


def pair_div(x, y):
    first = x[0] / y[0]
    p, e = two_prod(first, y[0])
    rest = ((x[0] - p) - e) + (x[1] - first * y[1])
    return quick(first, rest / y[0])


def minor(a, b, c, d):
    return pair_add(pair_mul(a, b), pair_neg(pair_mul(c, d)))


def pair_sum3(a, b, c):
    return pair_add(pair_add(a, b), c)


def small_solve(g, b):
    g00, g10, g11, g20, g21, g22 = g
    c00, c01, c02 = minor(g11, g22, g21, g21), minor(g20, g21, g10, g22), minor(g10, g21, g20, g11)
    c11, c12, c22 = minor(g00, g22, g20, g20), minor(g10, g20, g00, g21), minor(g00, g11, g10, g10)
    det = pair_sum3(pair_mul(g00, c00), pair_mul(g10, c01), pair_mul(g20, c02))
    three = det[0] > 1e-8 * (c22[0] * g22[0])
    two = c22[0] > 1e-8 * (g00[0] * g11[0])
    three = three & two
    rows = ((c00, c01, c02), (c01, c11, c12), (c02, c12, c22))
    full = [pair_div(pair_sum3(*[pair_mul(m, v) for m, v in zip(row, b)]), det)[0] for row in rows]
    half = [
        pair_div(minor(g11, b[0], g10, b[1]), c22)[0],
        pair_div(minor(g00, b[1], g10, b[0]), c22)[0],
        jnp.zeros_like(det[0]),
    ]
    alone = [b[0][0] / g00[0], half[2], half[2]]
    return [jnp.where(three, x, jnp.where(two, y, z)) for x, y, z in zip(full, half, alone)]


def coefficients(every_ref):
    total = quick(*rows_sum(every_ref[...]))

    def pick(x, at):
        return tuple(jnp.broadcast_to(v[:, at : at + 1], (8, LANES)) for v in x)

    def scaled(x, at):
        by = 1.0 / jnp.broadcast_to(x[0][:, at : at + 1], (8, LANES))
        p, e = two_prod(x[0], by)
        return quick(p, e + x[1] * by)

    first = scaled(total, 81)
    first = [pick(first, 81 + m) for m in range(9)]
    c = small_solve(first[:6], first[6:])
    terms = []
    for i in range(3):
        for j in range(3):
            shift = (LANES - 9 * (3 * i + j)) % LANES
            row = tuple(pltpu.roll(v, shift, 1) if shift else v for v in total)
            terms.append(pair_mul(row, two_prod(c[i], c[j])))
    while len(terms) > 1:
        odd = terms[len(terms) // 2 * 2 :]
        terms = [pair_add(terms[i], terms[i + 1]) for i in range(0, len(terms) - 1, 2)] + odd
    second = scaled(terms[0], 0)
    second = [pick(second, m) for m in range(9)]
    return c, small_solve(second[:6], second[6:])


def tracer_kernel(steric_ref, every_ref, field_ref, face_ref, far_ref, side_ref, mu_ref, rho_ref, tall_ref, sems):
    levels, rows, cols = mu_ref.shape

    def copy(level):
        return pltpu.make_async_copy(far_ref.at[level], tall_ref.at[level], sems.at[level])

    for level in range(levels):
        copy(level).start()
    high, wide = rows + 8, cols + LANES

    def trim(v):
        edge = jnp.where(iota((8, wide), 0) < 4, v[rows : rows + 8], v[rows + 8 :])
        return jnp.concatenate([v[:rows], edge], axis=0)

    c, e = coefficients(every_ref)
    c, e = [[jnp.broadcast_to(v[0:1, 0:1], (1, 1)) for v in part] for part in (c, e)]
    w = [trim(field_ref[i]) for i in range(3)]
    ocean = trim(face_ref[5])
    rho_1 = c[0] * w[0] + c[1] * w[1] + c[2] * w[2]
    rho_0 = e[0] * (ocean * rho_1)
    for k in (1, 2):
        v = [trim(field_ref[2 + k + 2 * i]) for i in range(3)]
        rho_0 = rho_0 + e[k] * (c[0] * v[0] + c[1] * v[1] + c[2] * v[2])
    rho_ref[...] = rho_0[:rows, :cols]

    def one_level(level, carry):
        copy(level).wait()
        height = steric_ref[level]
        full = lambda at: jnp.concatenate([tall_ref[level, at], side_ref[at, level]], axis=1)
        g = ocean * (full(0) + height * rho_1)
        dx = g - pltpu.roll(g, wide - 1, 1)
        dy = g - pltpu.roll(g, high - 1, 0)
        mu = g - (
            full(1) * dx + pltpu.roll(full(2) * dx, 1, 1) + full(3) * dy + pltpu.roll(full(4) * dy, 1, 0)
        )
        g = ocean * (mu + height * rho_0)
        dx = (g - pltpu.roll(g, wide - 1, 1))[:rows]
        dy = (g - pltpu.roll(g, high - 1, 0))[:, :cols]
        back_x = pltpu.roll(full(5)[:rows] * dx, 1, 1)[:, :cols]
        back_y = pltpu.roll(tall_ref[level, 6] * dy, 1, 0)[:rows]
        mu_ref[level] = g[:rows, :cols] - (
            tall_ref[level, 7, 0:rows, :] * dx[:, :cols] + back_x + tall_ref[level, 8, 0:rows, :] * dy[:rows] + back_y
        )
        return carry

    lax.fori_loop(0, levels, one_level, 0)


def tracers(steric, every, fields, faces, tall, side):
    levels, count, high, cols = tall.shape
    rows = high - 8
    return pl.pallas_call(
        tracer_kernel,
        out_shape=(shape(levels, rows, cols), shape(rows, cols)),
        in_specs=[SCALAR] + [VMEM] * 3 + [HBM, VMEM],
        out_specs=(VMEM, VMEM),
        scratch_shapes=[pltpu.VMEM((levels, count, high, cols), F32), pltpu.SemaphoreType.DMA((levels,))],
        compiler_params=params(20),
        name="tracer_steps",
    )(steric, every, fields, faces, *far((tall,)), side)


def beside(cells, axis, step):
    count = lax.axis_size(axis)
    return lax.ppermute(cells, axis, [((i + step) % count, i) for i in range(count)])


def tracer_fields(keep, lam, zonal_1, merid_1, zonal_0, merid_0, mix_x, mix_y):
    flow_x, flow_y = 0.5 * zonal_1, 0.5 * merid_1
    past_x, past_y = 0.5 * zonal_0, 0.5 * merid_0
    return (
        lam,
        flow_x + mix_x,
        flow_x - mix_x,
        keep * (flow_y + mix_y),
        keep * (flow_y - mix_y),
        past_x - mix_x,
        keep * (past_y - mix_y),
        past_x + mix_x,
        keep * (past_y + mix_y),
    )


def surface_fields(keep, diag_ref, east_ref, north_ref, land_ref, rows):
    return diag_ref[rows], east_ref[rows], keep * north_ref[rows], land_ref[rows].astype(F32)


UP = (0, 1, 2, 3)
DOWN = (0, 1, 2, 3, 4, 6)
SIDE = (0, 1, 2, 3, 4, 5)


def kept(token_ref, first, count, rows, cols):
    last = jnp.concatenate([token_ref[0:1, :]] * (cols // LANES), axis=1)
    return jnp.where((iota((count, cols), 0) + first == rows - 1) & (last == 1.0), 0.0, 1.0)


def rows_kernel(token_ref, lam_ref, zonal_ref, merid_ref, mix_x_ref, mix_y_ref, *refs):
    surface_refs, (up_ref, down_ref, next_ref, held_ref, sems) = refs[:4], refs[4:]
    levels, rows, cols = lam_ref.shape
    next_ref[...] = token_ref[...]
    copies = []
    for first in (0, rows - 8):
        block = pl.ds(first, 8)
        for source in (
            lam_ref.at[:, block, :],
            zonal_ref.at[1, :, block, :],
            merid_ref.at[1, :, block, :],
            mix_x_ref.at[:, block, :],
            mix_y_ref.at[:, block, :],
            merid_ref.at[0, :, block, :],
        ):
            at = len(copies)
            copies.append(pltpu.make_async_copy(source, held_ref.at[at], sems.at[at]))
            copies[-1].start()
    for part, (out_ref, picks, first, take) in enumerate(((up_ref, UP, 0, 0), (down_ref, DOWN, rows - 8, 6))):
        keep = kept(token_ref, first, 8, rows, cols)
        base = 2 * len(picks) * levels
        for at, field in enumerate(surface_fields(keep, *surface_refs, slice(first, first + 8))):
            out_ref[base + 8 * at : base + 8 * at + 8, :] = field
        for copy in copies[6 * part : 6 * part + 6]:
            copy.wait()
        for level in range(levels):
            lam, zonal_1, merid_1, mix_x, mix_y, merid_0 = [held_ref[6 * part + i, level] for i in range(6)]
            fields = tracer_fields(keep, lam, zonal_1, merid_1, zonal_1, merid_0, mix_x, mix_y)
            for at, pick in enumerate(picks):
                base = 2 * (at * levels + level)
                out_ref[base : base + 2, :] = fields[pick][take : take + 2]


def edge_rows(n_ref, s_ref, pick, levels, level, cols):
    zero = lambda count: jnp.zeros((count, cols), F32)
    north = zero(2)
    if pick in UP:
        base = 2 * (UP.index(pick) * levels + level)
        north = n_ref[base : base + 2, :]
    south = zero(2)
    if pick in DOWN:
        base = 2 * (DOWN.index(pick) * levels + level)
        south = s_ref[base : base + 2, :]
    return jnp.concatenate([north, zero(4), south], axis=0)


def halves(tall):
    lane = iota((tall.shape[0], LANES), 1)
    return jnp.where(lane < LANES // 2, tall[:, :LANES], tall[:, -LANES:])


GROUP = 4


def cols_kernel(token_ref, lam_ref, zonal_ref, merid_ref, mix_x_ref, mix_y_ref, *refs):
    surface_refs, height_refs, (n_ref, s_ref) = refs[:4], refs[4:6], refs[6:8]
    out_ref, far_ref, face_ref, height_ref, held_ref, flat_ref, tall_ref, sems, far_sems = refs[8:]
    levels, rows, cols = lam_ref.shape
    copies = []
    for group in range(levels // GROUP):
        block = pl.ds(group * GROUP, GROUP)
        for i, source in enumerate(
            (
                lam_ref.at[block],
                zonal_ref.at[1, block],
                merid_ref.at[1, block],
                zonal_ref.at[0, block],
                merid_ref.at[0, block],
                mix_x_ref.at[block],
                mix_y_ref.at[block],
            )
        ):
            copies.append(pltpu.make_async_copy(source, held_ref.at[i, block], sems.at[len(copies)]))
            copies[-1].start()
    keep = kept(token_ref, 0, rows, rows, cols)
    high = rows + 8
    used = 8 * len(SIDE)
    blocks = levels * high // LANES
    base = blocks * used
    up, down = 2 * len(UP) * levels, 2 * len(DOWN) * levels
    for at, field in enumerate(surface_fields(keep, *surface_refs, slice(0, rows))):
        tall = jnp.concatenate(
            [field, n_ref[up + 8 * at : up + 8 * at + 8, :], s_ref[down + 8 * at : down + 8 * at + 8, :]], axis=0
        )
        face_ref[at] = tall
        out_ref[base : base + rows + 16, :] = halves(tall)
        base += rows + 16
    for at, ref in enumerate(height_refs):
        height_ref[at] = ref[...]
    lane = iota((high, LANES), 1)
    far = []
    for level in range(levels):
        if level % GROUP == 0:
            for copy in copies[7 * (level // GROUP) : 7 * (level // GROUP) + 7]:
                copy.wait()
        fields = tracer_fields(keep, *[held_ref[i, level] for i in range(7)])
        mixed = jnp.zeros((high, LANES), F32)
        for pick, field in enumerate(fields):
            tall_ref[level, pick, 0:rows, :] = field
            edge = edge_rows(n_ref, s_ref, pick, levels, level, cols)
            tall_ref[level, pick, rows:high, :] = edge
            if pick in SIDE:
                at = SIDE.index(pick)
                tall = jnp.concatenate([field, edge], axis=0)
                mixed = jnp.where(lane // 8 == at, pltpu.roll(halves(tall), 4 + 8 * at, 1), mixed)
        flat_ref[level * high : (level + 1) * high, :] = mixed
        far.append(pltpu.make_async_copy(tall_ref.at[level], far_ref.at[level], far_sems.at[level]))
        far[-1].start()
    for b in range(blocks):
        turned = jnp.transpose(flat_ref[b * LANES : (b + 1) * LANES, :])
        out_ref[b * used : (b + 1) * used, :] = turned[:used]
    for copy in far:
        copy.wait()


def side_kernel(e_ref, w_ref, token_ref, side_ref, flat_ref):
    levels, high = side_ref.shape[1:3]
    used = 8 * len(SIDE)
    blocks = levels * high // LANES
    western = iota((used, LANES), 0) % 8 < 4
    for b in range(blocks):
        at = slice(b * used, (b + 1) * used)
        both = jnp.where(western, w_ref[at, :], e_ref[at, :])
        both = jnp.concatenate([both, jnp.zeros((LANES - used, LANES), F32)], axis=0)
        flat_ref[b * LANES : (b + 1) * LANES, :] = jnp.transpose(both)
    for level in range(levels):
        mixed = flat_ref[level * high : (level + 1) * high, :]
        for at in range(len(SIDE)):
            side_ref[at, level] = pltpu.roll(mixed, LANES - 4 - 8 * at, 1)


def face_halo_kernel(base, token_ref, tall_ref, e_ref, w_ref, face_ref):
    high = tall_ref.shape[1]
    eastern = iota((high, LANES), 1) < LANES // 2
    full = []
    for at in range(4):
        here = slice(base + at * high, base + (at + 1) * high)
        full.append(jnp.concatenate([tall_ref[at], jnp.where(eastern, e_ref[here, :], w_ref[here, :])], axis=1))
    diag, east, north, ocean = full
    west, south = pltpu.roll(east, 1, 1), pltpu.roll(north, 1, 0)
    face_ref[0] = (1.0 + diag) + east + west + north + south
    for at, field in enumerate((east, west, north, south, ocean)):
        face_ref[1 + at] = field


def edges_to_ty(token, tracer, surface):
    levels, rows, cols = tracer[0].shape
    up, down = 2 * len(UP) * levels + 32, 2 * len(DOWN) * levels + 32
    to_south, to_north, token = pl.pallas_call(
        rows_kernel,
        out_shape=(shape(up, cols), shape(down, cols), shape(*token.shape)),
        in_specs=[VMEM] + [HBM] * 5 + [VMEM] * 4,
        out_specs=(VMEM,) * 3,
        scratch_shapes=[pltpu.VMEM((12, levels, 8, cols), F32), pltpu.SemaphoreType.DMA((12,))],
        compiler_params=params(8),
        name="edge_rows",
    )(token, *far(tracer), *far(surface))
    return (beside(to_south, "ty", 1), beside(to_north, "ty", -1)), token


def edges_to_tx(token, tracer, surface, heights, north, south):
    levels, rows, cols = tracer[0].shape
    high = rows + 8
    side_rows = 8 * len(SIDE) * levels * high // LANES + 4 * (rows + 16)
    sides, tall, faces, heights = pl.pallas_call(
        cols_kernel,
        out_shape=(
            shape(side_rows, LANES),
            far_shape(levels, 9, high, cols),
            shape(4, rows + 16, cols),
            shape(2, rows, cols),
        ),
        in_specs=[VMEM] + [HBM] * 5 + [VMEM] * 8,
        out_specs=(VMEM, HBM, VMEM, VMEM),
        scratch_shapes=[
            pltpu.VMEM((7, levels, rows, cols), F32),
            pltpu.VMEM((levels * high, LANES), F32),
            pltpu.VMEM((levels, 9, high, cols), F32),
            pltpu.SemaphoreType.DMA((7 * levels // GROUP,)),
            pltpu.SemaphoreType.DMA((levels,)),
        ],
        compiler_params=params(24),
        name="edge_columns",
    )(token, *far(tracer), *far(surface), *far(heights), north, south)
    return (beside(sides, "tx", 1), beside(sides, "tx", -1)), tall, faces, heights


def faces_with_halo(token, tall, east, west):
    count, high, cols = tall.shape
    return pl.pallas_call(
        functools.partial(face_halo_kernel, east.shape[0] - count * high),
        out_shape=shape(6, high, cols + LANES),
        in_specs=[VMEM] * 4,
        out_specs=VMEM,
        compiler_params=params(6),
        name="surface_halos",
    )(token, tall, east, west)


def tracer_sides(token, levels, rows, east, west):
    high = rows + 8
    return pl.pallas_call(
        side_kernel,
        out_shape=shape(len(SIDE), levels, high, LANES),
        in_specs=[VMEM] * 3,
        out_specs=VMEM,
        scratch_shapes=[pltpu.VMEM((levels * high, LANES), F32)],
        compiler_params=params(8),
        name="tracer_halos",
    )(east, west, token)


def on_device(
    lam_tracer,
    lam_eta,
    land,
    zonal_flow,
    merid_flow,
    zonal_mixing,
    merid_mixing,
    surface_east,
    surface_north,
    surface_diag,
    steric,
    eta_saved,
    obs_sla,
    obs_weight,
    obs_tile,
    obs_start,
    obs_count,
):
    levels, rows, cols = lam_tracer.shape
    n_rows = lax.axis_size("ty")
    devices = n_rows * lax.axis_size("tx")
    capacity = 2 * obs_sla.shape[0] // devices
    token = jnp.full((8, LANES), lax.axis_index("ty") == n_rows - 1, F32)
    tracer = (lam_tracer, zonal_flow, merid_flow, zonal_mixing, merid_mixing)
    surface = (surface_diag, surface_east, surface_north, land)
    around_ty, token = edges_to_ty(token, tracer, surface)
    ranked = pack(obs_sla, obs_weight, obs_tile, obs_start, obs_count, token, capacity)
    sent, token = placed(*ranked, token, around_ty, capacity)
    got = lax.all_to_all(
        sent.reshape(devices, 1, -1), AXES, split_axis=0, concat_axis=0, tiled=True
    ).reshape(sent.shape)
    around_tx, tall, faces, heights = edges_to_tx(token, tracer, surface, (lam_eta, eta_saved), *around_ty)
    rhs, token = unpack(got, heights, faces, token, capacity)
    faces = faces_with_halo(token, faces, *around_tx)
    north, south = beside(rhs[:8], "ty", 1), beside(rhs[-8:], "ty", -1)
    side = halves(jnp.concatenate([rhs, north, south], axis=0))
    east, west = beside(side, "tx", 1), beside(side, "tx", -1)
    mine, krylov_fields, token = sums(rhs, north, south, east, west, faces, token)
    every = lax.all_to_all(
        mine.reshape(devices, 1, LANES), AXES, split_axis=0, concat_axis=0, tiled=True
    ).reshape(devices, LANES)
    sides = tracer_sides(token, levels, rows, *around_tx)
    return tracers(steric, every, krylov_fields, faces, tall, sides)


def solution(mesh):
    in_specs = (
        P(None, "ty", "tx"),
        P("ty", "tx"),
        P("ty", "tx"),
        P(None, None, "ty", "tx"),
        P(None, None, "ty", "tx"),
        P(None, "ty", "tx"),
        P(None, "ty", "tx"),
        P("ty", "tx"),
        P("ty", "tx"),
        P("ty", "tx"),
        P(),
        P("ty", "tx"),
        P(AXES, None),
        P(AXES, None),
        P(AXES, None),
        P(AXES),
        P(AXES),
    )
    out_specs = (P(None, "ty", "tx"), P("ty", "tx"))
    return jax.shard_map(
        on_device, mesh=mesh, in_specs=in_specs, out_specs=out_specs, check_vma=False
    )
```

```python
import functools

import jax
import jax.numpy as jnp
from jax import lax
from jax.experimental import pallas as pl
from jax.experimental.pallas import tpu as pltpu
from jax.sharding import PartitionSpec as P

AXES = ("ty", "tx")
SHIFT_0 = 1.6
SHIFT_1 = 35.0
SCALE_0 = 1.0 / 32.0
SCALE_1 = 1.0 / 16.0
LANES = 128
VMEM = pl.BlockSpec(memory_space=pltpu.VMEM)
SCALAR = pl.BlockSpec(memory_space=pltpu.SMEM)
HBM = pl.BlockSpec(memory_space=pltpu.HBM)
F32 = jnp.float32
BF16 = jnp.bfloat16


def params(mib):
    return pltpu.CompilerParams(vmem_limit_bytes=mib * 1024 * 1024)


def iota(dims, axis):
    return lax.broadcasted_iota(jnp.int32, dims, axis)


def shape(*dims):
    return jax.ShapeDtypeStruct(dims, F32)


def far_shape(*dims):
    return pltpu.HBM(dims, F32)


def far(arrays):
    return tuple(pltpu.with_memory_space_constraint(x, pltpu.HBM) for x in arrays)


def split(x):
    hi = x.astype(BF16)
    return hi, (x - hi.astype(F32)).astype(BF16)


def ranks(capacity, tile, start, count, place_ref, meta_ref):
    blocks = tile.shape[0]
    square = (LANES, LANES)
    sub, lane = iota(square, 0), iota(square, 1)
    prefix = jnp.concatenate([(sub < lane).astype(BF16), jnp.ones(square, BF16)], axis=1)
    carry = jnp.zeros(square, F32)
    hits, firsts = [], []
    for k in range(blocks):
        target = tile[k : k + 1]
        hit = sub == target
        hits.append(hit.astype(F32).astype(BF16))
        both = jnp.dot(hits[-1], prefix, preferred_element_type=F32)
        slot = jnp.sum(jnp.where(hit, both[:, :LANES] + carry, 0.0), axis=0, keepdims=True)
        carry = carry + both[:, LANES:]
        slot = slot.astype(jnp.int32)
        place_ref[k : k + 1, :] = target * capacity + slot
        begin = start[k : k + 1]
        block_of = jnp.where(sub == slot, begin // LANES, 0)
        lane_of = jnp.where(sub == slot + 64, begin & (LANES - 1), 0)
        firsts.append((block_of + lane_of).astype(F32).astype(BF16))
    meta_ref[...] = lax.dot_general(
        jnp.concatenate(hits, axis=1),
        jnp.concatenate(firsts, axis=1),
        (((1,), (1,)), ((), ())),
        preferred_element_type=F32,
    )
    col_t = jnp.transpose((start & (LANES - 1)).astype(F32)).astype(jnp.int32)
    return col_t, jnp.transpose(count.astype(F32)).astype(jnp.int32)


def turned_rows(data_ref, k, weight, sla, col, count):
    lane = iota((LANES, LANES), 1)
    weight = jnp.where(lane < count, weight, 0.0)
    value = weight * sla
    index = (lane - col) & (LANES - 1)
    weight = jnp.take_along_axis(weight, index, axis=1)
    value = jnp.take_along_axis(value, index, axis=1)
    data_ref[k * LANES : (k + 1) * LANES, :] = jnp.concatenate([*split(weight), *split(value)], axis=1)


def place_kernel(capacity, data_ref, place_ref, meta_ref, token_ref, out_ref, next_ref, made_ref, sems):
    next_ref[...] = token_ref[...]
    blocks = place_ref.shape[0]
    devices = LANES
    chunk = 2 * capacity + 1
    made_ref[pl.ds(2 * capacity, devices, stride=chunk), :] = meta_ref[...]
    place = jnp.concatenate([place_ref[k : k + 1, :] for k in range(blocks)], axis=1)
    group = 16
    height = group * capacity
    slots = iota((height, blocks * LANES), 0)
    copies = []
    for g in range(devices // group):
        pick = (slots == place - g * height).astype(F32).astype(BF16)
        moved = jnp.dot(pick, data_ref[...], preferred_element_type=F32)
        weight = moved[:, :LANES] + moved[:, LANES : 2 * LANES]
        value = moved[:, 2 * LANES : 3 * LANES] + moved[:, 3 * LANES :]
        for t in range(group):
            base = (g * group + t) * chunk
            rows = slice(t * capacity, (t + 1) * capacity)
            made_ref[base : base + capacity, :] = weight[rows]
            made_ref[base + capacity : base + 2 * capacity, :] = value[rows]
        ready = pl.ds(g * group * chunk, group * chunk)
        copies.append(pltpu.make_async_copy(made_ref.at[ready, :], out_ref.at[ready, :], sems.at[g]))
        copies[-1].start()
    for copy in copies:
        copy.wait()


def placed(data, place, meta, token, capacity):
    chunk = 2 * capacity + 1
    return pl.pallas_call(
        functools.partial(place_kernel, capacity),
        out_shape=(far_shape(LANES * chunk, LANES), shape(*token.shape)),
        in_specs=[VMEM] * 4,
        out_specs=(HBM, VMEM),
        scratch_shapes=[
            pltpu.VMEM((LANES * chunk, LANES), F32),
            pltpu.SemaphoreType.DMA((LANES // 16,)),
        ],
        compiler_params=params(12),
        name="place_segments",
    )(data, place, meta, token)


def unpack_kernel(capacity, got_ref, height_ref, face_ref, token_ref, q_ref, next_ref, sum_ref):
    next_ref[...] = token_ref[...]
    chunk = 2 * capacity + 1
    square = (LANES, LANES)
    lane = iota(square, 1)
    meta = got_ref[pl.ds(2 * capacity, LANES, stride=chunk), :]
    meta_t = jnp.transpose(meta)
    rows, cols = q_ref.shape
    cells = rows * cols // LANES
    blocks = iota((cells, LANES), 0).astype(F32)
    lane_f = lane.astype(F32)
    acc = jnp.zeros((cells, 4 * LANES), F32)
    for j in range(capacity):
        weight = got_ref[pl.ds(j, LANES, stride=chunk), :]
        value = got_ref[pl.ds(capacity + j, LANES, stride=chunk), :]
        here = lane_f >= meta[:, 64 + j : 65 + j]
        hit = (blocks == meta_t[j : j + 1]).astype(F32).astype(BF16)
        his, los = [], []
        for x in (weight, value):
            hi = x.astype(BF16).astype(F32)
            lo = x - hi
            for keep in (here, ~here):
                his.append(jnp.where(keep, hi, 0.0).astype(BF16))
                los.append(jnp.where(keep, lo, 0.0).astype(BF16))
        data = jnp.concatenate(
            [jnp.concatenate(his, axis=1), jnp.concatenate(los, axis=1)], axis=0
        )
        acc = acc + jnp.dot(
            jnp.concatenate([hit, hit], axis=1), data, preferred_element_type=F32
        )
    for i in range(2):
        here, after = acc[:, 2 * i * LANES : (2 * i + 1) * LANES], acc[:, (2 * i + 1) * LANES : (2 * i + 2) * LANES]
        sum_ref[i, :, :] = here + pltpu.roll(after, 1, 0)
    for half in range(2):
        at = slice(half * LANES, (half + 1) * LANES)
        weight = sum_ref[0, pl.ds(half, rows, stride=2), :]
        value = sum_ref[1, pl.ds(half, rows, stride=2), :]
        mu = height_ref[0, :, at] + (weight * height_ref[1, :, at] - value)
        q_ref[:, at] = face_ref[3, 0:rows, at] * mu


def unpack(got, heights, faces, token, capacity):
    rows, cols = heights.shape[1:]
    return pl.pallas_call(
        functools.partial(unpack_kernel, capacity),
        out_shape=(shape(rows, cols), shape(*token.shape)),
        in_specs=[VMEM] * 4,
        out_specs=(VMEM, VMEM),
        scratch_shapes=[pltpu.VMEM((2, rows * cols // LANES, LANES), F32)],
        compiler_params=params(10),
        name="forcing",
    )(got, heights, faces, token)


def two_sum(a, b):
    s = a + b
    t = s - a
    return s, (a - (s - t)) + (b - t)


def pair_sum(x, y):
    s, e = two_sum(x[0], y[0])
    e = e + (x[1] + y[1])
    return s, e


def tree(parts):
    while len(parts) > 1:
        odd = parts[len(parts) // 2 * 2 :]
        parts = [pair_sum(parts[i], parts[i + 1]) for i in range(0, len(parts) - 1, 2)] + odd
    return parts[0]


def rows_sum(hi):
    zero = jnp.zeros((8, LANES), F32)
    total = tree([(hi[8 * i : 8 * i + 8], zero) for i in range(16)])
    for step in (4, 2, 1):
        total = pair_sum(total, (pltpu.roll(total[0], step, 0), pltpu.roll(total[1], step, 0)))
    return total


def krylov(apply, start):
    first = apply(start)
    one = SCALE_0 * (first - SHIFT_0 * start)
    second = apply(one)
    two = SCALE_1 * (second - SHIFT_1 * one)
    return (start, one, two), (first, second, apply(two))


def sums_kernel(q_ref, north_ref, south_ref, east_ref, west_ref, face_ref, token_ref, row_ref, field_ref, next_ref, part_ref):
    next_ref[...] = token_ref[...]
    rows, cols = q_ref.shape
    high, wide = rows + 16, cols + LANES
    side = jnp.where(iota((high, LANES), 1) < LANES // 2, east_ref[...], west_ref[...])
    q = jnp.concatenate(
        [jnp.concatenate([q_ref[...], north_ref[...], south_ref[...]], axis=0), side], axis=1
    )

    def apply(v):
        return (
            face_ref[0] * v
            - face_ref[1] * pltpu.roll(v, wide - 1, 1)
            - face_ref[2] * pltpu.roll(v, 1, 1)
            - face_ref[3] * pltpu.roll(v, high - 1, 0)
            - face_ref[4] * pltpu.roll(v, 1, 0)
        )

    def inner(at, a, b):
        p = a[:rows, :cols] * b[:rows, :cols]
        p = (p[0:8] + p[8:16]) + (p[16:24] + p[24:32])
        part_ref[8 * at : 8 * at + 8, :] = p[:, :LANES] + p[:, LANES:]

    w, aw = krylov(apply, q)
    y, ay = zip(*[krylov(apply, face_ref[5] * v) for v in w])
    for i in range(3):
        field_ref[i] = w[i]
        field_ref[3 + 2 * i] = y[i][1]
        field_ref[4 + 2 * i] = y[i][2]
    orders = [(k, l) for k in range(3) for l in range(k + 1)]
    at = 0
    for i in range(3):
        for j in range(3):
            for k, l in orders:
                inner(at, y[i][k], ay[j][l])
                at += 1
            for k in range(3):
                inner(at, y[i][k], y[j][0])
                at += 1
    for k, l in orders:
        inner(at, w[k], aw[l])
        at += 1
    for k in range(3):
        inner(at, w[k], q)
        at += 1
    part_ref[8 * at :, :] = jnp.zeros((8 * (LANES - at), LANES), F32)
    zero = jnp.zeros((LANES, LANES), F32)
    pieces = [(part_ref[pl.ds(s, LANES, stride=8), :], zero) for s in range(8)]
    hi, lo = tree(pieces)
    hi, lo = jnp.transpose(hi), jnp.transpose(lo)
    total = rows_sum(hi)
    row = total[0] + (total[1] + rows_sum(lo)[0])
    row_ref[...] = jnp.broadcast_to(row[0:1], row_ref.shape)


def sums(q, north, south, east, west, faces, token):
    rows, cols = q.shape
    return pl.pallas_call(
        sums_kernel,
        out_shape=(shape(LANES, LANES), shape(9, rows + 16, cols + LANES), shape(*token.shape)),
        in_specs=[VMEM] * 7,
        out_specs=(VMEM,) * 3,
        scratch_shapes=[pltpu.VMEM((8 * LANES, LANES), F32)],
        compiler_params=params(8),
        name="krylov_sums",
    )(q, north, south, east, west, faces, token)


def two_prod(a, b):
    p = a * b
    t = 4097.0 * a
    ah = t - (t - a)
    al = a - ah
    t = 4097.0 * b
    bh = t - (t - b)
    bl = b - bh
    return p, ((ah * bh - p) + (ah * bl + al * bh)) + al * bl


def quick(s, e):
    t = s + e
    return t, e - (t - s)


def pair_add(x, y):
    s, e = two_sum(x[0], y[0])
    return quick(s, e + (x[1] + y[1]))


def pair_neg(x):
    return -x[0], -x[1]


def pair_mul(x, y):
    p, e = two_prod(x[0], y[0])
    return quick(p, e + (x[0] * y[1] + x[1] * y[0]))


def pair_div(x, y):
    first = x[0] / y[0]
    p, e = two_prod(first, y[0])
    rest = ((x[0] - p) - e) + (x[1] - first * y[1])
    return quick(first, rest / y[0])


def minor(a, b, c, d):
    return pair_add(pair_mul(a, b), pair_neg(pair_mul(c, d)))


def pair_sum3(a, b, c):
    return pair_add(pair_add(a, b), c)


def small_solve(g, b):
    g00, g10, g11, g20, g21, g22 = g
    c00, c01, c02 = minor(g11, g22, g21, g21), minor(g20, g21, g10, g22), minor(g10, g21, g20, g11)
    c11, c12, c22 = minor(g00, g22, g20, g20), minor(g10, g20, g00, g21), minor(g00, g11, g10, g10)
    det = pair_sum3(pair_mul(g00, c00), pair_mul(g10, c01), pair_mul(g20, c02))
    three = det[0] > 1e-8 * (c22[0] * g22[0])
    two = c22[0] > 1e-8 * (g00[0] * g11[0])
    three = three & two
    rows = ((c00, c01, c02), (c01, c11, c12), (c02, c12, c22))
    full = [pair_div(pair_sum3(*[pair_mul(m, v) for m, v in zip(row, b)]), det)[0] for row in rows]
    half = [
        pair_div(minor(g11, b[0], g10, b[1]), c22)[0],
        pair_div(minor(g00, b[1], g10, b[0]), c22)[0],
        jnp.zeros_like(det[0]),
    ]
    alone = [b[0][0] / g00[0], half[2], half[2]]
    return [jnp.where(three, x, jnp.where(two, y, z)) for x, y, z in zip(full, half, alone)]


def coefficients(every_ref):
    total = quick(*rows_sum(every_ref[...]))

    def pick(x, at):
        return tuple(jnp.broadcast_to(v[:, at : at + 1], (8, LANES)) for v in x)

    def scaled(x, at):
        by = 1.0 / jnp.broadcast_to(x[0][:, at : at + 1], (8, LANES))
        p, e = two_prod(x[0], by)
        return quick(p, e + x[1] * by)

    first = scaled(total, 81)
    first = [pick(first, 81 + m) for m in range(9)]
    c = small_solve(first[:6], first[6:])
    terms = []
    for i in range(3):
        for j in range(3):
            shift = (LANES - 9 * (3 * i + j)) % LANES
            row = tuple(pltpu.roll(v, shift, 1) if shift else v for v in total)
            terms.append(pair_mul(row, two_prod(c[i], c[j])))
    while len(terms) > 1:
        odd = terms[len(terms) // 2 * 2 :]
        terms = [pair_add(terms[i], terms[i + 1]) for i in range(0, len(terms) - 1, 2)] + odd
    second = scaled(terms[0], 0)
    second = [pick(second, m) for m in range(9)]
    return c, small_solve(second[:6], second[6:])


def tracer_kernel(steric_ref, every_ref, field_ref, face_ref, far_ref, side_ref, mu_ref, rho_ref, tall_ref, sems):
    levels, rows, cols = mu_ref.shape

    def copy(level):
        return pltpu.make_async_copy(far_ref.at[level], tall_ref.at[level], sems.at[level])

    for level in range(levels):
        copy(level).start()
    high, wide = rows + 8, cols + LANES

    def trim(v):
        edge = jnp.where(iota((8, wide), 0) < 4, v[rows : rows + 8], v[rows + 8 :])
        return jnp.concatenate([v[:rows], edge], axis=0)

    c, e = coefficients(every_ref)
    c, e = [[jnp.broadcast_to(v[0:1, 0:1], (1, 1)) for v in part] for part in (c, e)]
    w = [trim(field_ref[i]) for i in range(3)]
    ocean = trim(face_ref[5])
    rho_1 = c[0] * w[0] + c[1] * w[1] + c[2] * w[2]
    rho_0 = e[0] * (ocean * rho_1)
    for k in (1, 2):
        v = [trim(field_ref[2 + k + 2 * i]) for i in range(3)]
        rho_0 = rho_0 + e[k] * (c[0] * v[0] + c[1] * v[1] + c[2] * v[2])
    rho_ref[...] = rho_0[:rows, :cols]

    def one_level(level):
        height = steric_ref[level]
        full = lambda at: jnp.concatenate([tall_ref[level, at], side_ref[at, level]], axis=1)
        g = ocean * (full(0) + height * rho_1)
        dx = g - pltpu.roll(g, wide - 1, 1)
        dy = g - pltpu.roll(g, high - 1, 0)
        mu = g - (
            full(1) * dx + pltpu.roll(full(2) * dx, 1, 1) + full(3) * dy + pltpu.roll(full(4) * dy, 1, 0)
        )
        g = ocean * (mu + height * rho_0)
        dx = (g - pltpu.roll(g, wide - 1, 1))[:rows]
        dy = (g - pltpu.roll(g, high - 1, 0))[:, :cols]
        back_x = pltpu.roll(full(5)[:rows] * dx, 1, 1)[:, :cols]
        back_y = pltpu.roll(tall_ref[level, 6] * dy, 1, 0)[:rows]
        mu_ref[level] = g[:rows, :cols] - (
            tall_ref[level, 7, 0:rows, :] * dx[:, :cols] + back_x + tall_ref[level, 8, 0:rows, :] * dy[:rows] + back_y
        )

    def some_levels(group, carry):
        for i in range(GROUP):
            copy(group * GROUP + i).wait()
        for i in range(GROUP):
            one_level(group * GROUP + i)
        return carry

    lax.fori_loop(0, levels // GROUP, some_levels, 0)


def tracers(steric, every, fields, faces, tall, side):
    levels, count, high, cols = tall.shape
    rows = high - 8
    return pl.pallas_call(
        tracer_kernel,
        out_shape=(shape(levels, rows, cols), shape(rows, cols)),
        in_specs=[SCALAR] + [VMEM] * 3 + [HBM, VMEM],
        out_specs=(VMEM, VMEM),
        scratch_shapes=[pltpu.VMEM((levels, count, high, cols), F32), pltpu.SemaphoreType.DMA((levels,))],
        compiler_params=params(20),
        name="tracer_steps",
    )(steric, every, fields, faces, *far((tall,)), side)


def beside(cells, axis, step):
    count = lax.axis_size(axis)
    return lax.ppermute(cells, axis, [((i + step) % count, i) for i in range(count)])


def tracer_fields(keep, lam, zonal_1, merid_1, zonal_0, merid_0, mix_x, mix_y):
    flow_x, flow_y = 0.5 * zonal_1, 0.5 * merid_1
    past_x, past_y = 0.5 * zonal_0, 0.5 * merid_0
    return (
        lam,
        flow_x + mix_x,
        flow_x - mix_x,
        keep * (flow_y + mix_y),
        keep * (flow_y - mix_y),
        past_x - mix_x,
        keep * (past_y - mix_y),
        past_x + mix_x,
        keep * (past_y + mix_y),
    )


def surface_fields(keep, diag_ref, east_ref, north_ref, land_ref, rows):
    return diag_ref[rows], east_ref[rows], keep * north_ref[rows], land_ref[rows].astype(F32)


UP = (0, 1, 2, 3)
DOWN = (0, 1, 2, 3, 4, 6)
SIDE = (0, 1, 2, 3, 4, 5)


def kept(token_ref, first, count, rows, cols):
    last = jnp.concatenate([token_ref[0:1, :]] * (cols // LANES), axis=1)
    return jnp.where((iota((count, cols), 0) + first == rows - 1) & (last == 1.0), 0.0, 1.0)


def opening_kernel(capacity, token_ref, lam_ref, zonal_ref, merid_ref, mix_x_ref, mix_y_ref, *refs):
    surface_refs, (sla_ref, weight_ref), marks = refs[:4], refs[4:6], refs[6:9]
    up_ref, down_ref, next_ref, data_ref, place_ref, meta_ref = refs[9:15]
    held_ref, flat_ref, land_ref, segment_ref, mark_ref, sems, flat_sems, segment_sems, mark_sems = refs[15:]
    levels, rows, cols = lam_ref.shape
    blocks = mark_ref.shape[1]

    def started(source, target, sem):
        copy = pltpu.make_async_copy(source, target, sem)
        copy.start()
        return copy

    mark_copies = [started(ref, mark_ref.at[i], mark_sems.at[i]) for i, ref in enumerate(marks)]
    segment_copies = []
    for k in range(2):
        block = pl.ds(k * blocks * LANES // 2, blocks * LANES // 2)
        for i, ref in enumerate((sla_ref, weight_ref)):
            segment_copies.append(started(ref.at[block, :], segment_ref.at[i, block, :], segment_sems.at[2 * k + i]))
    copies, flat_copies = [], []
    for part, first in enumerate((0, rows - 8)):
        block = pl.ds(first, 8)
        for source in (
            lam_ref.at[:, block, :],
            zonal_ref.at[1, :, block, :],
            merid_ref.at[1, :, block, :],
            mix_x_ref.at[:, block, :],
            mix_y_ref.at[:, block, :],
            merid_ref.at[0, :, block, :],
        ):
            copies.append(started(source, held_ref.at[len(copies)], sems.at[len(copies)]))
        for i, ref in enumerate(surface_refs[:3]):
            flat_copies.append(started(ref.at[block, :], flat_ref.at[part, i], flat_sems.at[len(flat_copies)]))
        ref = surface_refs[3]
        flat_copies.append(started(ref.at[block, :], land_ref.at[part], flat_sems.at[len(flat_copies)]))
    next_ref[...] = token_ref[...]

    for copy in mark_copies:
        copy.wait()
    col_t, count_t = ranks(capacity, mark_ref[0], mark_ref[1], mark_ref[2], place_ref, meta_ref)
    for copy in copies + flat_copies:
        copy.wait()
    for part, (out_ref, picks, first, take) in enumerate(((up_ref, UP, 0, 0), (down_ref, DOWN, rows - 8, 6))):
        keep = kept(token_ref, first, 8, rows, cols)
        base = 2 * len(picks) * levels
        diag, east, north = [flat_ref[part, i] for i in range(3)]
        ocean = land_ref[part].astype(F32)
        for at, field in enumerate((diag, east, keep * north, ocean)):
            out_ref[base + 8 * at : base + 8 * at + 8, :] = field
        for level in range(levels):
            lam, zonal_1, merid_1, mix_x, mix_y, merid_0 = [held_ref[6 * part + i, level] for i in range(6)]
            fields = tracer_fields(keep, lam, zonal_1, merid_1, zonal_1, merid_0, mix_x, mix_y)
            for at, pick in enumerate(picks):
                base = 2 * (at * levels + level)
                out_ref[base : base + 2, :] = fields[pick][take : take + 2]
    for copy in segment_copies:
        copy.wait()
    for k in range(blocks):
        here = slice(k * LANES, (k + 1) * LANES)
        turned_rows(
            data_ref, k, segment_ref[1, here, :], segment_ref[0, here, :], col_t[:, k : k + 1], count_t[:, k : k + 1]
        )


def edge_rows(n_ref, s_ref, pick, levels, level, cols):
    zero = lambda count: jnp.zeros((count, cols), F32)
    north = zero(2)
    if pick in UP:
        base = 2 * (UP.index(pick) * levels + level)
        north = n_ref[base : base + 2, :]
    south = zero(2)
    if pick in DOWN:
        base = 2 * (DOWN.index(pick) * levels + level)
        south = s_ref[base : base + 2, :]
    return jnp.concatenate([north, zero(4), south], axis=0)


def halves(tall):
    lane = iota((tall.shape[0], LANES), 1)
    return jnp.where(lane < LANES // 2, tall[:, :LANES], tall[:, -LANES:])


def gathered(talls, width):
    lane = iota((talls[0].shape[0], LANES), 1)
    mixed = jnp.zeros((talls[0].shape[0], LANES), F32)
    for at, tall in enumerate(talls):
        mixed = jnp.where(lane // (2 * width) == at, pltpu.roll(halves(tall), width + 2 * width * at, 1), mixed)
    return mixed


def scattered(mixed, at, width):
    return pltpu.roll(mixed, LANES - width - 2 * width * at, 1)


TRACER_WIDTH = 2
FACE_WIDTH = 8


GROUP = 4


def cols_kernel(token_ref, lam_ref, zonal_ref, merid_ref, mix_x_ref, mix_y_ref, *refs):
    surface_refs, height_refs, (n_ref, s_ref) = refs[:4], refs[4:6], refs[6:8]
    out_ref, far_ref, face_ref, height_ref, held_ref, flat_ref, tall_ref, sems, far_sems = refs[8:]
    levels, rows, cols = lam_ref.shape
    copies = []
    for group in range(levels // GROUP):
        block = pl.ds(group * GROUP, GROUP)
        for i, source in enumerate(
            (
                lam_ref.at[block],
                zonal_ref.at[1, block],
                merid_ref.at[1, block],
                zonal_ref.at[0, block],
                merid_ref.at[0, block],
                mix_x_ref.at[block],
                mix_y_ref.at[block],
            )
        ):
            copies.append(pltpu.make_async_copy(source, held_ref.at[i, block], sems.at[len(copies)]))
            copies[-1].start()
    keep = kept(token_ref, 0, rows, rows, cols)
    high = rows + 8
    used = 2 * TRACER_WIDTH * len(SIDE)
    blocks = levels * high // LANES
    base = blocks * used
    up, down = 2 * len(UP) * levels, 2 * len(DOWN) * levels
    talls = []
    for at, field in enumerate(surface_fields(keep, *surface_refs, slice(0, rows))):
        tall = jnp.concatenate(
            [field, n_ref[up + 8 * at : up + 8 * at + 8, :], s_ref[down + 8 * at : down + 8 * at + 8, :]], axis=0
        )
        face_ref[at] = tall
        talls.append(tall)
    out_ref[base : base + rows + 16, :] = gathered(talls, FACE_WIDTH)
    for at, ref in enumerate(height_refs):
        height_ref[at] = ref[...]
    far = []
    for level in range(levels):
        if level % GROUP == 0:
            for copy in copies[7 * (level // GROUP) : 7 * (level // GROUP) + 7]:
                copy.wait()
        fields = tracer_fields(keep, *[held_ref[i, level] for i in range(7)])
        talls = []
        for pick, field in enumerate(fields):
            tall_ref[level, pick, 0:rows, :] = field
            edge = edge_rows(n_ref, s_ref, pick, levels, level, cols)
            tall_ref[level, pick, rows:high, :] = edge
            if pick in SIDE:
                talls.append(jnp.concatenate([field, edge], axis=0))
        flat_ref[level * high : (level + 1) * high, :] = gathered(talls, TRACER_WIDTH)
        far.append(pltpu.make_async_copy(tall_ref.at[level], far_ref.at[level], far_sems.at[level]))
        far[-1].start()
    for b in range(blocks):
        turned = jnp.transpose(flat_ref[b * LANES : (b + 1) * LANES, :])
        out_ref[b * used : (b + 1) * used, :] = turned[:used]
    for copy in far:
        copy.wait()


def side_kernel(e_ref, w_ref, token_ref, side_ref, flat_ref):
    levels, high = side_ref.shape[1:3]
    used = 2 * TRACER_WIDTH * len(SIDE)
    blocks = levels * high // LANES
    western = iota((used, LANES), 0) % (2 * TRACER_WIDTH) < TRACER_WIDTH
    for b in range(blocks):
        at = slice(b * used, (b + 1) * used)
        both = jnp.where(western, w_ref[at, :], e_ref[at, :])
        both = jnp.concatenate([both, jnp.zeros((LANES - used, LANES), F32)], axis=0)
        flat_ref[b * LANES : (b + 1) * LANES, :] = jnp.transpose(both)
    for level in range(levels):
        mixed = flat_ref[level * high : (level + 1) * high, :]
        for at in range(len(SIDE)):
            side_ref[at, level] = scattered(mixed, at, TRACER_WIDTH)


def face_halo_kernel(base, token_ref, tall_ref, e_ref, w_ref, face_ref):
    high = tall_ref.shape[1]
    western = iota((high, LANES), 1) % (2 * FACE_WIDTH) < FACE_WIDTH
    here = slice(base, base + high)
    mixed = jnp.where(western, w_ref[here, :], e_ref[here, :])
    full = [jnp.concatenate([tall_ref[at], scattered(mixed, at, FACE_WIDTH)], axis=1) for at in range(4)]
    diag, east, north, ocean = full
    west, south = pltpu.roll(east, 1, 1), pltpu.roll(north, 1, 0)
    face_ref[0] = (1.0 + diag) + east + west + north + south
    for at, field in enumerate((east, west, north, south, ocean)):
        face_ref[1 + at] = field


def opening(token, tracer, surface, segments, marks, capacity):
    levels, rows, cols = tracer[0].shape
    up, down = 2 * len(UP) * levels + 32, 2 * len(DOWN) * levels + 32
    blocks = segments[0].shape[0] // LANES
    marks = tuple(mark.reshape(blocks, LANES) for mark in marks)
    return pl.pallas_call(
        functools.partial(opening_kernel, capacity),
        out_shape=(
            shape(up, cols),
            shape(down, cols),
            shape(*token.shape),
            jax.ShapeDtypeStruct((blocks * LANES, 4 * LANES), BF16),
            jax.ShapeDtypeStruct((blocks, LANES), jnp.int32),
            shape(LANES, LANES),
        ),
        in_specs=[VMEM] + [HBM] * 14,
        out_specs=(VMEM,) * 6,
        scratch_shapes=[
            pltpu.VMEM((12, levels, 8, cols), F32),
            pltpu.VMEM((2, 3, 8, cols), F32),
            pltpu.VMEM((2, 8, cols), jnp.int32),
            pltpu.VMEM((2, blocks * LANES, LANES), F32),
            pltpu.VMEM((3, blocks, LANES), jnp.int32),
            pltpu.SemaphoreType.DMA((12,)),
            pltpu.SemaphoreType.DMA((8,)),
            pltpu.SemaphoreType.DMA((4,)),
            pltpu.SemaphoreType.DMA((3,)),
        ],
        compiler_params=params(12),
        name="opening",
    )(token, *far(tracer), *far(surface), *far(segments), *far(marks))


def edges_to_tx(token, tracer, surface, heights, north, south):
    levels, rows, cols = tracer[0].shape
    high = rows + 8
    side_rows = 2 * TRACER_WIDTH * len(SIDE) * levels * high // LANES + rows + 16
    sides, tall, faces, heights = pl.pallas_call(
        cols_kernel,
        out_shape=(
            shape(side_rows, LANES),
            far_shape(levels, 9, high, cols),
            shape(4, rows + 16, cols),
            shape(2, rows, cols),
        ),
        in_specs=[VMEM] + [HBM] * 5 + [VMEM] * 8,
        out_specs=(VMEM, HBM, VMEM, VMEM),
        scratch_shapes=[
            pltpu.VMEM((7, levels, rows, cols), F32),
            pltpu.VMEM((levels * high, LANES), F32),
            pltpu.VMEM((levels, 9, high, cols), F32),
            pltpu.SemaphoreType.DMA((7 * levels // GROUP,)),
            pltpu.SemaphoreType.DMA((levels,)),
        ],
        compiler_params=params(24),
        name="edge_columns",
    )(token, *far(tracer), *far(surface), *far(heights), north, south)
    return (beside(sides, "tx", 1), beside(sides, "tx", -1)), tall, faces, heights


def faces_with_halo(token, tall, east, west):
    count, high, cols = tall.shape
    return pl.pallas_call(
        functools.partial(face_halo_kernel, east.shape[0] - high),
        out_shape=shape(6, high, cols + LANES),
        in_specs=[VMEM] * 4,
        out_specs=VMEM,
        compiler_params=params(6),
        name="surface_halos",
    )(token, tall, east, west)


def tracer_sides(token, levels, rows, east, west):
    high = rows + 8
    return pl.pallas_call(
        side_kernel,
        out_shape=shape(len(SIDE), levels, high, LANES),
        in_specs=[VMEM] * 3,
        out_specs=VMEM,
        scratch_shapes=[pltpu.VMEM((levels * high, LANES), F32)],
        compiler_params=params(8),
        name="tracer_halos",
    )(east, west, token)


def on_device(
    lam_tracer,
    lam_eta,
    land,
    zonal_flow,
    merid_flow,
    zonal_mixing,
    merid_mixing,
    surface_east,
    surface_north,
    surface_diag,
    steric,
    eta_saved,
    obs_sla,
    obs_weight,
    obs_tile,
    obs_start,
    obs_count,
):
    levels, rows, cols = lam_tracer.shape
    n_rows = lax.axis_size("ty")
    devices = n_rows * lax.axis_size("tx")
    capacity = 2 * obs_sla.shape[0] // devices
    token = jnp.full((8, LANES), lax.axis_index("ty") == n_rows - 1, F32)
    tracer = (lam_tracer, zonal_flow, merid_flow, zonal_mixing, merid_mixing)
    surface = (surface_diag, surface_east, surface_north, land)
    to_south, to_north, token, *ranked = opening(
        token, tracer, surface, (obs_sla, obs_weight), (obs_tile, obs_start, obs_count), capacity
    )
    around_ty = beside(to_south, "ty", 1), beside(to_north, "ty", -1)
    sent, token = placed(*ranked, token, capacity)
    sent, *around_ty = lax.optimization_barrier((sent, *around_ty))
    got = lax.all_to_all(
        sent.reshape(devices, 1, -1), AXES, split_axis=0, concat_axis=0, tiled=True
    ).reshape(sent.shape)
    around_tx, tall, faces, heights = edges_to_tx(token, tracer, surface, (lam_eta, eta_saved), *around_ty)
    rhs, token = unpack(got, heights, faces, token, capacity)
    faces = faces_with_halo(token, faces, *around_tx)
    north, south = beside(rhs[:8], "ty", 1), beside(rhs[-8:], "ty", -1)
    side = halves(jnp.concatenate([rhs, north, south], axis=0))
    east, west = beside(side, "tx", 1), beside(side, "tx", -1)
    mine, krylov_fields, token = sums(rhs, north, south, east, west, faces, token)
    every = lax.all_to_all(
        mine.reshape(devices, 1, LANES), AXES, split_axis=0, concat_axis=0, tiled=True
    ).reshape(devices, LANES)
    sides = tracer_sides(token, levels, rows, *around_tx)
    return tracers(steric, every, krylov_fields, faces, tall, sides)


def solution(mesh):
    in_specs = (
        P(None, "ty", "tx"),
        P("ty", "tx"),
        P("ty", "tx"),
        P(None, None, "ty", "tx"),
        P(None, None, "ty", "tx"),
        P(None, "ty", "tx"),
        P(None, "ty", "tx"),
        P("ty", "tx"),
        P("ty", "tx"),
        P("ty", "tx"),
        P(),
        P("ty", "tx"),
        P(AXES, None),
        P(AXES, None),
        P(AXES, None),
        P(AXES),
        P(AXES),
    )
    out_specs = (P(None, "ty", "tx"), P("ty", "tx"))
    return jax.shard_map(
        on_device, mesh=mesh, in_specs=in_specs, out_specs=out_specs, check_vma=False
    )
```

```python
import functools

import jax
import jax.numpy as jnp
from jax import lax
from jax.experimental import pallas as pl
from jax.experimental.pallas import tpu as pltpu
from jax.sharding import PartitionSpec as P

AXES = ("ty", "tx")
SHIFT_0 = 1.6
SHIFT_1 = 35.0
SCALE_0 = 1.0 / 32.0
SCALE_1 = 1.0 / 16.0
LANES = 128
VMEM = pl.BlockSpec(memory_space=pltpu.VMEM)
SCALAR = pl.BlockSpec(memory_space=pltpu.SMEM)
HBM = pl.BlockSpec(memory_space=pltpu.HBM)
F32 = jnp.float32
BF16 = jnp.bfloat16


def params(mib):
    return pltpu.CompilerParams(vmem_limit_bytes=mib * 1024 * 1024)


def iota(dims, axis):
    return lax.broadcasted_iota(jnp.int32, dims, axis)


def shape(*dims):
    return jax.ShapeDtypeStruct(dims, F32)


def far_shape(*dims):
    return pltpu.HBM(dims, F32)


def far(arrays):
    return tuple(pltpu.with_memory_space_constraint(x, pltpu.HBM) for x in arrays)


def split(x):
    hi = x.astype(BF16)
    return hi, (x - hi.astype(F32)).astype(BF16)


def ranks(capacity, tile, start, count, place_ref, meta_ref):
    blocks = tile.shape[0]
    square = (LANES, LANES)
    sub, lane = iota(square, 0), iota(square, 1)
    prefix = jnp.concatenate([(sub < lane).astype(BF16), jnp.ones(square, BF16)], axis=1)
    carry = jnp.zeros(square, F32)
    hits, firsts = [], []
    for k in range(blocks):
        target = tile[k : k + 1]
        hit = sub == target
        hits.append(hit.astype(F32).astype(BF16))
        both = jnp.dot(hits[-1], prefix, preferred_element_type=F32)
        slot = jnp.sum(jnp.where(hit, both[:, :LANES] + carry, 0.0), axis=0, keepdims=True)
        carry = carry + both[:, LANES:]
        slot = slot.astype(jnp.int32)
        place_ref[k : k + 1, :] = target * capacity + slot
        begin = start[k : k + 1]
        block_of = jnp.where(sub == slot, begin // LANES, 0)
        lane_of = jnp.where(sub == slot + 64, begin & (LANES - 1), 0)
        firsts.append((block_of + lane_of).astype(F32).astype(BF16))
    meta_ref[...] = lax.dot_general(
        jnp.concatenate(hits, axis=1),
        jnp.concatenate(firsts, axis=1),
        (((1,), (1,)), ((), ())),
        preferred_element_type=F32,
    )
    col_t = jnp.transpose((start & (LANES - 1)).astype(F32)).astype(jnp.int32)
    return col_t, jnp.transpose(count.astype(F32)).astype(jnp.int32)


def turned_rows(data_ref, k, weight, sla, col, count):
    lane = iota((LANES, LANES), 1)
    weight = jnp.where(lane < count, weight, 0.0)
    value = weight * sla
    index = (lane - col) & (LANES - 1)
    weight = jnp.take_along_axis(weight, index, axis=1)
    value = jnp.take_along_axis(value, index, axis=1)
    data_ref[k * LANES : (k + 1) * LANES, :] = jnp.concatenate([*split(weight), *split(value)], axis=1)


EDGE = 5
WIDE = 2 * EDGE
FIRST_SLOTS = 12


def edge_lanes(rows):
    slot, lane = iota((rows, LANES), 0) % 16, iota((rows, LANES), 1)
    rest = 16 - FIRST_SLOTS
    late = slot - FIRST_SLOTS
    is_first = (lane // WIDE == slot) & (late < 0)
    is_late = ((lane // WIDE) % rest == late) & (lane < 2 * rest * WIDE)
    first = (lane - WIDE * slot) & (LANES - 1)
    second = (first + WIDE) & (LANES - 1)
    third = jnp.where(lane < rest * WIDE, lane - WIDE * late, lane - WIDE * (late + rest - 1)) & (LANES - 1)
    return (first, is_first), (second, is_first), (third, is_late)


def folded(parts):
    sub = iota((8, LANES), 0)
    for step in (4, 2, 1):
        low = (sub & step) == 0
        half = len(parts) // 2
        pairs = []
        for a, b in zip(parts[:half], parts[half:]):
            other = jnp.where(low, b, a)
            moved = jnp.where(low, pltpu.roll(other, 8 - step, 0), pltpu.roll(other, step, 0))
            pairs.append(jnp.where(low, a, b) + moved)
        parts = pairs
    return parts[0]


def place_kernel(capacity, n_cols, data_ref, place_ref, meta_ref, token_ref, out_ref, next_ref, made_ref, sems):
    next_ref[...] = token_ref[...]
    blocks = place_ref.shape[0]
    chunk = 2 * capacity + 4
    place = jnp.concatenate([place_ref[k : k + 1, :] for k in range(blocks)], axis=1)
    height = n_cols * capacity
    slots = iota((height, blocks * LANES), 0)
    lane = iota((capacity, LANES), 1)
    ends = jnp.where(lane < WIDE, lane % EDGE, LANES - EDGE + lane % EDGE)
    in_value = (lane // EDGE) % 2 == 1
    lanes = edge_lanes(capacity)
    western = iota((n_cols, LANES), 1) < WIDE * (16 - FIRST_SLOTS)
    east_of = lambda x: pltpu.roll(x, n_cols - 1, 0)
    west_of = lambda x: pltpu.roll(x, 1, 0)
    copies = []
    for g in range(LANES // n_cols):
        pick = (slots == place - g * height).astype(F32).astype(BF16)
        moved = jnp.dot(pick, data_ref[...], preferred_element_type=F32)
        weight = moved[:, :LANES] + moved[:, LANES : 2 * LANES]
        value = moved[:, 2 * LANES : 3 * LANES] + moved[:, 3 * LANES :]
        first = g * n_cols * chunk
        parts = [[], [], []]
        for t in range(n_cols):
            base = first + t * chunk
            rows = slice(t * capacity, (t + 1) * capacity)
            made_ref[base : base + capacity, :] = weight[rows]
            made_ref[base + capacity : base + 2 * capacity, :] = value[rows]
            both = jnp.where(
                in_value,
                jnp.take_along_axis(value[rows], ends, axis=1),
                jnp.take_along_axis(weight[rows], ends, axis=1),
            )
            for part, (index, mine) in zip(parts, lanes):
                spread = jnp.where(mine, jnp.take_along_axis(both, index, axis=1), 0.0)
                part.append(spread[:8] + spread[8:])
        edges = [
            jnp.concatenate([folded(part[i : i + 8]) for i in range(0, n_cols, 8)], axis=0) for part in parts
        ]
        meta = meta_ref[g * n_cols : (g + 1) * n_cols, :]
        meta = (
            meta + pltpu.roll(east_of(meta), capacity, 1) + pltpu.roll(west_of(meta), 2 * capacity, 1)
        )
        extra = (
            meta,
            east_of(edges[0]),
            west_of(edges[1]),
            jnp.where(western, east_of(edges[2]), west_of(edges[2])),
        )
        for i, rows in enumerate(extra):
            made_ref[pl.ds(first + 2 * capacity + i, n_cols, stride=chunk), :] = rows
        ready = pl.ds(first, n_cols * chunk)
        copies.append(pltpu.make_async_copy(made_ref.at[ready, :], out_ref.at[ready, :], sems.at[g]))
        copies[-1].start()
    for copy in copies:
        copy.wait()


def placed(data, place, meta, token, capacity, n_cols):
    chunk = 2 * capacity + 4
    return pl.pallas_call(
        functools.partial(place_kernel, capacity, n_cols),
        out_shape=(far_shape(LANES * chunk, LANES), shape(*token.shape)),
        in_specs=[VMEM] * 4,
        out_specs=(HBM, VMEM),
        scratch_shapes=[
            pltpu.VMEM((LANES * chunk, LANES), F32),
            pltpu.SemaphoreType.DMA((LANES // n_cols,)),
        ],
        compiler_params=params(12),
        name="place_segments",
    )(data, place, meta, token)


def unpack_kernel(capacity, got_ref, height_ref, face_ref, token_ref, q_ref, next_ref, sum_ref):
    next_ref[...] = token_ref[...]
    chunk = 2 * capacity + 4
    square = (LANES, LANES)
    lane = iota(square, 1)
    meta = got_ref[pl.ds(2 * capacity, LANES, stride=chunk), :]
    meta_t = jnp.transpose(meta)
    rows, cols = q_ref.shape[0], q_ref.shape[1] - LANES
    cells = rows * cols // LANES
    blocks = iota((cells, LANES), 0).astype(F32)
    lane_f = lane.astype(F32)
    acc = jnp.zeros((cells, 4 * LANES), F32)
    for j in range(capacity):
        weight = got_ref[pl.ds(j, LANES, stride=chunk), :]
        value = got_ref[pl.ds(capacity + j, LANES, stride=chunk), :]
        here = lane_f >= meta[:, 64 + j : 65 + j]
        hit = (blocks == meta_t[j : j + 1]).astype(F32).astype(BF16)
        his, los = [], []
        for x in (weight, value):
            hi = x.astype(BF16).astype(F32)
            lo = x - hi
            for keep in (here, ~here):
                his.append(jnp.where(keep, hi, 0.0).astype(BF16))
                los.append(jnp.where(keep, lo, 0.0).astype(BF16))
        data = jnp.concatenate(
            [jnp.concatenate(his, axis=1), jnp.concatenate(los, axis=1)], axis=0
        )
        acc = acc + jnp.dot(
            jnp.concatenate([hit, hit], axis=1), data, preferred_element_type=F32
        )
    for i in range(2):
        here, after = acc[:, 2 * i * LANES : (2 * i + 1) * LANES], acc[:, (2 * i + 1) * LANES : (2 * i + 2) * LANES]
        sum_ref[i, :, :] = here + pltpu.roll(after, 1, 0)
    for half in range(2):
        at = slice(half * LANES, (half + 1) * LANES)
        weight = sum_ref[0, pl.ds(half, rows, stride=2), :]
        value = sum_ref[1, pl.ds(half, rows, stride=2), :]
        mu = height_ref[0, :, at] + (weight * height_ref[1, :, at] - value)
        q_ref[:, at] = face_ref[5, 0:rows, at] * mu

    row_of = iota((rows, LANES), 0).astype(F32)
    group = iota((rows, LANES), 1) // WIDE
    rest = capacity - FIRST_SLOTS
    at = lane % EDGE
    first = capacity + jnp.minimum(lane // WIDE, FIRST_SLOTS - 1)
    late = capacity + FIRST_SLOTS + (lane // WIDE) % rest
    western = lane < rest * WIDE
    edges = []
    for i, (index, is_west) in enumerate(
        ((first, True), (first + capacity, False), (jnp.where(western, late, late + capacity), western))
    ):
        block = jnp.take_along_axis(meta, index, axis=1)
        start = jnp.take_along_axis(meta, index + 64, axis=1).astype(jnp.int32)
        odd = block != 2.0 * jnp.floor(0.5 * block)
        has_west = ~odd & (at >= start)
        has_east = odd | (LANES - EDGE + at < start)
        if is_west is True:
            valid = has_west
        elif is_west is False:
            valid = has_east
        else:
            valid = (is_west & has_west) | (~is_west & has_east)
        edge = got_ref[pl.ds(2 * capacity + 1 + i, LANES, stride=chunk), :]
        edges.append(jnp.concatenate(split(jnp.where(valid, edge, 0.0)), axis=0))

    def edge_sum(base, row, first_group):
        hits = []
        for j in range(capacity):
            hits.append((row_of == jnp.floor(0.5 * meta_t[base + j : base + j + 1])).astype(F32).astype(BF16))

        def spread(picks, edge):
            hit = jnp.concatenate(picks, axis=0)
            return jnp.dot(jnp.concatenate([hit, hit], axis=1), edges[edge], preferred_element_type=F32)

        total = jnp.zeros((rows, LANES), F32)
        full = spread(hits[:FIRST_SLOTS], row)
        for j in range(FIRST_SLOTS):
            total = jnp.where(group == j, full[j * rows : (j + 1) * rows], total)
        tail = spread(hits[FIRST_SLOTS:], 2)
        late = jnp.zeros((rows, LANES), F32)
        for j in range(rest):
            late = jnp.where(group == first_group + j, tail[j * rows : (j + 1) * rows], late)
        if first_group:
            late = pltpu.roll(late, LANES - WIDE * first_group, 1)
        total = total + late
        total = total + pltpu.roll(total, LANES - 6 * WIDE, 1)
        total = total + pltpu.roll(total, LANES - 3 * WIDE, 1)
        total = total + pltpu.roll(total, LANES - WIDE, 1) + pltpu.roll(total, LANES - 2 * WIDE, 1)
        return total, pltpu.roll(total, LANES - EDGE, 1)

    side = slice(cols, cols + LANES)
    eastern = iota((rows, LANES), 1) < LANES // 2
    weight, value = [
        jnp.where(eastern, e, pltpu.roll(w, LANES - EDGE, 1))
        for e, w in zip(edge_sum(capacity, 0, 0), edge_sum(2 * capacity, 1, rest))
    ]
    mu = height_ref[0, :, side] + (weight * height_ref[1, :, side] - value)
    q_ref[:, side] = face_ref[5, 0:rows, side] * mu


def unpack(got, heights, faces, token, capacity):
    rows, wide = heights.shape[1:]
    return pl.pallas_call(
        functools.partial(unpack_kernel, capacity),
        out_shape=(shape(rows, wide), shape(*token.shape)),
        in_specs=[VMEM] * 4,
        out_specs=(VMEM, VMEM),
        scratch_shapes=[pltpu.VMEM((2, rows * (wide - LANES) // LANES, LANES), F32)],
        compiler_params=params(10),
        name="forcing",
    )(got, heights, faces, token)


def two_sum(a, b):
    s = a + b
    t = s - a
    return s, (a - (s - t)) + (b - t)


def pair_sum(x, y):
    s, e = two_sum(x[0], y[0])
    e = e + (x[1] + y[1])
    return s, e


def tree(parts):
    while len(parts) > 1:
        odd = parts[len(parts) // 2 * 2 :]
        parts = [pair_sum(parts[i], parts[i + 1]) for i in range(0, len(parts) - 1, 2)] + odd
    return parts[0]


def rows_sum(hi):
    zero = jnp.zeros((8, LANES), F32)
    total = tree([(hi[8 * i : 8 * i + 8], zero) for i in range(16)])
    for step in (4, 2, 1):
        total = pair_sum(total, (pltpu.roll(total[0], step, 0), pltpu.roll(total[1], step, 0)))
    return total


def krylov(apply, start):
    first = apply(start)
    one = SCALE_0 * (first - SHIFT_0 * start)
    second = apply(one)
    two = SCALE_1 * (second - SHIFT_1 * one)
    return (start, one, two), (first, second, apply(two))


def sums_kernel(q_ref, north_ref, south_ref, face_ref, token_ref, row_ref, field_ref, next_ref, part_ref):
    next_ref[...] = token_ref[...]
    rows, cols = q_ref.shape[0], q_ref.shape[1] - LANES
    high, wide = rows + 16, cols + LANES
    q = jnp.concatenate([q_ref[...], north_ref[...], south_ref[...]], axis=0)

    def apply(v):
        return (
            face_ref[0] * v
            - face_ref[1] * pltpu.roll(v, wide - 1, 1)
            - face_ref[2] * pltpu.roll(v, 1, 1)
            - face_ref[3] * pltpu.roll(v, high - 1, 0)
            - face_ref[4] * pltpu.roll(v, 1, 0)
        )

    def inner(at, a, b):
        p = a[:rows, :cols] * b[:rows, :cols]
        p = (p[0:8] + p[8:16]) + (p[16:24] + p[24:32])
        part_ref[8 * at : 8 * at + 8, :] = p[:, :LANES] + p[:, LANES:]

    w, aw = krylov(apply, q)
    y, ay = zip(*[krylov(apply, face_ref[5] * v) for v in w])
    for i in range(3):
        field_ref[i] = w[i]
        field_ref[3 + 2 * i] = y[i][1]
        field_ref[4 + 2 * i] = y[i][2]
    orders = [(k, l) for k in range(3) for l in range(k + 1)]
    at = 0
    for i in range(3):
        for j in range(3):
            for k, l in orders:
                inner(at, y[i][k], ay[j][l])
                at += 1
            for k in range(3):
                inner(at, y[i][k], y[j][0])
                at += 1
    for k, l in orders:
        inner(at, w[k], aw[l])
        at += 1
    for k in range(3):
        inner(at, w[k], q)
        at += 1
    part_ref[8 * at :, :] = jnp.zeros((8 * (LANES - at), LANES), F32)
    zero = jnp.zeros((LANES, LANES), F32)
    pieces = [(part_ref[pl.ds(s, LANES, stride=8), :], zero) for s in range(8)]
    hi, lo = tree(pieces)
    hi, lo = jnp.transpose(hi), jnp.transpose(lo)
    total = rows_sum(hi)
    row = total[0] + (total[1] + rows_sum(lo)[0])
    row_ref[...] = jnp.broadcast_to(row[0:1], row_ref.shape)


def sums(q, north, south, faces, token):
    rows, wide = q.shape
    return pl.pallas_call(
        sums_kernel,
        out_shape=(shape(LANES, LANES), shape(9, rows + 16, wide), shape(*token.shape)),
        in_specs=[VMEM] * 5,
        out_specs=(VMEM,) * 3,
        scratch_shapes=[pltpu.VMEM((8 * LANES, LANES), F32)],
        compiler_params=params(8),
        name="krylov_sums",
    )(q, north, south, faces, token)


def two_prod(a, b):
    p = a * b
    t = 4097.0 * a
    ah = t - (t - a)
    al = a - ah
    t = 4097.0 * b
    bh = t - (t - b)
    bl = b - bh
    return p, ((ah * bh - p) + (ah * bl + al * bh)) + al * bl


def quick(s, e):
    t = s + e
    return t, e - (t - s)


def pair_add(x, y):
    s, e = two_sum(x[0], y[0])
    return quick(s, e + (x[1] + y[1]))


def pair_neg(x):
    return -x[0], -x[1]


def pair_mul(x, y):
    p, e = two_prod(x[0], y[0])
    return quick(p, e + (x[0] * y[1] + x[1] * y[0]))


def pair_div(x, y):
    first = x[0] / y[0]
    p, e = two_prod(first, y[0])
    rest = ((x[0] - p) - e) + (x[1] - first * y[1])
    return quick(first, rest / y[0])


def minor(a, b, c, d):
    return pair_add(pair_mul(a, b), pair_neg(pair_mul(c, d)))


def pair_sum3(a, b, c):
    return pair_add(pair_add(a, b), c)


def small_solve(g, b):
    g00, g10, g11, g20, g21, g22 = g
    c00, c01, c02 = minor(g11, g22, g21, g21), minor(g20, g21, g10, g22), minor(g10, g21, g20, g11)
    c11, c12, c22 = minor(g00, g22, g20, g20), minor(g10, g20, g00, g21), minor(g00, g11, g10, g10)
    det = pair_sum3(pair_mul(g00, c00), pair_mul(g10, c01), pair_mul(g20, c02))
    three = det[0] > 1e-8 * (c22[0] * g22[0])
    two = c22[0] > 1e-8 * (g00[0] * g11[0])
    three = three & two
    rows = ((c00, c01, c02), (c01, c11, c12), (c02, c12, c22))
    full = [pair_div(pair_sum3(*[pair_mul(m, v) for m, v in zip(row, b)]), det)[0] for row in rows]
    half = [
        pair_div(minor(g11, b[0], g10, b[1]), c22)[0],
        pair_div(minor(g00, b[1], g10, b[0]), c22)[0],
        jnp.zeros_like(det[0]),
    ]
    alone = [b[0][0] / g00[0], half[2], half[2]]
    return [jnp.where(three, x, jnp.where(two, y, z)) for x, y, z in zip(full, half, alone)]


def coefficients(every_ref):
    total = quick(*rows_sum(every_ref[...]))

    def pick(x, at):
        return tuple(jnp.broadcast_to(v[:, at : at + 1], (8, LANES)) for v in x)

    def scaled(x, at):
        by = 1.0 / jnp.broadcast_to(x[0][:, at : at + 1], (8, LANES))
        p, e = two_prod(x[0], by)
        return quick(p, e + x[1] * by)

    first = scaled(total, 81)
    first = [pick(first, 81 + m) for m in range(9)]
    c = small_solve(first[:6], first[6:])
    terms = []
    for i in range(3):
        for j in range(3):
            shift = (LANES - 9 * (3 * i + j)) % LANES
            row = tuple(pltpu.roll(v, shift, 1) if shift else v for v in total)
            terms.append(pair_mul(row, two_prod(c[i], c[j])))
    while len(terms) > 1:
        odd = terms[len(terms) // 2 * 2 :]
        terms = [pair_add(terms[i], terms[i + 1]) for i in range(0, len(terms) - 1, 2)] + odd
    second = scaled(terms[0], 0)
    second = [pick(second, m) for m in range(9)]
    return c, small_solve(second[:6], second[6:])


def tracer_kernel(steric_ref, every_ref, field_ref, face_ref, far_ref, side_ref, mu_ref, rho_ref, tall_ref, sems):
    levels, rows, cols = mu_ref.shape

    def copy(level):
        return pltpu.make_async_copy(far_ref.at[level], tall_ref.at[level], sems.at[level])

    for level in range(levels):
        copy(level).start()
    high, wide = rows + 8, cols + LANES

    def trim(v):
        edge = jnp.where(iota((8, wide), 0) < 4, v[rows : rows + 8], v[rows + 8 :])
        return jnp.concatenate([v[:rows], edge], axis=0)

    c, e = coefficients(every_ref)
    c, e = [[jnp.broadcast_to(v[0:1, 0:1], (1, 1)) for v in part] for part in (c, e)]
    w = [trim(field_ref[i]) for i in range(3)]
    ocean = trim(face_ref[5])
    rho_1 = c[0] * w[0] + c[1] * w[1] + c[2] * w[2]
    rho_0 = e[0] * (ocean * rho_1)
    for k in (1, 2):
        v = [trim(field_ref[2 + k + 2 * i]) for i in range(3)]
        rho_0 = rho_0 + e[k] * (c[0] * v[0] + c[1] * v[1] + c[2] * v[2])
    rho_ref[...] = rho_0[:rows, :cols]

    def one_level(level):
        height = steric_ref[level]
        full = lambda at: jnp.concatenate([tall_ref[level, at], side_ref[at, level]], axis=1)
        g = ocean * (full(0) + height * rho_1)
        dx = g - pltpu.roll(g, wide - 1, 1)
        dy = g - pltpu.roll(g, high - 1, 0)
        mu = g - (
            full(1) * dx + pltpu.roll(full(2) * dx, 1, 1) + full(3) * dy + pltpu.roll(full(4) * dy, 1, 0)
        )
        g = ocean * (mu + height * rho_0)
        dx = (g - pltpu.roll(g, wide - 1, 1))[:rows]
        dy = (g - pltpu.roll(g, high - 1, 0))[:, :cols]
        back_x = pltpu.roll(full(5)[:rows] * dx, 1, 1)[:, :cols]
        back_y = pltpu.roll(tall_ref[level, 6] * dy, 1, 0)[:rows]
        mu_ref[level] = g[:rows, :cols] - (
            tall_ref[level, 7, 0:rows, :] * dx[:, :cols] + back_x + tall_ref[level, 8, 0:rows, :] * dy[:rows] + back_y
        )

    def some_levels(group, carry):
        for i in range(GROUP):
            copy(group * GROUP + i).wait()
        for i in range(GROUP):
            one_level(group * GROUP + i)
        return carry

    lax.fori_loop(0, levels // GROUP, some_levels, 0)


def tracers(steric, every, fields, faces, tall, side):
    levels, count, high, cols = tall.shape
    rows = high - 8
    return pl.pallas_call(
        tracer_kernel,
        out_shape=(shape(levels, rows, cols), shape(rows, cols)),
        in_specs=[SCALAR] + [VMEM] * 3 + [HBM, VMEM],
        out_specs=(VMEM, VMEM),
        scratch_shapes=[pltpu.VMEM((levels, count, high, cols), F32), pltpu.SemaphoreType.DMA((levels,))],
        compiler_params=params(20),
        name="tracer_steps",
    )(steric, every, fields, faces, *far((tall,)), side)


def beside(cells, axis, step):
    count = lax.axis_size(axis)
    return lax.ppermute(cells, axis, [((i + step) % count, i) for i in range(count)])


def tracer_fields(keep, lam, zonal_1, merid_1, zonal_0, merid_0, mix_x, mix_y):
    flow_x, flow_y = 0.5 * zonal_1, 0.5 * merid_1
    past_x, past_y = 0.5 * zonal_0, 0.5 * merid_0
    return (
        lam,
        flow_x + mix_x,
        flow_x - mix_x,
        keep * (flow_y + mix_y),
        keep * (flow_y - mix_y),
        past_x - mix_x,
        keep * (past_y - mix_y),
        past_x + mix_x,
        keep * (past_y + mix_y),
    )


def surface_fields(keep, diag_ref, east_ref, north_ref, land_ref, rows):
    return diag_ref[rows], east_ref[rows], keep * north_ref[rows], land_ref[rows].astype(F32)


UP = (0, 1, 2, 3)
DOWN = (0, 1, 2, 3, 4, 6)
SIDE = (0, 1, 2, 3, 4, 5)


def kept(token_ref, first, count, rows, cols):
    last = jnp.concatenate([token_ref[0:1, :]] * (cols // LANES), axis=1)
    return jnp.where((iota((count, cols), 0) + first == rows - 1) & (last == 1.0), 0.0, 1.0)


def opening_kernel(capacity, token_ref, lam_ref, zonal_ref, merid_ref, mix_x_ref, mix_y_ref, *refs):
    surface_refs, (sla_ref, weight_ref), marks = refs[:4], refs[4:6], refs[6:9]
    up_ref, down_ref, next_ref, data_ref, place_ref, meta_ref = refs[9:15]
    held_ref, flat_ref, land_ref, segment_ref, mark_ref, sems, flat_sems, segment_sems, mark_sems = refs[15:]
    levels, rows, cols = lam_ref.shape
    blocks = mark_ref.shape[1]

    def started(source, target, sem):
        copy = pltpu.make_async_copy(source, target, sem)
        copy.start()
        return copy

    mark_copies = [started(ref, mark_ref.at[i], mark_sems.at[i]) for i, ref in enumerate(marks)]
    segment_copies = []
    for k in range(2):
        block = pl.ds(k * blocks * LANES // 2, blocks * LANES // 2)
        for i, ref in enumerate((sla_ref, weight_ref)):
            segment_copies.append(started(ref.at[block, :], segment_ref.at[i, block, :], segment_sems.at[2 * k + i]))
    copies, flat_copies = [], []
    for part, first in enumerate((0, rows - 8)):
        block = pl.ds(first, 8)
        for source in (
            lam_ref.at[:, block, :],
            zonal_ref.at[1, :, block, :],
            merid_ref.at[1, :, block, :],
            mix_x_ref.at[:, block, :],
            mix_y_ref.at[:, block, :],
            merid_ref.at[0, :, block, :],
        ):
            copies.append(started(source, held_ref.at[len(copies)], sems.at[len(copies)]))
        for i, ref in enumerate(surface_refs[:3]):
            flat_copies.append(started(ref.at[block, :], flat_ref.at[part, i], flat_sems.at[len(flat_copies)]))
        ref = surface_refs[3]
        flat_copies.append(started(ref.at[block, :], land_ref.at[part], flat_sems.at[len(flat_copies)]))
    next_ref[...] = token_ref[...]

    for copy in mark_copies:
        copy.wait()
    col_t, count_t = ranks(capacity, mark_ref[0], mark_ref[1], mark_ref[2], place_ref, meta_ref)
    for copy in copies + flat_copies:
        copy.wait()
    for part, (out_ref, picks, first, take) in enumerate(((up_ref, UP, 0, 0), (down_ref, DOWN, rows - 8, 6))):
        keep = kept(token_ref, first, 8, rows, cols)
        base = 2 * len(picks) * levels
        diag, east, north = [flat_ref[part, i] for i in range(3)]
        ocean = land_ref[part].astype(F32)
        for at, field in enumerate((diag, east, keep * north, ocean)):
            out_ref[base + 8 * at : base + 8 * at + 8, :] = field
        for level in range(levels):
            lam, zonal_1, merid_1, mix_x, mix_y, merid_0 = [held_ref[6 * part + i, level] for i in range(6)]
            fields = tracer_fields(keep, lam, zonal_1, merid_1, zonal_1, merid_0, mix_x, mix_y)
            for at, pick in enumerate(picks):
                base = 2 * (at * levels + level)
                out_ref[base : base + 2, :] = fields[pick][take : take + 2]
    for copy in segment_copies:
        copy.wait()
    for k in range(blocks):
        here = slice(k * LANES, (k + 1) * LANES)
        turned_rows(
            data_ref, k, segment_ref[1, here, :], segment_ref[0, here, :], col_t[:, k : k + 1], count_t[:, k : k + 1]
        )


def edge_rows(n_ref, s_ref, pick, levels, level, cols):
    zero = lambda count: jnp.zeros((count, cols), F32)
    north = zero(2)
    if pick in UP:
        base = 2 * (UP.index(pick) * levels + level)
        north = n_ref[base : base + 2, :]
    south = zero(2)
    if pick in DOWN:
        base = 2 * (DOWN.index(pick) * levels + level)
        south = s_ref[base : base + 2, :]
    return jnp.concatenate([north, zero(4), south], axis=0)


def halves(tall):
    lane = iota((tall.shape[0], LANES), 1)
    return jnp.where(lane < LANES // 2, tall[:, :LANES], tall[:, -LANES:])


def gathered(talls, width):
    lane = iota((talls[0].shape[0], LANES), 1)
    mixed = jnp.zeros((talls[0].shape[0], LANES), F32)
    for at, tall in enumerate(talls):
        mixed = jnp.where(lane // (2 * width) == at, pltpu.roll(halves(tall), width + 2 * width * at, 1), mixed)
    return mixed


def scattered(mixed, at, width):
    return pltpu.roll(mixed, LANES - width - 2 * width * at, 1)


TRACER_WIDTH = 2
FACE_WIDTH = 8


GROUP = 4


def cols_kernel(token_ref, lam_ref, zonal_ref, merid_ref, mix_x_ref, mix_y_ref, *refs):
    surface_refs, height_refs, (n_ref, s_ref) = refs[:4], refs[4:6], refs[6:8]
    out_ref, far_ref, face_ref, height_ref, held_ref, flat_ref, tall_ref, sems, far_sems = refs[8:]
    levels, rows, cols = lam_ref.shape
    copies = []
    for group in range(levels // GROUP):
        block = pl.ds(group * GROUP, GROUP)
        for i, source in enumerate(
            (
                lam_ref.at[block],
                zonal_ref.at[1, block],
                merid_ref.at[1, block],
                zonal_ref.at[0, block],
                merid_ref.at[0, block],
                mix_x_ref.at[block],
                mix_y_ref.at[block],
            )
        ):
            copies.append(pltpu.make_async_copy(source, held_ref.at[i, block], sems.at[len(copies)]))
            copies[-1].start()
    keep = kept(token_ref, 0, rows, rows, cols)
    high = rows + 8
    used = 2 * TRACER_WIDTH * len(SIDE)
    blocks = levels * high // LANES
    base = blocks * used
    up, down = 2 * len(UP) * levels, 2 * len(DOWN) * levels
    talls = []
    for at, field in enumerate(surface_fields(keep, *surface_refs, slice(0, rows))):
        tall = jnp.concatenate(
            [field, n_ref[up + 8 * at : up + 8 * at + 8, :], s_ref[down + 8 * at : down + 8 * at + 8, :]], axis=0
        )
        face_ref[at] = tall
        talls.append(tall)
    for at, ref in enumerate(height_refs):
        height_ref[at] = ref[...]
        talls.append(jnp.concatenate([ref[...], jnp.zeros((16, cols), F32)], axis=0))
    out_ref[base : base + rows + 16, :] = gathered(talls, FACE_WIDTH)
    far = []
    for level in range(levels):
        if level % GROUP == 0:
            for copy in copies[7 * (level // GROUP) : 7 * (level // GROUP) + 7]:
                copy.wait()
        fields = tracer_fields(keep, *[held_ref[i, level] for i in range(7)])
        talls = []
        for pick, field in enumerate(fields):
            tall_ref[level, pick, 0:rows, :] = field
            edge = edge_rows(n_ref, s_ref, pick, levels, level, cols)
            tall_ref[level, pick, rows:high, :] = edge
            if pick in SIDE:
                talls.append(jnp.concatenate([field, edge], axis=0))
        flat_ref[level * high : (level + 1) * high, :] = gathered(talls, TRACER_WIDTH)
        far.append(pltpu.make_async_copy(tall_ref.at[level], far_ref.at[level], far_sems.at[level]))
        far[-1].start()
    for b in range(blocks):
        turned = jnp.transpose(flat_ref[b * LANES : (b + 1) * LANES, :])
        out_ref[b * used : (b + 1) * used, :] = turned[:used]
    for copy in far:
        copy.wait()


def side_kernel(e_ref, w_ref, token_ref, side_ref, flat_ref):
    levels, high = side_ref.shape[1:3]
    used = 2 * TRACER_WIDTH * len(SIDE)
    blocks = levels * high // LANES
    western = iota((used, LANES), 0) % (2 * TRACER_WIDTH) < TRACER_WIDTH
    for b in range(blocks):
        at = slice(b * used, (b + 1) * used)
        both = jnp.where(western, w_ref[at, :], e_ref[at, :])
        both = jnp.concatenate([both, jnp.zeros((LANES - used, LANES), F32)], axis=0)
        flat_ref[b * LANES : (b + 1) * LANES, :] = jnp.transpose(both)
    for level in range(levels):
        mixed = flat_ref[level * high : (level + 1) * high, :]
        for at in range(len(SIDE)):
            side_ref[at, level] = scattered(mixed, at, TRACER_WIDTH)


def face_halo_kernel(base, token_ref, tall_ref, height_ref, e_ref, w_ref, face_ref, full_ref):
    high = tall_ref.shape[1]
    rows = height_ref.shape[1]
    for at in range(2):
        full_ref[at, :, : -LANES] = height_ref[at]
    western = iota((high, LANES), 1) % (2 * FACE_WIDTH) < FACE_WIDTH
    here = slice(base, base + high)
    mixed = jnp.where(western, w_ref[here, :], e_ref[here, :])
    for at in range(2):
        full_ref[at, :, -LANES:] = scattered(mixed, 4 + at, FACE_WIDTH)[:rows]
    full = [jnp.concatenate([tall_ref[at], scattered(mixed, at, FACE_WIDTH)], axis=1) for at in range(4)]
    diag, east, north, ocean = full
    west, south = pltpu.roll(east, 1, 1), pltpu.roll(north, 1, 0)
    face_ref[0] = (1.0 + diag) + east + west + north + south
    for at, field in enumerate((east, west, north, south, ocean)):
        face_ref[1 + at] = field


def opening(token, tracer, surface, segments, marks, capacity):
    levels, rows, cols = tracer[0].shape
    up, down = 2 * len(UP) * levels + 32, 2 * len(DOWN) * levels + 32
    blocks = segments[0].shape[0] // LANES
    marks = tuple(mark.reshape(blocks, LANES) for mark in marks)
    return pl.pallas_call(
        functools.partial(opening_kernel, capacity),
        out_shape=(
            shape(up, cols),
            shape(down, cols),
            shape(*token.shape),
            jax.ShapeDtypeStruct((blocks * LANES, 4 * LANES), BF16),
            jax.ShapeDtypeStruct((blocks, LANES), jnp.int32),
            shape(LANES, LANES),
        ),
        in_specs=[VMEM] + [HBM] * 14,
        out_specs=(VMEM,) * 6,
        scratch_shapes=[
            pltpu.VMEM((12, levels, 8, cols), F32),
            pltpu.VMEM((2, 3, 8, cols), F32),
            pltpu.VMEM((2, 8, cols), jnp.int32),
            pltpu.VMEM((2, blocks * LANES, LANES), F32),
            pltpu.VMEM((3, blocks, LANES), jnp.int32),
            pltpu.SemaphoreType.DMA((12,)),
            pltpu.SemaphoreType.DMA((8,)),
            pltpu.SemaphoreType.DMA((4,)),
            pltpu.SemaphoreType.DMA((3,)),
        ],
        compiler_params=params(12),
        name="opening",
    )(token, *far(tracer), *far(surface), *far(segments), *far(marks))


def edges_to_tx(token, tracer, surface, heights, north, south):
    levels, rows, cols = tracer[0].shape
    high = rows + 8
    side_rows = 2 * TRACER_WIDTH * len(SIDE) * levels * high // LANES + rows + 16
    sides, tall, faces, heights = pl.pallas_call(
        cols_kernel,
        out_shape=(
            shape(side_rows, LANES),
            far_shape(levels, 9, high, cols),
            shape(4, rows + 16, cols),
            shape(2, rows, cols),
        ),
        in_specs=[VMEM] + [HBM] * 5 + [VMEM] * 8,
        out_specs=(VMEM, HBM, VMEM, VMEM),
        scratch_shapes=[
            pltpu.VMEM((7, levels, rows, cols), F32),
            pltpu.VMEM((levels * high, LANES), F32),
            pltpu.VMEM((levels, 9, high, cols), F32),
            pltpu.SemaphoreType.DMA((7 * levels // GROUP,)),
            pltpu.SemaphoreType.DMA((levels,)),
        ],
        compiler_params=params(24),
        name="edge_columns",
    )(token, *far(tracer), *far(surface), *far(heights), north, south)
    return (beside(sides, "tx", 1), beside(sides, "tx", -1)), tall, faces, heights


def faces_with_halo(token, tall, heights, east, west):
    count, high, cols = tall.shape
    return pl.pallas_call(
        functools.partial(face_halo_kernel, east.shape[0] - high),
        out_shape=(shape(6, high, cols + LANES), shape(2, heights.shape[1], cols + LANES)),
        in_specs=[VMEM] * 5,
        out_specs=(VMEM,) * 2,
        compiler_params=params(6),
        name="surface_halos",
    )(token, tall, heights, east, west)


def tracer_sides(token, levels, rows, east, west):
    high = rows + 8
    return pl.pallas_call(
        side_kernel,
        out_shape=shape(len(SIDE), levels, high, LANES),
        in_specs=[VMEM] * 3,
        out_specs=VMEM,
        scratch_shapes=[pltpu.VMEM((levels * high, LANES), F32)],
        compiler_params=params(8),
        name="tracer_halos",
    )(east, west, token)


def on_device(
    lam_tracer,
    lam_eta,
    land,
    zonal_flow,
    merid_flow,
    zonal_mixing,
    merid_mixing,
    surface_east,
    surface_north,
    surface_diag,
    steric,
    eta_saved,
    obs_sla,
    obs_weight,
    obs_tile,
    obs_start,
    obs_count,
):
    levels, rows, cols = lam_tracer.shape
    n_rows = lax.axis_size("ty")
    devices = n_rows * lax.axis_size("tx")
    capacity = 2 * obs_sla.shape[0] // devices
    token = jnp.full((8, LANES), lax.axis_index("ty") == n_rows - 1, F32)
    tracer = (lam_tracer, zonal_flow, merid_flow, zonal_mixing, merid_mixing)
    surface = (surface_diag, surface_east, surface_north, land)
    to_south, to_north, token, *ranked = opening(
        token, tracer, surface, (obs_sla, obs_weight), (obs_tile, obs_start, obs_count), capacity
    )
    around_ty = beside(to_south, "ty", 1), beside(to_north, "ty", -1)
    sent, token = placed(*ranked, token, capacity, devices // n_rows)
    sent, *around_ty = lax.optimization_barrier((sent, *around_ty))
    got = lax.all_to_all(
        sent.reshape(devices, 1, -1), AXES, split_axis=0, concat_axis=0, tiled=True
    ).reshape(sent.shape)
    around_tx, tall, faces, heights = edges_to_tx(token, tracer, surface, (lam_eta, eta_saved), *around_ty)
    faces, heights = faces_with_halo(token, faces, heights, *around_tx)
    rhs, token = unpack(got, heights, faces, token, capacity)
    north, south = beside(rhs[:8], "ty", 1), beside(rhs[-8:], "ty", -1)
    mine, krylov_fields, token = sums(rhs, north, south, faces, token)
    every = lax.all_to_all(
        mine.reshape(devices, 1, LANES), AXES, split_axis=0, concat_axis=0, tiled=True
    ).reshape(devices, LANES)
    sides = tracer_sides(token, levels, rows, *around_tx)
    return tracers(steric, every, krylov_fields, faces, tall, sides)


def solution(mesh):
    in_specs = (
        P(None, "ty", "tx"),
        P("ty", "tx"),
        P("ty", "tx"),
        P(None, None, "ty", "tx"),
        P(None, None, "ty", "tx"),
        P(None, "ty", "tx"),
        P(None, "ty", "tx"),
        P("ty", "tx"),
        P("ty", "tx"),
        P("ty", "tx"),
        P(),
        P("ty", "tx"),
        P(AXES, None),
        P(AXES, None),
        P(AXES, None),
        P(AXES),
        P(AXES),
    )
    out_specs = (P(None, "ty", "tx"), P("ty", "tx"))
    return jax.shard_map(
        on_device, mesh=mesh, in_specs=in_specs, out_specs=out_specs, check_vma=False
    )
```

```python
import functools

import jax
import jax.numpy as jnp
from jax import lax
from jax.experimental import pallas as pl
from jax.experimental.pallas import tpu as pltpu
from jax.sharding import PartitionSpec as P

AXES = ("ty", "tx")
SHIFT_0 = 1.6
SHIFT_1 = 35.0
SCALE_0 = 1.0 / 32.0
SCALE_1 = 1.0 / 16.0
LANES = 128
VMEM = pl.BlockSpec(memory_space=pltpu.VMEM)
SCALAR = pl.BlockSpec(memory_space=pltpu.SMEM)
HBM = pl.BlockSpec(memory_space=pltpu.HBM)
F32 = jnp.float32
BF16 = jnp.bfloat16


def params(mib):
    return pltpu.CompilerParams(vmem_limit_bytes=mib * 1024 * 1024)


def iota(dims, axis):
    return lax.broadcasted_iota(jnp.int32, dims, axis)


def shape(*dims):
    return jax.ShapeDtypeStruct(dims, F32)


def far_shape(*dims):
    return pltpu.HBM(dims, F32)


def far(arrays):
    return tuple(pltpu.with_memory_space_constraint(x, pltpu.HBM) for x in arrays)


def split(x):
    hi = x.astype(BF16)
    return hi, (x - hi.astype(F32)).astype(BF16)


def ranks(capacity, tile, start, count, place_ref, meta_ref):
    blocks = tile.shape[0]
    square = (LANES, LANES)
    sub, lane = iota(square, 0), iota(square, 1)
    prefix = jnp.concatenate([(sub < lane).astype(BF16), jnp.ones(square, BF16)], axis=1)
    carry = jnp.zeros(square, F32)
    hits, firsts = [], []
    for k in range(blocks):
        target = tile[k : k + 1]
        hit = sub == target
        hits.append(hit.astype(F32).astype(BF16))
        both = jnp.dot(hits[-1], prefix, preferred_element_type=F32)
        slot = jnp.sum(jnp.where(hit, both[:, :LANES] + carry, 0.0), axis=0, keepdims=True)
        carry = carry + both[:, LANES:]
        slot = slot.astype(jnp.int32)
        place_ref[k : k + 1, :] = target * capacity + slot
        begin = start[k : k + 1]
        block_of = jnp.where(sub == slot, begin // LANES, 0)
        lane_of = jnp.where(sub == slot + 64, begin & (LANES - 1), 0)
        firsts.append((block_of + lane_of).astype(F32).astype(BF16))
    meta_ref[...] = lax.dot_general(
        jnp.concatenate(hits, axis=1),
        jnp.concatenate(firsts, axis=1),
        (((1,), (1,)), ((), ())),
        preferred_element_type=F32,
    )
    col_t = jnp.transpose((start & (LANES - 1)).astype(F32)).astype(jnp.int32)
    return col_t, jnp.transpose(count.astype(F32)).astype(jnp.int32)


def turned_rows(data_ref, k, weight, sla, col, count):
    lane = iota((LANES, LANES), 1)
    weight = jnp.where(lane < count, weight, 0.0)
    value = weight * sla
    index = (lane - col) & (LANES - 1)
    weight = jnp.take_along_axis(weight, index, axis=1)
    value = jnp.take_along_axis(value, index, axis=1)
    data_ref[k * LANES : (k + 1) * LANES, :] = jnp.concatenate([*split(weight), *split(value)], axis=1)


EDGE = 5
WIDE = 2 * EDGE
FIRST_SLOTS = 12


def edge_lanes(rows):
    slot, lane = iota((rows, LANES), 0) % 16, iota((rows, LANES), 1)
    rest = 16 - FIRST_SLOTS
    late = slot - FIRST_SLOTS
    is_first = (lane // WIDE == slot) & (late < 0)
    is_late = ((lane // WIDE) % rest == late) & (lane < 2 * rest * WIDE)
    first = (lane - WIDE * slot) & (LANES - 1)
    second = (first + WIDE) & (LANES - 1)
    third = jnp.where(lane < rest * WIDE, lane - WIDE * late, lane - WIDE * (late + rest - 1)) & (LANES - 1)
    return (first, is_first), (second, is_first), (third, is_late)


def folded(parts):
    sub = iota((8, LANES), 0)
    for step in (4, 2, 1):
        low = (sub & step) == 0
        half = len(parts) // 2
        pairs = []
        for a, b in zip(parts[:half], parts[half:]):
            other = jnp.where(low, b, a)
            moved = jnp.where(low, pltpu.roll(other, 8 - step, 0), pltpu.roll(other, step, 0))
            pairs.append(jnp.where(low, a, b) + moved)
        parts = pairs
    return parts[0]


def place_kernel(capacity, n_cols, data_ref, place_ref, meta_ref, token_ref, out_ref, next_ref, made_ref, sems):
    next_ref[...] = token_ref[...]
    blocks = place_ref.shape[0]
    chunk = 2 * capacity + 4
    place = jnp.concatenate([place_ref[k : k + 1, :] for k in range(blocks)], axis=1)
    height = n_cols * capacity
    slots = iota((height, blocks * LANES), 0)
    lane = iota((capacity, LANES), 1)
    ends = jnp.where(lane < WIDE, lane % EDGE, LANES - EDGE + lane % EDGE)
    in_value = (lane // EDGE) % 2 == 1
    lanes = edge_lanes(capacity)
    western = iota((n_cols, LANES), 1) < WIDE * (16 - FIRST_SLOTS)
    east_of = lambda x: pltpu.roll(x, n_cols - 1, 0)
    west_of = lambda x: pltpu.roll(x, 1, 0)
    copies = []
    for g in range(LANES // n_cols):
        pick = (slots == place - g * height).astype(F32).astype(BF16)
        moved = jnp.dot(pick, data_ref[...], preferred_element_type=F32)
        weight = moved[:, :LANES] + moved[:, LANES : 2 * LANES]
        value = moved[:, 2 * LANES : 3 * LANES] + moved[:, 3 * LANES :]
        first = g * n_cols * chunk
        parts = [[], [], []]
        for t in range(n_cols):
            base = first + t * chunk
            rows = slice(t * capacity, (t + 1) * capacity)
            made_ref[base : base + capacity, :] = weight[rows]
            made_ref[base + capacity : base + 2 * capacity, :] = value[rows]
            both = jnp.where(
                in_value,
                jnp.take_along_axis(value[rows], ends, axis=1),
                jnp.take_along_axis(weight[rows], ends, axis=1),
            )
            for part, (index, mine) in zip(parts, lanes):
                spread = jnp.where(mine, jnp.take_along_axis(both, index, axis=1), 0.0)
                part.append(spread[:8] + spread[8:])
        edges = [
            jnp.concatenate([folded(part[i : i + 8]) for i in range(0, n_cols, 8)], axis=0) for part in parts
        ]
        meta = meta_ref[g * n_cols : (g + 1) * n_cols, :]
        meta = (
            meta + pltpu.roll(east_of(meta), capacity, 1) + pltpu.roll(west_of(meta), 2 * capacity, 1)
        )
        extra = (
            meta,
            east_of(edges[0]),
            west_of(edges[1]),
            jnp.where(western, east_of(edges[2]), west_of(edges[2])),
        )
        for i, rows in enumerate(extra):
            made_ref[pl.ds(first + 2 * capacity + i, n_cols, stride=chunk), :] = rows
        ready = pl.ds(first, n_cols * chunk)
        copies.append(pltpu.make_async_copy(made_ref.at[ready, :], out_ref.at[ready, :], sems.at[g]))
        copies[-1].start()
    for copy in copies:
        copy.wait()


def placed(data, place, meta, token, capacity, n_cols):
    chunk = 2 * capacity + 4
    return pl.pallas_call(
        functools.partial(place_kernel, capacity, n_cols),
        out_shape=(far_shape(LANES * chunk, LANES), shape(*token.shape)),
        in_specs=[VMEM] * 4,
        out_specs=(HBM, VMEM),
        scratch_shapes=[
            pltpu.VMEM((LANES * chunk, LANES), F32),
            pltpu.SemaphoreType.DMA((LANES // n_cols,)),
        ],
        compiler_params=params(12),
        name="place_segments",
    )(data, place, meta, token)


def unpack_kernel(capacity, got_ref, height_ref, face_ref, token_ref, q_ref, next_ref, sum_ref):
    next_ref[...] = token_ref[...]
    chunk = 2 * capacity + 4
    square = (LANES, LANES)
    lane = iota(square, 1)
    meta = got_ref[pl.ds(2 * capacity, LANES, stride=chunk), :]
    meta_t = jnp.transpose(meta)
    rows, cols = q_ref.shape[0], q_ref.shape[1] - LANES
    cells = rows * cols // LANES
    blocks = iota((cells, LANES), 0).astype(F32)
    lane_f = lane.astype(F32)
    acc = jnp.zeros((cells, 4 * LANES), F32)
    for j in range(capacity):
        weight = got_ref[pl.ds(j, LANES, stride=chunk), :]
        value = got_ref[pl.ds(capacity + j, LANES, stride=chunk), :]
        here = lane_f >= meta[:, 64 + j : 65 + j]
        hit = (blocks == meta_t[j : j + 1]).astype(F32).astype(BF16)
        his, los = [], []
        for x in (weight, value):
            hi = x.astype(BF16).astype(F32)
            lo = x - hi
            for keep in (here, ~here):
                his.append(jnp.where(keep, hi, 0.0).astype(BF16))
                los.append(jnp.where(keep, lo, 0.0).astype(BF16))
        data = jnp.concatenate(
            [jnp.concatenate(his, axis=1), jnp.concatenate(los, axis=1)], axis=0
        )
        acc = acc + jnp.dot(
            jnp.concatenate([hit, hit], axis=1), data, preferred_element_type=F32
        )
    for i in range(2):
        here, after = acc[:, 2 * i * LANES : (2 * i + 1) * LANES], acc[:, (2 * i + 1) * LANES : (2 * i + 2) * LANES]
        sum_ref[i, :, :] = here + pltpu.roll(after, 1, 0)
    for half in range(2):
        at = slice(half * LANES, (half + 1) * LANES)
        weight = sum_ref[0, pl.ds(half, rows, stride=2), :]
        value = sum_ref[1, pl.ds(half, rows, stride=2), :]
        mu = height_ref[0, :, at] + (weight * height_ref[1, :, at] - value)
        q_ref[:, at] = face_ref[5, 0:rows, at] * mu

    row_of = iota((rows, LANES), 0).astype(F32)
    group = iota((rows, LANES), 1) // WIDE
    rest = capacity - FIRST_SLOTS
    at = lane % EDGE
    first = capacity + jnp.minimum(lane // WIDE, FIRST_SLOTS - 1)
    late = capacity + FIRST_SLOTS + (lane // WIDE) % rest
    western = lane < rest * WIDE
    edges = []
    for i, (index, is_west) in enumerate(
        ((first, True), (first + capacity, False), (jnp.where(western, late, late + capacity), western))
    ):
        block = jnp.take_along_axis(meta, index, axis=1)
        start = jnp.take_along_axis(meta, index + 64, axis=1).astype(jnp.int32)
        odd = block != 2.0 * jnp.floor(0.5 * block)
        has_west = ~odd & (at >= start)
        has_east = odd | (LANES - EDGE + at < start)
        if is_west is True:
            valid = has_west
        elif is_west is False:
            valid = has_east
        else:
            valid = (is_west & has_west) | (~is_west & has_east)
        edge = got_ref[pl.ds(2 * capacity + 1 + i, LANES, stride=chunk), :]
        edges.append(jnp.concatenate(split(jnp.where(valid, edge, 0.0)), axis=0))

    def edge_sum(base, row, first_group):
        hits = []
        for j in range(capacity):
            hits.append((row_of == jnp.floor(0.5 * meta_t[base + j : base + j + 1])).astype(F32).astype(BF16))

        def spread(picks, edge):
            hit = jnp.concatenate(picks, axis=0)
            return jnp.dot(jnp.concatenate([hit, hit], axis=1), edges[edge], preferred_element_type=F32)

        total = jnp.zeros((rows, LANES), F32)
        full = spread(hits[:FIRST_SLOTS], row)
        for j in range(FIRST_SLOTS):
            total = jnp.where(group == j, full[j * rows : (j + 1) * rows], total)
        tail = spread(hits[FIRST_SLOTS:], 2)
        late = jnp.zeros((rows, LANES), F32)
        for j in range(rest):
            late = jnp.where(group == first_group + j, tail[j * rows : (j + 1) * rows], late)
        if first_group:
            late = pltpu.roll(late, LANES - WIDE * first_group, 1)
        total = total + late
        total = total + pltpu.roll(total, LANES - 6 * WIDE, 1)
        total = total + pltpu.roll(total, LANES - 3 * WIDE, 1)
        total = total + pltpu.roll(total, LANES - WIDE, 1) + pltpu.roll(total, LANES - 2 * WIDE, 1)
        return total, pltpu.roll(total, LANES - EDGE, 1)

    side = slice(cols, cols + LANES)
    eastern = iota((rows, LANES), 1) < LANES // 2
    weight, value = [
        jnp.where(eastern, e, pltpu.roll(w, LANES - EDGE, 1))
        for e, w in zip(edge_sum(capacity, 0, 0), edge_sum(2 * capacity, 1, rest))
    ]
    mu = height_ref[0, :, side] + (weight * height_ref[1, :, side] - value)
    q_ref[:, side] = face_ref[5, 0:rows, side] * mu


def unpack(got, heights, faces, token, capacity):
    rows, wide = heights.shape[1:]
    return pl.pallas_call(
        functools.partial(unpack_kernel, capacity),
        out_shape=(shape(rows, wide), shape(*token.shape)),
        in_specs=[VMEM] * 4,
        out_specs=(VMEM, VMEM),
        scratch_shapes=[pltpu.VMEM((2, rows * (wide - LANES) // LANES, LANES), F32)],
        compiler_params=params(10),
        name="forcing",
    )(got, heights, faces, token)


def two_sum(a, b):
    s = a + b
    t = s - a
    return s, (a - (s - t)) + (b - t)


def pair_sum(x, y):
    s, e = two_sum(x[0], y[0])
    e = e + (x[1] + y[1])
    return s, e


def tree(parts):
    while len(parts) > 1:
        odd = parts[len(parts) // 2 * 2 :]
        parts = [pair_sum(parts[i], parts[i + 1]) for i in range(0, len(parts) - 1, 2)] + odd
    return parts[0]


def rows_sum(hi):
    zero = jnp.zeros((8, LANES), F32)
    total = tree([(hi[8 * i : 8 * i + 8], zero) for i in range(16)])
    for step in (4, 2, 1):
        total = pair_sum(total, (pltpu.roll(total[0], step, 0), pltpu.roll(total[1], step, 0)))
    return total


def krylov(apply, start):
    first = apply(start)
    one = SCALE_0 * (first - SHIFT_0 * start)
    second = apply(one)
    two = SCALE_1 * (second - SHIFT_1 * one)
    return (start, one, two), (first, second, apply(two))


def sums_kernel(q_ref, north_ref, south_ref, face_ref, token_ref, row_ref, field_ref, next_ref, part_ref):
    next_ref[...] = token_ref[...]
    rows, cols = q_ref.shape[0], q_ref.shape[1] - LANES
    high, wide = rows + 16, cols + LANES
    q = jnp.concatenate([q_ref[...], north_ref[...], south_ref[...]], axis=0)

    def apply(v):
        return (
            face_ref[0] * v
            - face_ref[1] * pltpu.roll(v, wide - 1, 1)
            - face_ref[2] * pltpu.roll(v, 1, 1)
            - face_ref[3] * pltpu.roll(v, high - 1, 0)
            - face_ref[4] * pltpu.roll(v, 1, 0)
        )

    def inner(at, a, b):
        p = a[:rows, :cols] * b[:rows, :cols]
        p = (p[0:8] + p[8:16]) + (p[16:24] + p[24:32])
        part_ref[8 * at : 8 * at + 8, :] = p[:, :LANES] + p[:, LANES:]

    w, aw = krylov(apply, q)
    y, ay = zip(*[krylov(apply, face_ref[5] * v) for v in w])
    for i in range(3):
        field_ref[i] = w[i]
        field_ref[3 + 2 * i] = y[i][1]
        field_ref[4 + 2 * i] = y[i][2]
    orders = [(k, l) for k in range(3) for l in range(k + 1)]
    at = 0
    for i in range(3):
        for j in range(3):
            for k, l in orders:
                inner(at, y[i][k], ay[j][l])
                at += 1
            for k in range(3):
                inner(at, y[i][k], y[j][0])
                at += 1
    for k, l in orders:
        inner(at, w[k], aw[l])
        at += 1
    for k in range(3):
        inner(at, w[k], q)
        at += 1
    part_ref[8 * at :, :] = jnp.zeros((8 * (LANES - at), LANES), F32)
    zero = jnp.zeros((LANES, LANES), F32)
    pieces = [(part_ref[pl.ds(s, LANES, stride=8), :], zero) for s in range(8)]
    hi, lo = tree(pieces)
    hi, lo = jnp.transpose(hi), jnp.transpose(lo)
    total = rows_sum(hi)
    row = total[0] + (total[1] + rows_sum(lo)[0])
    row_ref[...] = jnp.broadcast_to(row[0:1], row_ref.shape)


def sums(q, north, south, faces, token):
    rows, wide = q.shape
    return pl.pallas_call(
        sums_kernel,
        out_shape=(shape(LANES, LANES), shape(9, rows + 16, wide), shape(*token.shape)),
        in_specs=[VMEM] * 5,
        out_specs=(VMEM,) * 3,
        scratch_shapes=[pltpu.VMEM((8 * LANES, LANES), F32)],
        compiler_params=params(8),
        name="krylov_sums",
    )(q, north, south, faces, token)


def two_prod(a, b):
    p = a * b
    t = 4097.0 * a
    ah = t - (t - a)
    al = a - ah
    t = 4097.0 * b
    bh = t - (t - b)
    bl = b - bh
    return p, ((ah * bh - p) + (ah * bl + al * bh)) + al * bl


def quick(s, e):
    t = s + e
    return t, e - (t - s)


def pair_add(x, y):
    s, e = two_sum(x[0], y[0])
    return quick(s, e + (x[1] + y[1]))


def pair_neg(x):
    return -x[0], -x[1]


def pair_mul(x, y):
    p, e = two_prod(x[0], y[0])
    return quick(p, e + (x[0] * y[1] + x[1] * y[0]))


def pair_div(x, y):
    first = x[0] / y[0]
    p, e = two_prod(first, y[0])
    rest = ((x[0] - p) - e) + (x[1] - first * y[1])
    return quick(first, rest / y[0])


def minor(a, b, c, d):
    return pair_add(pair_mul(a, b), pair_neg(pair_mul(c, d)))


def pair_sum3(a, b, c):
    return pair_add(pair_add(a, b), c)


def small_solve(g, b):
    g00, g10, g11, g20, g21, g22 = g
    c00, c01, c02 = minor(g11, g22, g21, g21), minor(g20, g21, g10, g22), minor(g10, g21, g20, g11)
    c11, c12, c22 = minor(g00, g22, g20, g20), minor(g10, g20, g00, g21), minor(g00, g11, g10, g10)
    det = pair_sum3(pair_mul(g00, c00), pair_mul(g10, c01), pair_mul(g20, c02))
    three = det[0] > 1e-8 * (c22[0] * g22[0])
    two = c22[0] > 1e-8 * (g00[0] * g11[0])
    three = three & two
    rows = ((c00, c01, c02), (c01, c11, c12), (c02, c12, c22))
    full = [pair_div(pair_sum3(*[pair_mul(m, v) for m, v in zip(row, b)]), det)[0] for row in rows]
    half = [
        pair_div(minor(g11, b[0], g10, b[1]), c22)[0],
        pair_div(minor(g00, b[1], g10, b[0]), c22)[0],
        jnp.zeros_like(det[0]),
    ]
    alone = [b[0][0] / g00[0], half[2], half[2]]
    return [jnp.where(three, x, jnp.where(two, y, z)) for x, y, z in zip(full, half, alone)]


def coefficients(every_ref):
    total = quick(*rows_sum(every_ref[...]))

    def pick(x, at):
        return tuple(jnp.broadcast_to(v[:, at : at + 1], (8, LANES)) for v in x)

    def scaled(x, at):
        by = 1.0 / jnp.broadcast_to(x[0][:, at : at + 1], (8, LANES))
        p, e = two_prod(x[0], by)
        return quick(p, e + x[1] * by)

    first = scaled(total, 81)
    first = [pick(first, 81 + m) for m in range(9)]
    c = small_solve(first[:6], first[6:])
    terms = []
    for i in range(3):
        for j in range(3):
            shift = (LANES - 9 * (3 * i + j)) % LANES
            row = tuple(pltpu.roll(v, shift, 1) if shift else v for v in total)
            terms.append(pair_mul(row, two_prod(c[i], c[j])))
    while len(terms) > 1:
        odd = terms[len(terms) // 2 * 2 :]
        terms = [pair_add(terms[i], terms[i + 1]) for i in range(0, len(terms) - 1, 2)] + odd
    second = scaled(terms[0], 0)
    second = [pick(second, m) for m in range(9)]
    return c, small_solve(second[:6], second[6:])


def tracer_kernel(steric_ref, every_ref, field_ref, face_ref, far_ref, side_ref, mu_ref, rho_ref, tall_ref, sems):
    levels, rows, cols = mu_ref.shape

    def copy(level):
        return pltpu.make_async_copy(far_ref.at[level], tall_ref.at[level], sems.at[level])

    for level in range(levels):
        copy(level).start()
    high, wide = rows + 8, cols + LANES

    def trim(v):
        edge = jnp.where(iota((8, wide), 0) < 4, v[rows : rows + 8], v[rows + 8 :])
        return jnp.concatenate([v[:rows], edge], axis=0)

    c, e = coefficients(every_ref)
    c, e = [[jnp.broadcast_to(v[0:1, 0:1], (1, 1)) for v in part] for part in (c, e)]
    w = [trim(field_ref[i]) for i in range(3)]
    ocean = trim(face_ref[5])
    rho_1 = c[0] * w[0] + c[1] * w[1] + c[2] * w[2]
    rho_0 = e[0] * (ocean * rho_1)
    for k in (1, 2):
        v = [trim(field_ref[2 + k + 2 * i]) for i in range(3)]
        rho_0 = rho_0 + e[k] * (c[0] * v[0] + c[1] * v[1] + c[2] * v[2])
    rho_ref[...] = rho_0[:rows, :cols]

    def one_level(level):
        height = steric_ref[level]
        full = lambda at: jnp.concatenate([tall_ref[level, at], side_ref[at, level]], axis=1)
        g = ocean * (full(0) + height * rho_1)
        dx = g - pltpu.roll(g, wide - 1, 1)
        dy = g - pltpu.roll(g, high - 1, 0)
        mu = g - (
            full(1) * dx + pltpu.roll(full(2) * dx, 1, 1) + full(3) * dy + pltpu.roll(full(4) * dy, 1, 0)
        )
        g = ocean * (mu + height * rho_0)
        dx = (g - pltpu.roll(g, wide - 1, 1))[:rows]
        dy = (g - pltpu.roll(g, high - 1, 0))[:, :cols]
        back_x = pltpu.roll(full(5)[:rows] * dx, 1, 1)[:, :cols]
        back_y = pltpu.roll(tall_ref[level, 6] * dy, 1, 0)[:rows]
        mu_ref[level] = g[:rows, :cols] - (
            tall_ref[level, 7, 0:rows, :] * dx[:, :cols] + back_x + tall_ref[level, 8, 0:rows, :] * dy[:rows] + back_y
        )

    def some_levels(group, carry):
        for i in range(GROUP):
            copy(group * GROUP + i).wait()
        for i in range(GROUP):
            one_level(group * GROUP + i)
        return carry

    lax.fori_loop(0, levels // GROUP, some_levels, 0)


def tracers(steric, every, fields, faces, tall, side):
    levels, count, high, cols = tall.shape
    rows = high - 8
    return pl.pallas_call(
        tracer_kernel,
        out_shape=(shape(levels, rows, cols), shape(rows, cols)),
        in_specs=[SCALAR] + [VMEM] * 3 + [HBM, VMEM],
        out_specs=(VMEM, VMEM),
        scratch_shapes=[pltpu.VMEM((levels, count, high, cols), F32), pltpu.SemaphoreType.DMA((levels,))],
        compiler_params=params(20),
        name="tracer_steps",
    )(steric, every, fields, faces, *far((tall,)), side)


def beside(cells, axis, step):
    count = lax.axis_size(axis)
    return lax.ppermute(cells, axis, [((i + step) % count, i) for i in range(count)])


def tracer_fields(keep, lam, zonal_1, merid_1, zonal_0, merid_0, mix_x, mix_y):
    flow_x, flow_y = 0.5 * zonal_1, 0.5 * merid_1
    past_x, past_y = 0.5 * zonal_0, 0.5 * merid_0
    return (
        lam,
        flow_x + mix_x,
        flow_x - mix_x,
        keep * (flow_y + mix_y),
        keep * (flow_y - mix_y),
        past_x - mix_x,
        keep * (past_y - mix_y),
        past_x + mix_x,
        keep * (past_y + mix_y),
    )


def surface_fields(keep, diag_ref, east_ref, north_ref, land_ref, rows):
    return diag_ref[rows], east_ref[rows], keep * north_ref[rows], land_ref[rows].astype(F32)


UP = (0, 1, 2, 3)
DOWN = (0, 1, 2, 3, 4, 6)
SIDE = (0, 1, 2, 3, 4, 5)


def kept(token_ref, first, count, rows, cols):
    last = jnp.concatenate([token_ref[0:1, :]] * (cols // LANES), axis=1)
    return jnp.where((iota((count, cols), 0) + first == rows - 1) & (last == 1.0), 0.0, 1.0)


def opening_kernel(capacity, token_ref, lam_ref, zonal_ref, merid_ref, mix_x_ref, mix_y_ref, *refs):
    surface_refs, (sla_ref, weight_ref), marks = refs[:4], refs[4:6], refs[6:9]
    up_ref, down_ref, next_ref, data_ref, place_ref, meta_ref = refs[9:15]
    held_ref, flat_ref, land_ref, segment_ref, mark_ref, sems, flat_sems, segment_sems, mark_sems = refs[15:]
    levels, rows, cols = lam_ref.shape
    blocks = mark_ref.shape[1]

    def started(source, target, sem):
        copy = pltpu.make_async_copy(source, target, sem)
        copy.start()
        return copy

    mark_copies = [started(ref, mark_ref.at[i], mark_sems.at[i]) for i, ref in enumerate(marks)]
    segment_copies = []
    for k in range(2):
        block = pl.ds(k * blocks * LANES // 2, blocks * LANES // 2)
        for i, ref in enumerate((sla_ref, weight_ref)):
            segment_copies.append(started(ref.at[block, :], segment_ref.at[i, block, :], segment_sems.at[2 * k + i]))
    copies, flat_copies = [], []
    for part, (first, outer) in enumerate(((0, 0), (rows - 8, rows - 2))):
        block = pl.ds(outer, 2)
        for source in (
            lam_ref.at[:, block, :],
            zonal_ref.at[1, :, block, :],
            merid_ref.at[1, :, block, :],
            mix_x_ref.at[:, block, :],
            mix_y_ref.at[:, block, :],
            merid_ref.at[0, :, block, :],
        )[: 5 + part]:
            copies.append(started(source, held_ref.at[len(copies)], sems.at[len(copies)]))
        block = pl.ds(first, 8)
        for i, ref in enumerate(surface_refs[:3]):
            flat_copies.append(started(ref.at[block, :], flat_ref.at[part, i], flat_sems.at[len(flat_copies)]))
        ref = surface_refs[3]
        flat_copies.append(started(ref.at[block, :], land_ref.at[part], flat_sems.at[len(flat_copies)]))
    next_ref[...] = token_ref[...]

    for copy in mark_copies:
        copy.wait()
    col_t, count_t = ranks(capacity, mark_ref[0], mark_ref[1], mark_ref[2], place_ref, meta_ref)
    for copy in copies + flat_copies:
        copy.wait()
    for part, (out_ref, picks, first, take) in enumerate(((up_ref, UP, 0, 0), (down_ref, DOWN, rows - 8, 6))):
        keep = kept(token_ref, first, 8, rows, cols)
        base = 2 * len(picks) * levels
        diag, east, north = [flat_ref[part, i] for i in range(3)]
        ocean = land_ref[part].astype(F32)
        for at, field in enumerate((diag, east, keep * north, ocean)):
            out_ref[base + 8 * at : base + 8 * at + 8, :] = field
        for level in range(levels):
            lam, zonal_1, merid_1, mix_x, mix_y, merid_0 = [held_ref[5 * part + min(i, 4 + part), level] for i in range(6)]
            fields = tracer_fields(keep[take : take + 2], lam, zonal_1, merid_1, zonal_1, merid_0, mix_x, mix_y)
            for at, pick in enumerate(picks):
                base = 2 * (at * levels + level)
                out_ref[base : base + 2, :] = fields[pick]
    for copy in segment_copies:
        copy.wait()
    for k in range(blocks):
        here = slice(k * LANES, (k + 1) * LANES)
        turned_rows(
            data_ref, k, segment_ref[1, here, :], segment_ref[0, here, :], col_t[:, k : k + 1], count_t[:, k : k + 1]
        )


def edge_rows(n_ref, s_ref, pick, levels, level, cols):
    zero = lambda count: jnp.zeros((count, cols), F32)
    north = zero(2)
    if pick in UP:
        base = 2 * (UP.index(pick) * levels + level)
        north = n_ref[base : base + 2, :]
    south = zero(2)
    if pick in DOWN:
        base = 2 * (DOWN.index(pick) * levels + level)
        south = s_ref[base : base + 2, :]
    return jnp.concatenate([north, zero(4), south], axis=0)


def halves(tall):
    lane = iota((tall.shape[0], LANES), 1)
    return jnp.where(lane < LANES // 2, tall[:, :LANES], tall[:, -LANES:])


def gathered(talls, width):
    lane = iota((talls[0].shape[0], LANES), 1)
    mixed = jnp.zeros((talls[0].shape[0], LANES), F32)
    for at, tall in enumerate(talls):
        mixed = jnp.where(lane // (2 * width) == at, pltpu.roll(halves(tall), width + 2 * width * at, 1), mixed)
    return mixed


def scattered(mixed, at, width):
    return pltpu.roll(mixed, LANES - width - 2 * width * at, 1)


TRACER_WIDTH = 2
FACE_WIDTH = 8


GROUP = 4


def cols_kernel(token_ref, lam_ref, zonal_ref, merid_ref, mix_x_ref, mix_y_ref, *refs):
    surface_refs, height_refs, (n_ref, s_ref) = refs[:4], refs[4:6], refs[6:8]
    out_ref, far_ref, face_ref, height_ref, held_ref, flat_ref, tall_ref, sems, far_sems = refs[8:]
    levels, rows, cols = lam_ref.shape
    copies = []
    for group in range(levels // GROUP):
        block = pl.ds(group * GROUP, GROUP)
        for i, source in enumerate(
            (
                lam_ref.at[block],
                zonal_ref.at[1, block],
                merid_ref.at[1, block],
                zonal_ref.at[0, block],
                merid_ref.at[0, block],
                mix_x_ref.at[block],
                mix_y_ref.at[block],
            )
        ):
            copies.append(pltpu.make_async_copy(source, held_ref.at[i, block], sems.at[len(copies)]))
            copies[-1].start()
    keep = kept(token_ref, 0, rows, rows, cols)
    high = rows + 8
    used = 2 * TRACER_WIDTH * len(SIDE)
    blocks = levels * high // LANES
    base = blocks * used
    up, down = 2 * len(UP) * levels, 2 * len(DOWN) * levels
    talls = []
    for at, field in enumerate(surface_fields(keep, *surface_refs, slice(0, rows))):
        tall = jnp.concatenate(
            [field, n_ref[up + 8 * at : up + 8 * at + 8, :], s_ref[down + 8 * at : down + 8 * at + 8, :]], axis=0
        )
        face_ref[at] = tall
        talls.append(tall)
    for at, ref in enumerate(height_refs):
        height_ref[at] = ref[...]
        talls.append(jnp.concatenate([ref[...], jnp.zeros((16, cols), F32)], axis=0))
    out_ref[base : base + rows + 16, :] = gathered(talls, FACE_WIDTH)
    far = []
    for level in range(levels):
        if level % GROUP == 0:
            for copy in copies[7 * (level // GROUP) : 7 * (level // GROUP) + 7]:
                copy.wait()
        fields = tracer_fields(keep, *[held_ref[i, level] for i in range(7)])
        talls = []
        for pick, field in enumerate(fields):
            tall_ref[level, pick, 0:rows, :] = field
            edge = edge_rows(n_ref, s_ref, pick, levels, level, cols)
            tall_ref[level, pick, rows:high, :] = edge
            if pick in SIDE:
                talls.append(jnp.concatenate([field, edge], axis=0))
        flat_ref[level * high : (level + 1) * high, :] = gathered(talls, TRACER_WIDTH)
        far.append(pltpu.make_async_copy(tall_ref.at[level], far_ref.at[level], far_sems.at[level]))
        far[-1].start()
    for b in range(blocks):
        turned = jnp.transpose(flat_ref[b * LANES : (b + 1) * LANES, :])
        out_ref[b * used : (b + 1) * used, :] = turned[:used]
    for copy in far:
        copy.wait()


def side_kernel(strip_ref, token_ref, side_ref, flat_ref):
    levels, high = side_ref.shape[1:3]
    used = 2 * TRACER_WIDTH * len(SIDE)
    blocks = levels * high // LANES
    for b in range(blocks):
        both = strip_ref[b * used : (b + 1) * used, :]
        both = jnp.concatenate([both, jnp.zeros((LANES - used, LANES), F32)], axis=0)
        flat_ref[b * LANES : (b + 1) * LANES, :] = jnp.transpose(both)
    for level in range(levels):
        mixed = flat_ref[level * high : (level + 1) * high, :]
        for at in range(len(SIDE)):
            side_ref[at, level] = scattered(mixed, at, TRACER_WIDTH)


def face_halo_kernel(base, token_ref, tall_ref, height_ref, e_ref, w_ref, face_ref, full_ref, strip_ref):
    from_west = iota((base, LANES), 0) % (2 * TRACER_WIDTH) < TRACER_WIDTH
    strip_ref[...] = jnp.where(from_west, w_ref[0:base, :], e_ref[0:base, :])
    high = tall_ref.shape[1]
    rows = height_ref.shape[1]
    for at in range(2):
        full_ref[at, :, : -LANES] = height_ref[at]
    western = iota((high, LANES), 1) % (2 * FACE_WIDTH) < FACE_WIDTH
    here = slice(base, base + high)
    mixed = jnp.where(western, w_ref[here, :], e_ref[here, :])
    for at in range(2):
        full_ref[at, :, -LANES:] = scattered(mixed, 4 + at, FACE_WIDTH)[:rows]
    full = [jnp.concatenate([tall_ref[at], scattered(mixed, at, FACE_WIDTH)], axis=1) for at in range(4)]
    diag, east, north, ocean = full
    west, south = pltpu.roll(east, 1, 1), pltpu.roll(north, 1, 0)
    face_ref[0] = (1.0 + diag) + east + west + north + south
    for at, field in enumerate((east, west, north, south, ocean)):
        face_ref[1 + at] = field


def opening(token, tracer, surface, segments, marks, capacity):
    levels, rows, cols = tracer[0].shape
    up, down = 2 * len(UP) * levels + 32, 2 * len(DOWN) * levels + 32
    blocks = segments[0].shape[0] // LANES
    marks = tuple(mark.reshape(blocks, LANES) for mark in marks)
    return pl.pallas_call(
        functools.partial(opening_kernel, capacity),
        out_shape=(
            shape(up, cols),
            shape(down, cols),
            shape(*token.shape),
            jax.ShapeDtypeStruct((blocks * LANES, 4 * LANES), BF16),
            jax.ShapeDtypeStruct((blocks, LANES), jnp.int32),
            shape(LANES, LANES),
        ),
        in_specs=[VMEM] + [HBM] * 14,
        out_specs=(VMEM,) * 6,
        scratch_shapes=[
            pltpu.VMEM((11, levels, 2, cols), F32),
            pltpu.VMEM((2, 3, 8, cols), F32),
            pltpu.VMEM((2, 8, cols), jnp.int32),
            pltpu.VMEM((2, blocks * LANES, LANES), F32),
            pltpu.VMEM((3, blocks, LANES), jnp.int32),
            pltpu.SemaphoreType.DMA((11,)),
            pltpu.SemaphoreType.DMA((8,)),
            pltpu.SemaphoreType.DMA((4,)),
            pltpu.SemaphoreType.DMA((3,)),
        ],
        compiler_params=params(12),
        name="opening",
    )(token, *far(tracer), *far(surface), *far(segments), *far(marks))


def edges_to_tx(token, tracer, surface, heights, north, south):
    levels, rows, cols = tracer[0].shape
    high = rows + 8
    side_rows = 2 * TRACER_WIDTH * len(SIDE) * levels * high // LANES + rows + 16
    sides, tall, faces, heights = pl.pallas_call(
        cols_kernel,
        out_shape=(
            shape(side_rows, LANES),
            far_shape(levels, 9, high, cols),
            shape(4, rows + 16, cols),
            shape(2, rows, cols),
        ),
        in_specs=[VMEM] + [HBM] * 5 + [VMEM] * 8,
        out_specs=(VMEM, HBM, VMEM, VMEM),
        scratch_shapes=[
            pltpu.VMEM((7, levels, rows, cols), F32),
            pltpu.VMEM((levels * high, LANES), F32),
            pltpu.VMEM((levels, 9, high, cols), F32),
            pltpu.SemaphoreType.DMA((7 * levels // GROUP,)),
            pltpu.SemaphoreType.DMA((levels,)),
        ],
        compiler_params=params(24),
        name="edge_columns",
    )(token, *far(tracer), *far(surface), *far(heights), north, south)
    return (beside(sides, "tx", 1), beside(sides, "tx", -1)), tall, faces, heights


def faces_with_halo(token, tall, heights, east, west):
    count, high, cols = tall.shape
    base = east.shape[0] - high
    return pl.pallas_call(
        functools.partial(face_halo_kernel, base),
        out_shape=(shape(6, high, cols + LANES), shape(2, heights.shape[1], cols + LANES), shape(base, LANES)),
        in_specs=[VMEM] * 5,
        out_specs=(VMEM,) * 3,
        compiler_params=params(6),
        name="surface_halos",
    )(token, tall, heights, east, west)


def tracer_sides(token, strips, levels, rows):
    high = rows + 8
    return pl.pallas_call(
        side_kernel,
        out_shape=shape(len(SIDE), levels, high, LANES),
        in_specs=[VMEM] * 2,
        out_specs=VMEM,
        scratch_shapes=[pltpu.VMEM((levels * high, LANES), F32)],
        compiler_params=params(8),
        name="tracer_halos",
    )(strips, token)


def on_device(
    lam_tracer,
    lam_eta,
    land,
    zonal_flow,
    merid_flow,
    zonal_mixing,
    merid_mixing,
    surface_east,
    surface_north,
    surface_diag,
    steric,
    eta_saved,
    obs_sla,
    obs_weight,
    obs_tile,
    obs_start,
    obs_count,
):
    levels, rows, cols = lam_tracer.shape
    n_rows = lax.axis_size("ty")
    devices = n_rows * lax.axis_size("tx")
    capacity = 2 * obs_sla.shape[0] // devices
    token = jnp.full((8, LANES), lax.axis_index("ty") == n_rows - 1, F32)
    tracer = (lam_tracer, zonal_flow, merid_flow, zonal_mixing, merid_mixing)
    surface = (surface_diag, surface_east, surface_north, land)
    to_south, to_north, token, *ranked = opening(
        token, tracer, surface, (obs_sla, obs_weight), (obs_tile, obs_start, obs_count), capacity
    )
    around_ty = beside(to_south, "ty", 1), beside(to_north, "ty", -1)
    sent, token = placed(*ranked, token, capacity, devices // n_rows)
    sent, *around_ty = lax.optimization_barrier((sent, *around_ty))
    got = lax.all_to_all(
        sent.reshape(devices, 1, -1), AXES, split_axis=0, concat_axis=0, tiled=True
    ).reshape(sent.shape)
    around_tx, tall, faces, heights = edges_to_tx(token, tracer, surface, (lam_eta, eta_saved), *around_ty)
    faces, heights, strips = faces_with_halo(token, faces, heights, *around_tx)
    rhs, token = unpack(got, heights, faces, token, capacity)
    north, south = beside(rhs[:8], "ty", 1), beside(rhs[-8:], "ty", -1)
    mine, krylov_fields, token = sums(rhs, north, south, faces, token)
    every = lax.all_to_all(
        mine.reshape(devices, 1, LANES), AXES, split_axis=0, concat_axis=0, tiled=True
    ).reshape(devices, LANES)
    sides = tracer_sides(token, strips, levels, rows)
    return tracers(steric, every, krylov_fields, faces, tall, sides)


def solution(mesh):
    in_specs = (
        P(None, "ty", "tx"),
        P("ty", "tx"),
        P("ty", "tx"),
        P(None, None, "ty", "tx"),
        P(None, None, "ty", "tx"),
        P(None, "ty", "tx"),
        P(None, "ty", "tx"),
        P("ty", "tx"),
        P("ty", "tx"),
        P("ty", "tx"),
        P(),
        P("ty", "tx"),
        P(AXES, None),
        P(AXES, None),
        P(AXES, None),
        P(AXES),
        P(AXES),
    )
    out_specs = (P(None, "ty", "tx"), P("ty", "tx"))
    return jax.shard_map(
        on_device, mesh=mesh, in_specs=in_specs, out_specs=out_specs, check_vma=False
    )
```

```python
import functools

import jax
import jax.numpy as jnp
from jax import lax
from jax.experimental import pallas as pl
from jax.experimental.pallas import tpu as pltpu
from jax.sharding import PartitionSpec as P

AXES = ("ty", "tx")
SHIFT_0 = 1.6
SHIFT_1 = 35.0
SCALE_0 = 1.0 / 32.0
SCALE_1 = 1.0 / 16.0
LANES = 128
VMEM = pl.BlockSpec(memory_space=pltpu.VMEM)
SCALAR = pl.BlockSpec(memory_space=pltpu.SMEM)
HBM = pl.BlockSpec(memory_space=pltpu.HBM)
F32 = jnp.float32
BF16 = jnp.bfloat16


def params(mib):
    return pltpu.CompilerParams(vmem_limit_bytes=mib * 1024 * 1024)


def iota(dims, axis):
    return lax.broadcasted_iota(jnp.int32, dims, axis)


def shape(*dims):
    return jax.ShapeDtypeStruct(dims, F32)


def far_shape(*dims):
    return pltpu.HBM(dims, F32)


def far(arrays):
    return tuple(pltpu.with_memory_space_constraint(x, pltpu.HBM) for x in arrays)


def split(x):
    hi = x.astype(BF16)
    return hi, (x - hi.astype(F32)).astype(BF16)


def ranks(capacity, tile, start, count, place_ref, meta_ref):
    blocks = tile.shape[0]
    square = (LANES, LANES)
    sub, lane = iota(square, 0), iota(square, 1)
    prefix = jnp.concatenate([(sub < lane).astype(BF16), jnp.ones(square, BF16)], axis=1)
    carry = jnp.zeros(square, F32)
    hits, firsts = [], []
    for k in range(blocks):
        target = tile[k : k + 1]
        hit = sub == target
        hits.append(hit.astype(F32).astype(BF16))
        both = jnp.dot(hits[-1], prefix, preferred_element_type=F32)
        slot = jnp.sum(jnp.where(hit, both[:, :LANES] + carry, 0.0), axis=0, keepdims=True)
        carry = carry + both[:, LANES:]
        slot = slot.astype(jnp.int32)
        place_ref[k : k + 1, :] = target * capacity + slot
        begin = start[k : k + 1]
        block_of = jnp.where(sub == slot, begin // LANES, 0)
        lane_of = jnp.where(sub == slot + 64, begin & (LANES - 1), 0)
        firsts.append((block_of + lane_of).astype(F32).astype(BF16))
    meta_ref[...] = lax.dot_general(
        jnp.concatenate(hits, axis=1),
        jnp.concatenate(firsts, axis=1),
        (((1,), (1,)), ((), ())),
        preferred_element_type=F32,
    )
    col_t = jnp.transpose((start & (LANES - 1)).astype(F32)).astype(jnp.int32)
    return col_t, jnp.transpose(count.astype(F32)).astype(jnp.int32)


def turned_rows(data_ref, k, weight, sla, col, count):
    lane = iota((LANES, LANES), 1)
    weight = jnp.where(lane < count, weight, 0.0)
    value = weight * sla
    index = (lane - col) & (LANES - 1)
    weight = jnp.take_along_axis(weight, index, axis=1)
    value = jnp.take_along_axis(value, index, axis=1)
    data_ref[k * LANES : (k + 1) * LANES, :] = jnp.concatenate([*split(weight), *split(value)], axis=1)


EDGE = 5
WIDE = 2 * EDGE
FIRST_SLOTS = 12


def edge_lanes(rows):
    slot, lane = iota((rows, LANES), 0) % 16, iota((rows, LANES), 1)
    rest = 16 - FIRST_SLOTS
    late = slot - FIRST_SLOTS
    is_first = (lane // WIDE == slot) & (late < 0)
    is_late = ((lane // WIDE) % rest == late) & (lane < 2 * rest * WIDE)
    first = (lane - WIDE * slot) & (LANES - 1)
    second = (first + WIDE) & (LANES - 1)
    third = jnp.where(lane < rest * WIDE, lane - WIDE * late, lane - WIDE * (late + rest - 1)) & (LANES - 1)
    return (first, is_first), (second, is_first), (third, is_late)


def folded(parts):
    sub = iota((8, LANES), 0)
    for step in (4, 2, 1):
        low = (sub & step) == 0
        half = len(parts) // 2
        pairs = []
        for a, b in zip(parts[:half], parts[half:]):
            other = jnp.where(low, b, a)
            moved = jnp.where(low, pltpu.roll(other, 8 - step, 0), pltpu.roll(other, step, 0))
            pairs.append(jnp.where(low, a, b) + moved)
        parts = pairs
    return parts[0]


def place_kernel(capacity, n_cols, data_ref, place_ref, meta_ref, token_ref, out_ref, next_ref, made_ref, sems):
    next_ref[...] = token_ref[...]
    blocks = place_ref.shape[0]
    chunk = 2 * capacity + 4
    place = jnp.concatenate([place_ref[k : k + 1, :] for k in range(blocks)], axis=1)
    height = n_cols * capacity
    slots = iota((height, blocks * LANES), 0)
    lane = iota((capacity, LANES), 1)
    ends = jnp.where(lane < WIDE, lane % EDGE, LANES - EDGE + lane % EDGE)
    in_value = (lane // EDGE) % 2 == 1
    lanes = edge_lanes(capacity)
    western = iota((n_cols, LANES), 1) < WIDE * (16 - FIRST_SLOTS)
    east_of = lambda x: pltpu.roll(x, n_cols - 1, 0)
    west_of = lambda x: pltpu.roll(x, 1, 0)
    copies = []
    for g in range(LANES // n_cols):
        pick = (slots == place - g * height).astype(F32).astype(BF16)
        moved = jnp.dot(pick, data_ref[...], preferred_element_type=F32)
        weight = moved[:, :LANES] + moved[:, LANES : 2 * LANES]
        value = moved[:, 2 * LANES : 3 * LANES] + moved[:, 3 * LANES :]
        first = g * n_cols * chunk
        parts = [[], [], []]
        for t in range(n_cols):
            base = first + t * chunk
            rows = slice(t * capacity, (t + 1) * capacity)
            made_ref[base : base + capacity, :] = weight[rows]
            made_ref[base + capacity : base + 2 * capacity, :] = value[rows]
            both = jnp.where(
                in_value,
                jnp.take_along_axis(value[rows], ends, axis=1),
                jnp.take_along_axis(weight[rows], ends, axis=1),
            )
            for part, (index, mine) in zip(parts, lanes):
                spread = jnp.where(mine, jnp.take_along_axis(both, index, axis=1), 0.0)
                part.append(spread[:8] + spread[8:])
        edges = [
            jnp.concatenate([folded(part[i : i + 8]) for i in range(0, n_cols, 8)], axis=0) for part in parts
        ]
        meta = meta_ref[g * n_cols : (g + 1) * n_cols, :]
        meta = (
            meta + pltpu.roll(east_of(meta), capacity, 1) + pltpu.roll(west_of(meta), 2 * capacity, 1)
        )
        extra = (
            meta,
            east_of(edges[0]),
            west_of(edges[1]),
            jnp.where(western, east_of(edges[2]), west_of(edges[2])),
        )
        for i, rows in enumerate(extra):
            made_ref[pl.ds(first + 2 * capacity + i, n_cols, stride=chunk), :] = rows
        ready = pl.ds(first, n_cols * chunk)
        copies.append(pltpu.make_async_copy(made_ref.at[ready, :], out_ref.at[ready, :], sems.at[g]))
        copies[-1].start()
    for copy in copies:
        copy.wait()


def placed(data, place, meta, token, capacity, n_cols):
    chunk = 2 * capacity + 4
    return pl.pallas_call(
        functools.partial(place_kernel, capacity, n_cols),
        out_shape=(far_shape(LANES * chunk, LANES), shape(*token.shape)),
        in_specs=[VMEM] * 4,
        out_specs=(HBM, VMEM),
        scratch_shapes=[
            pltpu.VMEM((LANES * chunk, LANES), F32),
            pltpu.SemaphoreType.DMA((LANES // n_cols,)),
        ],
        compiler_params=params(12),
        name="place_segments",
    )(data, place, meta, token)


def unpack_kernel(capacity, got_ref, height_ref, face_ref, token_ref, q_ref, next_ref, sum_ref):
    next_ref[...] = token_ref[...]
    chunk = 2 * capacity + 4
    square = (LANES, LANES)
    lane = iota(square, 1)
    meta = got_ref[pl.ds(2 * capacity, LANES, stride=chunk), :]
    meta_t = jnp.transpose(meta)
    rows, cols = q_ref.shape[0], q_ref.shape[1] - LANES
    cells = rows * cols // LANES
    blocks = iota((cells, LANES), 0).astype(F32)
    lane_f = lane.astype(F32)
    acc = jnp.zeros((cells, 4 * LANES), F32)
    for j in range(capacity):
        weight = got_ref[pl.ds(j, LANES, stride=chunk), :]
        value = got_ref[pl.ds(capacity + j, LANES, stride=chunk), :]
        here = lane_f >= meta[:, 64 + j : 65 + j]
        hit = (blocks == meta_t[j : j + 1]).astype(F32).astype(BF16)
        his, los = [], []
        for x in (weight, value):
            hi = x.astype(BF16).astype(F32)
            lo = x - hi
            for keep in (here, ~here):
                his.append(jnp.where(keep, hi, 0.0).astype(BF16))
                los.append(jnp.where(keep, lo, 0.0).astype(BF16))
        data = jnp.concatenate(
            [jnp.concatenate(his, axis=1), jnp.concatenate(los, axis=1)], axis=0
        )
        acc = acc + jnp.dot(
            jnp.concatenate([hit, hit], axis=1), data, preferred_element_type=F32
        )
    for i in range(2):
        here, after = acc[:, 2 * i * LANES : (2 * i + 1) * LANES], acc[:, (2 * i + 1) * LANES : (2 * i + 2) * LANES]
        sum_ref[i, :, :] = here + pltpu.roll(after, 1, 0)
    for half in range(2):
        at = slice(half * LANES, (half + 1) * LANES)
        weight = sum_ref[0, pl.ds(half, rows, stride=2), :]
        value = sum_ref[1, pl.ds(half, rows, stride=2), :]
        mu = height_ref[0, :, at] + (weight * height_ref[1, :, at] - value)
        q_ref[:, at] = face_ref[5, 0:rows, at] * mu

    row_of = iota((rows, LANES), 0).astype(F32)
    group = iota((rows, LANES), 1) // WIDE
    rest = capacity - FIRST_SLOTS
    at = lane % EDGE
    first = capacity + jnp.minimum(lane // WIDE, FIRST_SLOTS - 1)
    late = capacity + FIRST_SLOTS + (lane // WIDE) % rest
    western = lane < rest * WIDE
    edges = []
    for i, (index, is_west) in enumerate(
        ((first, True), (first + capacity, False), (jnp.where(western, late, late + capacity), western))
    ):
        block = jnp.take_along_axis(meta, index, axis=1)
        start = jnp.take_along_axis(meta, index + 64, axis=1).astype(jnp.int32)
        odd = block != 2.0 * jnp.floor(0.5 * block)
        has_west = ~odd & (at >= start)
        has_east = odd | (LANES - EDGE + at < start)
        if is_west is True:
            valid = has_west
        elif is_west is False:
            valid = has_east
        else:
            valid = (is_west & has_west) | (~is_west & has_east)
        edge = got_ref[pl.ds(2 * capacity + 1 + i, LANES, stride=chunk), :]
        edges.append(jnp.concatenate(split(jnp.where(valid, edge, 0.0)), axis=0))

    def edge_sum(base, row, first_group):
        hits = []
        for j in range(capacity):
            hits.append((row_of == jnp.floor(0.5 * meta_t[base + j : base + j + 1])).astype(F32).astype(BF16))

        def spread(picks, edge):
            hit = jnp.concatenate(picks, axis=0)
            return jnp.dot(jnp.concatenate([hit, hit], axis=1), edges[edge], preferred_element_type=F32)

        total = jnp.zeros((rows, LANES), F32)
        full = spread(hits[:FIRST_SLOTS], row)
        for j in range(FIRST_SLOTS):
            total = jnp.where(group == j, full[j * rows : (j + 1) * rows], total)
        tail = spread(hits[FIRST_SLOTS:], 2)
        late = jnp.zeros((rows, LANES), F32)
        for j in range(rest):
            late = jnp.where(group == first_group + j, tail[j * rows : (j + 1) * rows], late)
        if first_group:
            late = pltpu.roll(late, LANES - WIDE * first_group, 1)
        total = total + late
        total = total + pltpu.roll(total, LANES - 6 * WIDE, 1)
        total = total + pltpu.roll(total, LANES - 3 * WIDE, 1)
        total = total + pltpu.roll(total, LANES - WIDE, 1) + pltpu.roll(total, LANES - 2 * WIDE, 1)
        return total, pltpu.roll(total, LANES - EDGE, 1)

    side = slice(cols, cols + LANES)
    eastern = iota((rows, LANES), 1) < LANES // 2
    weight, value = [
        jnp.where(eastern, e, pltpu.roll(w, LANES - EDGE, 1))
        for e, w in zip(edge_sum(capacity, 0, 0), edge_sum(2 * capacity, 1, rest))
    ]
    mu = height_ref[0, :, side] + (weight * height_ref[1, :, side] - value)
    q_ref[:, side] = face_ref[5, 0:rows, side] * mu


def unpack(got, heights, faces, token, capacity):
    rows, wide = heights.shape[1:]
    return pl.pallas_call(
        functools.partial(unpack_kernel, capacity),
        out_shape=(shape(rows, wide), shape(*token.shape)),
        in_specs=[VMEM] * 4,
        out_specs=(VMEM, VMEM),
        scratch_shapes=[pltpu.VMEM((2, rows * (wide - LANES) // LANES, LANES), F32)],
        compiler_params=params(10),
        name="forcing",
    )(got, heights, faces, token)


def two_sum(a, b):
    s = a + b
    t = s - a
    return s, (a - (s - t)) + (b - t)


def pair_sum(x, y):
    s, e = two_sum(x[0], y[0])
    e = e + (x[1] + y[1])
    return s, e


def tree(parts):
    while len(parts) > 1:
        odd = parts[len(parts) // 2 * 2 :]
        parts = [pair_sum(parts[i], parts[i + 1]) for i in range(0, len(parts) - 1, 2)] + odd
    return parts[0]


def rows_sum(hi):
    zero = jnp.zeros((8, LANES), F32)
    total = tree([(hi[8 * i : 8 * i + 8], zero) for i in range(16)])
    for step in (4, 2, 1):
        total = pair_sum(total, (pltpu.roll(total[0], step, 0), pltpu.roll(total[1], step, 0)))
    return total


def krylov(apply, start):
    first = apply(start)
    one = SCALE_0 * (first - SHIFT_0 * start)
    second = apply(one)
    two = SCALE_1 * (second - SHIFT_1 * one)
    return (start, one, two), (first, second, apply(two))


def sums_kernel(q_ref, north_ref, south_ref, face_ref, token_ref, row_ref, field_ref, part_ref):
    rows, cols = q_ref.shape[0], q_ref.shape[1] - LANES
    high, wide = rows + 16, cols + LANES
    q = jnp.concatenate([q_ref[...], north_ref[...], south_ref[...]], axis=0)

    def apply(v):
        return (
            face_ref[0] * v
            - face_ref[1] * pltpu.roll(v, wide - 1, 1)
            - face_ref[2] * pltpu.roll(v, 1, 1)
            - face_ref[3] * pltpu.roll(v, high - 1, 0)
            - face_ref[4] * pltpu.roll(v, 1, 0)
        )

    def inner(at, a, b):
        p = a[:rows, :cols] * b[:rows, :cols]
        p = (p[0:8] + p[8:16]) + (p[16:24] + p[24:32])
        part_ref[8 * at : 8 * at + 8, :] = p[:, :LANES] + p[:, LANES:]

    w, aw = krylov(apply, q)
    y, ay = zip(*[krylov(apply, face_ref[5] * v) for v in w])
    for i in range(3):
        field_ref[i] = w[i]
        field_ref[3 + 2 * i] = y[i][1]
        field_ref[4 + 2 * i] = y[i][2]
    orders = [(k, l) for k in range(3) for l in range(k + 1)]
    at = 0
    for i in range(3):
        for j in range(3):
            for k, l in orders:
                inner(at, y[i][k], ay[j][l])
                at += 1
            for k in range(3):
                inner(at, y[i][k], y[j][0])
                at += 1
    for k, l in orders:
        inner(at, w[k], aw[l])
        at += 1
    for k in range(3):
        inner(at, w[k], q)
        at += 1
    part_ref[8 * at :, :] = jnp.zeros((8 * (LANES - at), LANES), F32)
    zero = jnp.zeros((LANES, LANES), F32)
    pieces = [(part_ref[pl.ds(s, LANES, stride=8), :], zero) for s in range(8)]
    hi, lo = tree(pieces)
    hi, lo = jnp.transpose(hi), jnp.transpose(lo)
    total = rows_sum(hi)
    row = total[0] + (total[1] + rows_sum(lo)[0])
    row_ref[...] = jnp.broadcast_to(row[0:1], row_ref.shape)


def sums(q, north, south, faces, token):
    rows, wide = q.shape
    return pl.pallas_call(
        sums_kernel,
        out_shape=(shape(LANES, LANES), shape(9, rows + 16, wide)),
        in_specs=[VMEM] * 5,
        out_specs=(VMEM,) * 2,
        scratch_shapes=[pltpu.VMEM((8 * LANES, LANES), F32)],
        compiler_params=params(8),
        name="krylov_sums",
    )(q, north, south, faces, token)


def two_prod(a, b):
    p = a * b
    t = 4097.0 * a
    ah = t - (t - a)
    al = a - ah
    t = 4097.0 * b
    bh = t - (t - b)
    bl = b - bh
    return p, ((ah * bh - p) + (ah * bl + al * bh)) + al * bl


def quick(s, e):
    t = s + e
    return t, e - (t - s)


def pair_add(x, y):
    s, e = two_sum(x[0], y[0])
    return quick(s, e + (x[1] + y[1]))


def pair_neg(x):
    return -x[0], -x[1]


def pair_mul(x, y):
    p, e = two_prod(x[0], y[0])
    return quick(p, e + (x[0] * y[1] + x[1] * y[0]))


def pair_div(x, y):
    first = x[0] / y[0]
    p, e = two_prod(first, y[0])
    rest = ((x[0] - p) - e) + (x[1] - first * y[1])
    return quick(first, rest / y[0])


def minor(a, b, c, d):
    return pair_add(pair_mul(a, b), pair_neg(pair_mul(c, d)))


def pair_sum3(a, b, c):
    return pair_add(pair_add(a, b), c)


def small_solve(g, b):
    g00, g10, g11, g20, g21, g22 = g
    c00, c01, c02 = minor(g11, g22, g21, g21), minor(g20, g21, g10, g22), minor(g10, g21, g20, g11)
    c11, c12, c22 = minor(g00, g22, g20, g20), minor(g10, g20, g00, g21), minor(g00, g11, g10, g10)
    det = pair_sum3(pair_mul(g00, c00), pair_mul(g10, c01), pair_mul(g20, c02))
    three = det[0] > 1e-8 * (c22[0] * g22[0])
    two = c22[0] > 1e-8 * (g00[0] * g11[0])
    three = three & two
    rows = ((c00, c01, c02), (c01, c11, c12), (c02, c12, c22))
    full = [pair_div(pair_sum3(*[pair_mul(m, v) for m, v in zip(row, b)]), det)[0] for row in rows]
    half = [
        pair_div(minor(g11, b[0], g10, b[1]), c22)[0],
        pair_div(minor(g00, b[1], g10, b[0]), c22)[0],
        jnp.zeros_like(det[0]),
    ]
    alone = [b[0][0] / g00[0], half[2], half[2]]
    return [jnp.where(three, x, jnp.where(two, y, z)) for x, y, z in zip(full, half, alone)]


def coefficients(every_ref):
    total = quick(*rows_sum(every_ref[...]))

    def pick(x, at):
        return tuple(jnp.broadcast_to(v[:, at : at + 1], (8, LANES)) for v in x)

    def scaled(x, at):
        by = 1.0 / jnp.broadcast_to(x[0][:, at : at + 1], (8, LANES))
        p, e = two_prod(x[0], by)
        return quick(p, e + x[1] * by)

    first = scaled(total, 81)
    first = [pick(first, 81 + m) for m in range(9)]
    c = small_solve(first[:6], first[6:])
    terms = []
    for i in range(3):
        for j in range(3):
            shift = (LANES - 9 * (3 * i + j)) % LANES
            row = tuple(pltpu.roll(v, shift, 1) if shift else v for v in total)
            terms.append(pair_mul(row, two_prod(c[i], c[j])))
    while len(terms) > 1:
        odd = terms[len(terms) // 2 * 2 :]
        terms = [pair_add(terms[i], terms[i + 1]) for i in range(0, len(terms) - 1, 2)] + odd
    second = scaled(terms[0], 0)
    second = [pick(second, m) for m in range(9)]
    return c, small_solve(second[:6], second[6:])


def tracer_kernel(steric_ref, every_ref, field_ref, face_ref, far_ref, side_ref, mu_ref, rho_ref, tall_ref, sems):
    levels, rows, cols = mu_ref.shape

    def copy(level):
        return pltpu.make_async_copy(far_ref.at[level], tall_ref.at[level], sems.at[level])

    for level in range(levels):
        copy(level).start()
    high, wide = rows + 8, cols + LANES

    def trim(v):
        edge = jnp.where(iota((8, wide), 0) < 4, v[rows : rows + 8], v[rows + 8 :])
        return jnp.concatenate([v[:rows], edge], axis=0)

    c, e = coefficients(every_ref)
    c, e = [[jnp.broadcast_to(v[0:1, 0:1], (1, 1)) for v in part] for part in (c, e)]
    w = [trim(field_ref[i]) for i in range(3)]
    ocean = trim(face_ref[5])
    rho_1 = c[0] * w[0] + c[1] * w[1] + c[2] * w[2]
    rho_0 = e[0] * (ocean * rho_1)
    for k in (1, 2):
        v = [trim(field_ref[2 + k + 2 * i]) for i in range(3)]
        rho_0 = rho_0 + e[k] * (c[0] * v[0] + c[1] * v[1] + c[2] * v[2])
    rho_ref[...] = rho_0[:rows, :cols]

    def one_level(level):
        height = steric_ref[level]
        full = lambda at: jnp.concatenate([tall_ref[level, at], side_ref[at, level]], axis=1)
        g = ocean * (full(0) + height * rho_1)
        dx = g - pltpu.roll(g, wide - 1, 1)
        dy = g - pltpu.roll(g, high - 1, 0)
        mu = g - (
            full(1) * dx + pltpu.roll(full(2) * dx, 1, 1) + full(3) * dy + pltpu.roll(full(4) * dy, 1, 0)
        )
        g = ocean * (mu + height * rho_0)
        dx = (g - pltpu.roll(g, wide - 1, 1))[:rows]
        dy = (g - pltpu.roll(g, high - 1, 0))[:, :cols]
        back_x = pltpu.roll(full(5)[:rows] * dx, 1, 1)[:, :cols]
        back_y = pltpu.roll(tall_ref[level, 6] * dy, 1, 0)[:rows]
        mu_ref[level] = g[:rows, :cols] - (
            tall_ref[level, 7, 0:rows, :] * dx[:, :cols] + back_x + tall_ref[level, 8, 0:rows, :] * dy[:rows] + back_y
        )

    def some_levels(group, carry):
        for i in range(GROUP):
            copy(group * GROUP + i).wait()
        for i in range(GROUP):
            one_level(group * GROUP + i)
        return carry

    lax.fori_loop(0, levels // GROUP, some_levels, 0)


def tracers(steric, every, fields, faces, tall, side):
    levels, count, high, cols = tall.shape
    rows = high - 8
    return pl.pallas_call(
        tracer_kernel,
        out_shape=(shape(levels, rows, cols), shape(rows, cols)),
        in_specs=[SCALAR] + [VMEM] * 3 + [HBM, VMEM],
        out_specs=(VMEM, VMEM),
        scratch_shapes=[pltpu.VMEM((levels, count, high, cols), F32), pltpu.SemaphoreType.DMA((levels,))],
        compiler_params=params(20),
        name="tracer_steps",
    )(steric, every, fields, faces, *far((tall,)), side)


def beside(cells, axis, step):
    count = lax.axis_size(axis)
    return lax.ppermute(cells, axis, [((i + step) % count, i) for i in range(count)])


def tracer_fields(keep, lam, zonal_1, merid_1, zonal_0, merid_0, mix_x, mix_y):
    flow_x, flow_y = 0.5 * zonal_1, 0.5 * merid_1
    past_x, past_y = 0.5 * zonal_0, 0.5 * merid_0
    return (
        lam,
        flow_x + mix_x,
        flow_x - mix_x,
        keep * (flow_y + mix_y),
        keep * (flow_y - mix_y),
        past_x - mix_x,
        keep * (past_y - mix_y),
        past_x + mix_x,
        keep * (past_y + mix_y),
    )


def surface_fields(keep, diag_ref, east_ref, north_ref, land_ref, rows):
    return diag_ref[rows], east_ref[rows], keep * north_ref[rows], land_ref[rows].astype(F32)


UP = (0, 1, 2, 3)
DOWN = (0, 1, 2, 3, 4, 6)
SIDE = (0, 1, 2, 3, 4, 5)


def kept(token_ref, first, count, rows, cols):
    last = jnp.concatenate([token_ref[0:1, :]] * (cols // LANES), axis=1)
    return jnp.where((iota((count, cols), 0) + first == rows - 1) & (last == 1.0), 0.0, 1.0)


def opening_kernel(capacity, token_ref, lam_ref, zonal_ref, merid_ref, mix_x_ref, mix_y_ref, *refs):
    surface_refs, (sla_ref, weight_ref), marks = refs[:4], refs[4:6], refs[6:9]
    up_ref, down_ref, next_ref, data_ref, place_ref, meta_ref = refs[9:15]
    held_ref, flat_ref, land_ref, segment_ref, mark_ref, sems, flat_sems, segment_sems, mark_sems = refs[15:]
    levels, rows, cols = lam_ref.shape
    blocks = mark_ref.shape[1]

    def started(source, target, sem):
        copy = pltpu.make_async_copy(source, target, sem)
        copy.start()
        return copy

    mark_copies = [started(ref, mark_ref.at[i], mark_sems.at[i]) for i, ref in enumerate(marks)]
    segment_copies = []
    for k in range(2):
        block = pl.ds(k * blocks * LANES // 2, blocks * LANES // 2)
        for i, ref in enumerate((sla_ref, weight_ref)):
            segment_copies.append(started(ref.at[block, :], segment_ref.at[i, block, :], segment_sems.at[2 * k + i]))
    copies, flat_copies = [], []
    for part, (first, outer) in enumerate(((0, 0), (rows - 8, rows - 2))):
        block = pl.ds(outer, 2)
        for source in (
            lam_ref.at[:, block, :],
            zonal_ref.at[1, :, block, :],
            merid_ref.at[1, :, block, :],
            mix_x_ref.at[:, block, :],
            mix_y_ref.at[:, block, :],
            merid_ref.at[0, :, block, :],
        )[: 5 + part]:
            copies.append(started(source, held_ref.at[len(copies)], sems.at[len(copies)]))
        block = pl.ds(first, 8)
        for i, ref in enumerate(surface_refs[:3]):
            flat_copies.append(started(ref.at[block, :], flat_ref.at[part, i], flat_sems.at[len(flat_copies)]))
        ref = surface_refs[3]
        flat_copies.append(started(ref.at[block, :], land_ref.at[part], flat_sems.at[len(flat_copies)]))
    next_ref[...] = token_ref[...]

    for copy in mark_copies:
        copy.wait()
    col_t, count_t = ranks(capacity, mark_ref[0], mark_ref[1], mark_ref[2], place_ref, meta_ref)
    for copy in copies + flat_copies:
        copy.wait()
    for part, (out_ref, picks, first, take) in enumerate(((up_ref, UP, 0, 0), (down_ref, DOWN, rows - 8, 6))):
        keep = kept(token_ref, first, 8, rows, cols)
        base = 2 * len(picks) * levels
        diag, east, north = [flat_ref[part, i] for i in range(3)]
        ocean = land_ref[part].astype(F32)
        for at, field in enumerate((diag, east, keep * north, ocean)):
            out_ref[base + 8 * at : base + 8 * at + 8, :] = field
        for level in range(levels):
            lam, zonal_1, merid_1, mix_x, mix_y, merid_0 = [held_ref[5 * part + min(i, 4 + part), level] for i in range(6)]
            fields = tracer_fields(keep[take : take + 2], lam, zonal_1, merid_1, zonal_1, merid_0, mix_x, mix_y)
            for at, pick in enumerate(picks):
                base = 2 * (at * levels + level)
                out_ref[base : base + 2, :] = fields[pick]
    for copy in segment_copies:
        copy.wait()
    for k in range(blocks):
        here = slice(k * LANES, (k + 1) * LANES)
        turned_rows(
            data_ref, k, segment_ref[1, here, :], segment_ref[0, here, :], col_t[:, k : k + 1], count_t[:, k : k + 1]
        )


def edge_rows(n_ref, s_ref, pick, levels, level, cols):
    zero = lambda count: jnp.zeros((count, cols), F32)
    north = zero(2)
    if pick in UP:
        base = 2 * (UP.index(pick) * levels + level)
        north = n_ref[base : base + 2, :]
    south = zero(2)
    if pick in DOWN:
        base = 2 * (DOWN.index(pick) * levels + level)
        south = s_ref[base : base + 2, :]
    return jnp.concatenate([north, zero(4), south], axis=0)


def halves(tall):
    lane = iota((tall.shape[0], LANES), 1)
    return jnp.where(lane < LANES // 2, tall[:, :LANES], tall[:, -LANES:])


def gathered(talls, width):
    lane = iota((talls[0].shape[0], LANES), 1)
    mixed = jnp.zeros((talls[0].shape[0], LANES), F32)
    for at, tall in enumerate(talls):
        mixed = jnp.where(lane // (2 * width) == at, pltpu.roll(halves(tall), width + 2 * width * at, 1), mixed)
    return mixed


def scattered(mixed, at, width):
    return pltpu.roll(mixed, LANES - width - 2 * width * at, 1)


TRACER_WIDTH = 2
FACE_WIDTH = 8


GROUP = 4


def cols_kernel(token_ref, lam_ref, zonal_ref, merid_ref, mix_x_ref, mix_y_ref, *refs):
    surface_refs, height_refs, (n_ref, s_ref) = refs[:4], refs[4:6], refs[6:8]
    out_ref, far_ref, face_ref, height_ref, held_ref, flat_ref, tall_ref, sems, far_sems = refs[8:]
    levels, rows, cols = lam_ref.shape
    copies = []
    for group in range(levels // GROUP):
        block = pl.ds(group * GROUP, GROUP)
        for i, source in enumerate(
            (
                lam_ref.at[block],
                zonal_ref.at[1, block],
                merid_ref.at[1, block],
                zonal_ref.at[0, block],
                merid_ref.at[0, block],
                mix_x_ref.at[block],
                mix_y_ref.at[block],
            )
        ):
            copies.append(pltpu.make_async_copy(source, held_ref.at[i, block], sems.at[len(copies)]))
            copies[-1].start()
    keep = kept(token_ref, 0, rows, rows, cols)
    high = rows + 8
    used = 2 * TRACER_WIDTH * len(SIDE)
    blocks = levels * high // LANES
    base = blocks * used
    up, down = 2 * len(UP) * levels, 2 * len(DOWN) * levels
    talls = []
    for at, field in enumerate(surface_fields(keep, *surface_refs, slice(0, rows))):
        tall = jnp.concatenate(
            [field, n_ref[up + 8 * at : up + 8 * at + 8, :], s_ref[down + 8 * at : down + 8 * at + 8, :]], axis=0
        )
        face_ref[at] = tall
        talls.append(tall)
    for at, ref in enumerate(height_refs):
        height_ref[at] = ref[...]
        talls.append(jnp.concatenate([ref[...], jnp.zeros((16, cols), F32)], axis=0))
    out_ref[base : base + rows + 16, :] = gathered(talls, FACE_WIDTH)
    far = []
    for level in range(levels):
        if level % GROUP == 0:
            for copy in copies[7 * (level // GROUP) : 7 * (level // GROUP) + 7]:
                copy.wait()
        fields = tracer_fields(keep, *[held_ref[i, level] for i in range(7)])
        talls = []
        for pick, field in enumerate(fields):
            tall_ref[level, pick, 0:rows, :] = field
            edge = edge_rows(n_ref, s_ref, pick, levels, level, cols)
            tall_ref[level, pick, rows:high, :] = edge
            if pick in SIDE:
                talls.append(jnp.concatenate([field, edge], axis=0))
        flat_ref[level * high : (level + 1) * high, :] = gathered(talls, TRACER_WIDTH)
        far.append(pltpu.make_async_copy(tall_ref.at[level], far_ref.at[level], far_sems.at[level]))
        far[-1].start()
    for b in range(blocks):
        turned = jnp.transpose(flat_ref[b * LANES : (b + 1) * LANES, :])
        out_ref[b * used : (b + 1) * used, :] = turned[:used]
    for copy in far:
        copy.wait()


def side_kernel(strip_ref, token_ref, side_ref, next_ref, flat_ref):
    next_ref[...] = token_ref[...]
    levels, high = side_ref.shape[1:3]
    used = 2 * TRACER_WIDTH * len(SIDE)
    blocks = levels * high // LANES
    for b in range(blocks):
        both = strip_ref[b * used : (b + 1) * used, :]
        both = jnp.concatenate([both, jnp.zeros((LANES - used, LANES), F32)], axis=0)
        flat_ref[b * LANES : (b + 1) * LANES, :] = jnp.transpose(both)
    for level in range(levels):
        mixed = flat_ref[level * high : (level + 1) * high, :]
        for at in range(len(SIDE)):
            side_ref[at, level] = scattered(mixed, at, TRACER_WIDTH)


def face_halo_kernel(base, token_ref, tall_ref, height_ref, e_ref, w_ref, face_ref, full_ref, strip_ref):
    from_west = iota((base, LANES), 0) % (2 * TRACER_WIDTH) < TRACER_WIDTH
    strip_ref[...] = jnp.where(from_west, w_ref[0:base, :], e_ref[0:base, :])
    high = tall_ref.shape[1]
    rows = height_ref.shape[1]
    for at in range(2):
        full_ref[at, :, : -LANES] = height_ref[at]
    western = iota((high, LANES), 1) % (2 * FACE_WIDTH) < FACE_WIDTH
    here = slice(base, base + high)
    mixed = jnp.where(western, w_ref[here, :], e_ref[here, :])
    for at in range(2):
        full_ref[at, :, -LANES:] = scattered(mixed, 4 + at, FACE_WIDTH)[:rows]
    full = [jnp.concatenate([tall_ref[at], scattered(mixed, at, FACE_WIDTH)], axis=1) for at in range(4)]
    diag, east, north, ocean = full
    west, south = pltpu.roll(east, 1, 1), pltpu.roll(north, 1, 0)
    face_ref[0] = (1.0 + diag) + east + west + north + south
    for at, field in enumerate((east, west, north, south, ocean)):
        face_ref[1 + at] = field


def opening(token, tracer, surface, segments, marks, capacity):
    levels, rows, cols = tracer[0].shape
    up, down = 2 * len(UP) * levels + 32, 2 * len(DOWN) * levels + 32
    blocks = segments[0].shape[0] // LANES
    marks = tuple(mark.reshape(blocks, LANES) for mark in marks)
    return pl.pallas_call(
        functools.partial(opening_kernel, capacity),
        out_shape=(
            shape(up, cols),
            shape(down, cols),
            shape(*token.shape),
            jax.ShapeDtypeStruct((blocks * LANES, 4 * LANES), BF16),
            jax.ShapeDtypeStruct((blocks, LANES), jnp.int32),
            shape(LANES, LANES),
        ),
        in_specs=[VMEM] + [HBM] * 14,
        out_specs=(VMEM,) * 6,
        scratch_shapes=[
            pltpu.VMEM((11, levels, 2, cols), F32),
            pltpu.VMEM((2, 3, 8, cols), F32),
            pltpu.VMEM((2, 8, cols), jnp.int32),
            pltpu.VMEM((2, blocks * LANES, LANES), F32),
            pltpu.VMEM((3, blocks, LANES), jnp.int32),
            pltpu.SemaphoreType.DMA((11,)),
            pltpu.SemaphoreType.DMA((8,)),
            pltpu.SemaphoreType.DMA((4,)),
            pltpu.SemaphoreType.DMA((3,)),
        ],
        compiler_params=params(12),
        name="opening",
    )(token, *far(tracer), *far(surface), *far(segments), *far(marks))


def edges_to_tx(token, tracer, surface, heights, north, south):
    levels, rows, cols = tracer[0].shape
    high = rows + 8
    side_rows = 2 * TRACER_WIDTH * len(SIDE) * levels * high // LANES + rows + 16
    sides, tall, faces, heights = pl.pallas_call(
        cols_kernel,
        out_shape=(
            shape(side_rows, LANES),
            far_shape(levels, 9, high, cols),
            shape(4, rows + 16, cols),
            shape(2, rows, cols),
        ),
        in_specs=[VMEM] + [HBM] * 5 + [VMEM] * 8,
        out_specs=(VMEM, HBM, VMEM, VMEM),
        scratch_shapes=[
            pltpu.VMEM((7, levels, rows, cols), F32),
            pltpu.VMEM((levels * high, LANES), F32),
            pltpu.VMEM((levels, 9, high, cols), F32),
            pltpu.SemaphoreType.DMA((7 * levels // GROUP,)),
            pltpu.SemaphoreType.DMA((levels,)),
        ],
        compiler_params=params(24),
        name="edge_columns",
    )(token, *far(tracer), *far(surface), *far(heights), north, south)
    return (beside(sides, "tx", 1), beside(sides, "tx", -1)), tall, faces, heights


def faces_with_halo(token, tall, heights, east, west):
    count, high, cols = tall.shape
    base = east.shape[0] - high
    return pl.pallas_call(
        functools.partial(face_halo_kernel, base),
        out_shape=(shape(6, high, cols + LANES), shape(2, heights.shape[1], cols + LANES), shape(base, LANES)),
        in_specs=[VMEM] * 5,
        out_specs=(VMEM,) * 3,
        compiler_params=params(6),
        name="surface_halos",
    )(token, tall, heights, east, west)


def tracer_sides(token, strips, levels, rows):
    high = rows + 8
    return pl.pallas_call(
        side_kernel,
        out_shape=(shape(len(SIDE), levels, high, LANES), shape(*token.shape)),
        in_specs=[VMEM] * 2,
        out_specs=(VMEM, VMEM),
        scratch_shapes=[pltpu.VMEM((levels * high, LANES), F32)],
        compiler_params=params(8),
        name="tracer_halos",
    )(strips, token)


def on_device(
    lam_tracer,
    lam_eta,
    land,
    zonal_flow,
    merid_flow,
    zonal_mixing,
    merid_mixing,
    surface_east,
    surface_north,
    surface_diag,
    steric,
    eta_saved,
    obs_sla,
    obs_weight,
    obs_tile,
    obs_start,
    obs_count,
):
    levels, rows, cols = lam_tracer.shape
    n_rows = lax.axis_size("ty")
    devices = n_rows * lax.axis_size("tx")
    capacity = 2 * obs_sla.shape[0] // devices
    token = jnp.full((8, LANES), lax.axis_index("ty") == n_rows - 1, F32)
    tracer = (lam_tracer, zonal_flow, merid_flow, zonal_mixing, merid_mixing)
    surface = (surface_diag, surface_east, surface_north, land)
    to_south, to_north, token, *ranked = opening(
        token, tracer, surface, (obs_sla, obs_weight), (obs_tile, obs_start, obs_count), capacity
    )
    around_ty = beside(to_south, "ty", 1), beside(to_north, "ty", -1)
    sent, token = placed(*ranked, token, capacity, devices // n_rows)
    sent, *around_ty = lax.optimization_barrier((sent, *around_ty))
    got = lax.all_to_all(
        sent.reshape(devices, 1, -1), AXES, split_axis=0, concat_axis=0, tiled=True
    ).reshape(sent.shape)
    around_tx, tall, faces, heights = edges_to_tx(token, tracer, surface, (lam_eta, eta_saved), *around_ty)
    faces, heights, strips = faces_with_halo(token, faces, heights, *around_tx)
    rhs, token = unpack(got, heights, faces, token, capacity)
    north, south = beside(rhs[:8], "ty", 1), beside(rhs[-8:], "ty", -1)
    sides, token = tracer_sides(token, strips, levels, rows)
    mine, krylov_fields = sums(rhs, north, south, faces, token)
    every = lax.all_to_all(
        mine.reshape(devices, 1, LANES), AXES, split_axis=0, concat_axis=0, tiled=True
    ).reshape(devices, LANES)
    return tracers(steric, every, krylov_fields, faces, tall, sides)


def solution(mesh):
    in_specs = (
        P(None, "ty", "tx"),
        P("ty", "tx"),
        P("ty", "tx"),
        P(None, None, "ty", "tx"),
        P(None, None, "ty", "tx"),
        P(None, "ty", "tx"),
        P(None, "ty", "tx"),
        P("ty", "tx"),
        P("ty", "tx"),
        P("ty", "tx"),
        P(),
        P("ty", "tx"),
        P(AXES, None),
        P(AXES, None),
        P(AXES, None),
        P(AXES),
        P(AXES),
    )
    out_specs = (P(None, "ty", "tx"), P("ty", "tx"))
    return jax.shard_map(
        on_device, mesh=mesh, in_specs=in_specs, out_specs=out_specs, check_vma=False
    )
```

```python
import functools

import jax
import jax.numpy as jnp
from jax import lax
from jax.experimental import pallas as pl
from jax.experimental.pallas import tpu as pltpu
from jax.sharding import PartitionSpec as P

AXES = ("ty", "tx")
SHIFT_0 = 1.6
SHIFT_1 = 35.0
SCALE_0 = 1.0 / 32.0
SCALE_1 = 1.0 / 16.0
LANES = 128
VMEM = pl.BlockSpec(memory_space=pltpu.VMEM)
SCALAR = pl.BlockSpec(memory_space=pltpu.SMEM)
HBM = pl.BlockSpec(memory_space=pltpu.HBM)
F32 = jnp.float32
BF16 = jnp.bfloat16


def params(mib):
    return pltpu.CompilerParams(vmem_limit_bytes=mib * 1024 * 1024)


def iota(dims, axis):
    return lax.broadcasted_iota(jnp.int32, dims, axis)


def shape(*dims):
    return jax.ShapeDtypeStruct(dims, F32)


def far_shape(*dims):
    return pltpu.HBM(dims, F32)


def far(arrays):
    return tuple(pltpu.with_memory_space_constraint(x, pltpu.HBM) for x in arrays)


def split(x):
    hi = x.astype(BF16)
    return hi, (x - hi.astype(F32)).astype(BF16)


def ranks(capacity, tile, start, count, place_ref, meta_ref):
    blocks = tile.shape[0]
    square = (LANES, LANES)
    sub, lane = iota(square, 0), iota(square, 1)
    prefix = jnp.concatenate([(sub < lane).astype(BF16), jnp.ones(square, BF16)], axis=1)
    carry = jnp.zeros(square, F32)
    hits, firsts = [], []
    for k in range(blocks):
        target = tile[k : k + 1]
        hit = sub == target
        hits.append(hit.astype(F32).astype(BF16))
        both = jnp.dot(hits[-1], prefix, preferred_element_type=F32)
        slot = jnp.sum(jnp.where(hit, both[:, :LANES] + carry, 0.0), axis=0, keepdims=True)
        carry = carry + both[:, LANES:]
        slot = slot.astype(jnp.int32)
        place_ref[k : k + 1, :] = target * capacity + slot
        begin = start[k : k + 1]
        block_of = jnp.where(sub == slot, begin // LANES, 0)
        lane_of = jnp.where(sub == slot + 64, begin & (LANES - 1), 0)
        firsts.append((block_of + lane_of).astype(F32).astype(BF16))
    meta_ref[...] = lax.dot_general(
        jnp.concatenate(hits, axis=1),
        jnp.concatenate(firsts, axis=1),
        (((1,), (1,)), ((), ())),
        preferred_element_type=F32,
    )
    col_t = jnp.transpose((start & (LANES - 1)).astype(F32)).astype(jnp.int32)
    return col_t, jnp.transpose(count.astype(F32)).astype(jnp.int32)


def turned_rows(data_ref, k, weight, sla, col, count):
    lane = iota((LANES, LANES), 1)
    weight = jnp.where(lane < count, weight, 0.0)
    value = weight * sla
    index = (lane - col) & (LANES - 1)
    weight = jnp.take_along_axis(weight, index, axis=1)
    value = jnp.take_along_axis(value, index, axis=1)
    data_ref[k * LANES : (k + 1) * LANES, :] = jnp.concatenate([*split(weight), *split(value)], axis=1)


EDGE = 5
WIDE = 2 * EDGE
FIRST_SLOTS = 12


def edge_lanes(rows):
    slot, lane = iota((rows, LANES), 0) % 16, iota((rows, LANES), 1)
    rest = 16 - FIRST_SLOTS
    late = slot - FIRST_SLOTS
    is_first = (lane // WIDE == slot) & (late < 0)
    is_late = ((lane // WIDE) % rest == late) & (lane < 2 * rest * WIDE)
    first = (lane - WIDE * slot) & (LANES - 1)
    second = (first + WIDE) & (LANES - 1)
    third = jnp.where(lane < rest * WIDE, lane - WIDE * late, lane - WIDE * (late + rest - 1)) & (LANES - 1)
    return (first, is_first), (second, is_first), (third, is_late)


def folded(parts):
    sub = iota((8, LANES), 0)
    for step in (4, 2, 1):
        low = (sub & step) == 0
        half = len(parts) // 2
        pairs = []
        for a, b in zip(parts[:half], parts[half:]):
            other = jnp.where(low, b, a)
            moved = jnp.where(low, pltpu.roll(other, 8 - step, 0), pltpu.roll(other, step, 0))
            pairs.append(jnp.where(low, a, b) + moved)
        parts = pairs
    return parts[0]


def place_kernel(capacity, n_cols, data_ref, place_ref, meta_ref, token_ref, out_ref, next_ref, made_ref, sems):
    next_ref[...] = token_ref[...]
    blocks = place_ref.shape[0]
    chunk = 2 * capacity + 4
    place = jnp.concatenate([place_ref[k : k + 1, :] for k in range(blocks)], axis=1)
    height = n_cols * capacity
    slots = iota((height, blocks * LANES), 0)
    lane = iota((capacity, LANES), 1)
    ends = jnp.where(lane < WIDE, lane % EDGE, LANES - EDGE + lane % EDGE)
    in_value = (lane // EDGE) % 2 == 1
    lanes = edge_lanes(capacity)
    western = iota((n_cols, LANES), 1) < WIDE * (16 - FIRST_SLOTS)
    east_of = lambda x: pltpu.roll(x, n_cols - 1, 0)
    west_of = lambda x: pltpu.roll(x, 1, 0)
    copies = []
    for g in range(LANES // n_cols):
        pick = (slots == place - g * height).astype(F32).astype(BF16)
        moved = jnp.dot(pick, data_ref[...], preferred_element_type=F32)
        weight = moved[:, :LANES] + moved[:, LANES : 2 * LANES]
        value = moved[:, 2 * LANES : 3 * LANES] + moved[:, 3 * LANES :]
        first = g * n_cols * chunk
        parts = [[], [], []]
        for t in range(n_cols):
            base = first + t * chunk
            rows = slice(t * capacity, (t + 1) * capacity)
            made_ref[base : base + capacity, :] = weight[rows]
            made_ref[base + capacity : base + 2 * capacity, :] = value[rows]
            both = jnp.where(
                in_value,
                jnp.take_along_axis(value[rows], ends, axis=1),
                jnp.take_along_axis(weight[rows], ends, axis=1),
            )
            for part, (index, mine) in zip(parts[:2], lanes):
                spread = jnp.where(mine, jnp.take_along_axis(both, index, axis=1), 0.0)
                part.append(spread[:8] + spread[8:])
            index, mine = lanes[2]
            parts[2].append(jnp.where(mine[8:], jnp.take_along_axis(both[8:], index[8:], axis=1), 0.0))
        edges = [
            jnp.concatenate([folded(part[i : i + 8]) for i in range(0, n_cols, 8)], axis=0) for part in parts
        ]
        meta = meta_ref[g * n_cols : (g + 1) * n_cols, :]
        meta = (
            meta + pltpu.roll(east_of(meta), capacity, 1) + pltpu.roll(west_of(meta), 2 * capacity, 1)
        )
        extra = (
            meta,
            east_of(edges[0]),
            west_of(edges[1]),
            jnp.where(western, east_of(edges[2]), west_of(edges[2])),
        )
        for i, rows in enumerate(extra):
            made_ref[pl.ds(first + 2 * capacity + i, n_cols, stride=chunk), :] = rows
        ready = pl.ds(first, n_cols * chunk)
        copies.append(pltpu.make_async_copy(made_ref.at[ready, :], out_ref.at[ready, :], sems.at[g]))
        copies[-1].start()
    for copy in copies:
        copy.wait()


def placed(data, place, meta, token, capacity, n_cols):
    chunk = 2 * capacity + 4
    return pl.pallas_call(
        functools.partial(place_kernel, capacity, n_cols),
        out_shape=(far_shape(LANES * chunk, LANES), shape(*token.shape)),
        in_specs=[VMEM] * 4,
        out_specs=(HBM, VMEM),
        scratch_shapes=[
            pltpu.VMEM((LANES * chunk, LANES), F32),
            pltpu.SemaphoreType.DMA((LANES // n_cols,)),
        ],
        compiler_params=params(12),
        name="place_segments",
    )(data, place, meta, token)


def unpack_kernel(capacity, got_ref, height_ref, face_ref, token_ref, q_ref, next_ref, sum_ref):
    next_ref[...] = token_ref[...]
    chunk = 2 * capacity + 4
    square = (LANES, LANES)
    lane = iota(square, 1)
    meta = got_ref[pl.ds(2 * capacity, LANES, stride=chunk), :]
    meta_t = jnp.transpose(meta)
    rows, cols = q_ref.shape[0], q_ref.shape[1] - LANES
    cells = rows * cols // LANES
    blocks = iota((cells, LANES), 0).astype(F32)
    lane_f = lane.astype(F32)
    acc = jnp.zeros((cells, 4 * LANES), F32)
    for j in range(capacity):
        weight = got_ref[pl.ds(j, LANES, stride=chunk), :]
        value = got_ref[pl.ds(capacity + j, LANES, stride=chunk), :]
        here = lane_f >= meta[:, 64 + j : 65 + j]
        hit = (blocks == meta_t[j : j + 1]).astype(F32).astype(BF16)
        his, los = [], []
        for x in (weight, value):
            hi = x.astype(BF16).astype(F32)
            lo = x - hi
            for keep in (here, ~here):
                his.append(jnp.where(keep, hi, 0.0).astype(BF16))
                los.append(jnp.where(keep, lo, 0.0).astype(BF16))
        data = jnp.concatenate(
            [jnp.concatenate(his, axis=1), jnp.concatenate(los, axis=1)], axis=0
        )
        acc = acc + jnp.dot(
            jnp.concatenate([hit, hit], axis=1), data, preferred_element_type=F32
        )
    for i in range(2):
        here, after = acc[:, 2 * i * LANES : (2 * i + 1) * LANES], acc[:, (2 * i + 1) * LANES : (2 * i + 2) * LANES]
        sum_ref[i, :, :] = here + pltpu.roll(after, 1, 0)
    for half in range(2):
        at = slice(half * LANES, (half + 1) * LANES)
        weight = sum_ref[0, pl.ds(half, rows, stride=2), :]
        value = sum_ref[1, pl.ds(half, rows, stride=2), :]
        mu = height_ref[0, :, at] + (weight * height_ref[1, :, at] - value)
        q_ref[:, at] = face_ref[5, 0:rows, at] * mu

    row_of = iota((rows, LANES), 0).astype(F32)
    group = iota((rows, LANES), 1) // WIDE
    rest = capacity - FIRST_SLOTS
    at = lane % EDGE
    first = capacity + jnp.minimum(lane // WIDE, FIRST_SLOTS - 1)
    late = capacity + FIRST_SLOTS + (lane // WIDE) % rest
    western = lane < rest * WIDE
    edges = []
    for i, (index, is_west) in enumerate(
        ((first, True), (first + capacity, False), (jnp.where(western, late, late + capacity), western))
    ):
        block = jnp.take_along_axis(meta, index, axis=1)
        start = jnp.take_along_axis(meta, index + 64, axis=1).astype(jnp.int32)
        odd = block != 2.0 * jnp.floor(0.5 * block)
        has_west = ~odd & (at >= start)
        has_east = odd | (LANES - EDGE + at < start)
        if is_west is True:
            valid = has_west
        elif is_west is False:
            valid = has_east
        else:
            valid = (is_west & has_west) | (~is_west & has_east)
        edge = got_ref[pl.ds(2 * capacity + 1 + i, LANES, stride=chunk), :]
        edges.append(jnp.concatenate(split(jnp.where(valid, edge, 0.0)), axis=0))

    def edge_sum(base, row, first_group):
        hits = []
        for j in range(capacity):
            hits.append((row_of == jnp.floor(0.5 * meta_t[base + j : base + j + 1])).astype(F32).astype(BF16))

        def spread(picks, edge):
            hit = jnp.concatenate(picks, axis=0)
            return jnp.dot(jnp.concatenate([hit, hit], axis=1), edges[edge], preferred_element_type=F32)

        total = jnp.zeros((rows, LANES), F32)
        full = spread(hits[:FIRST_SLOTS], row)
        for j in range(FIRST_SLOTS):
            total = jnp.where(group == j, full[j * rows : (j + 1) * rows], total)
        tail = spread(hits[FIRST_SLOTS:], 2)
        late = jnp.zeros((rows, LANES), F32)
        for j in range(rest):
            late = jnp.where(group == first_group + j, tail[j * rows : (j + 1) * rows], late)
        if first_group:
            late = pltpu.roll(late, LANES - WIDE * first_group, 1)
        total = total + late
        total = total + pltpu.roll(total, LANES - 6 * WIDE, 1)
        total = total + pltpu.roll(total, LANES - 3 * WIDE, 1)
        total = total + pltpu.roll(total, LANES - WIDE, 1) + pltpu.roll(total, LANES - 2 * WIDE, 1)
        return total, pltpu.roll(total, LANES - EDGE, 1)

    side = slice(cols, cols + LANES)
    eastern = iota((rows, LANES), 1) < LANES // 2
    weight, value = [
        jnp.where(eastern, e, pltpu.roll(w, LANES - EDGE, 1))
        for e, w in zip(edge_sum(capacity, 0, 0), edge_sum(2 * capacity, 1, rest))
    ]
    mu = height_ref[0, :, side] + (weight * height_ref[1, :, side] - value)
    q_ref[:, side] = face_ref[5, 0:rows, side] * mu


def unpack(got, heights, faces, token, capacity):
    rows, wide = heights.shape[1:]
    return pl.pallas_call(
        functools.partial(unpack_kernel, capacity),
        out_shape=(shape(rows, wide), shape(*token.shape)),
        in_specs=[VMEM] * 4,
        out_specs=(VMEM, VMEM),
        scratch_shapes=[pltpu.VMEM((2, rows * (wide - LANES) // LANES, LANES), F32)],
        compiler_params=params(10),
        name="forcing",
    )(got, heights, faces, token)


def two_sum(a, b):
    s = a + b
    t = s - a
    return s, (a - (s - t)) + (b - t)


def pair_sum(x, y):
    s, e = two_sum(x[0], y[0])
    e = e + (x[1] + y[1])
    return s, e


def tree(parts):
    while len(parts) > 1:
        odd = parts[len(parts) // 2 * 2 :]
        parts = [pair_sum(parts[i], parts[i + 1]) for i in range(0, len(parts) - 1, 2)] + odd
    return parts[0]


def rows_sum(hi):
    zero = jnp.zeros((8, LANES), F32)
    total = tree([(hi[8 * i : 8 * i + 8], zero) for i in range(16)])
    for step in (4, 2, 1):
        total = pair_sum(total, (pltpu.roll(total[0], step, 0), pltpu.roll(total[1], step, 0)))
    return total


def krylov(apply, start):
    first = apply(start)
    one = SCALE_0 * (first - SHIFT_0 * start)
    second = apply(one)
    two = SCALE_1 * (second - SHIFT_1 * one)
    return (start, one, two), (first, second, apply(two))


def sums_kernel(q_ref, north_ref, south_ref, face_ref, token_ref, row_ref, field_ref, part_ref):
    rows, cols = q_ref.shape[0], q_ref.shape[1] - LANES
    high, wide = rows + 16, cols + LANES
    q = jnp.concatenate([q_ref[...], north_ref[...], south_ref[...]], axis=0)

    def apply(v):
        return (
            face_ref[0] * v
            - face_ref[1] * pltpu.roll(v, wide - 1, 1)
            - face_ref[2] * pltpu.roll(v, 1, 1)
            - face_ref[3] * pltpu.roll(v, high - 1, 0)
            - face_ref[4] * pltpu.roll(v, 1, 0)
        )

    def inner(at, a, b):
        p = a[:rows, :cols] * b[:rows, :cols]
        p = (p[0:8] + p[8:16]) + (p[16:24] + p[24:32])
        part_ref[8 * at : 8 * at + 8, :] = p[:, :LANES] + p[:, LANES:]

    w, aw = krylov(apply, q)
    y, ay = zip(*[krylov(apply, face_ref[5] * v) for v in w])
    for i in range(3):
        field_ref[i] = w[i]
        field_ref[3 + 2 * i] = y[i][1]
        field_ref[4 + 2 * i] = y[i][2]
    orders = [(k, l) for k in range(3) for l in range(k + 1)]
    at = 0
    for i in range(3):
        for j in range(3):
            for k, l in orders:
                inner(at, y[i][k], ay[j][l])
                at += 1
            for k in range(3):
                inner(at, y[i][k], y[j][0])
                at += 1
    for k, l in orders:
        inner(at, w[k], aw[l])
        at += 1
    for k in range(3):
        inner(at, w[k], q)
        at += 1
    part_ref[8 * at :, :] = jnp.zeros((8 * (LANES - at), LANES), F32)
    zero = jnp.zeros((LANES, LANES), F32)
    pieces = [(part_ref[pl.ds(s, LANES, stride=8), :], zero) for s in range(8)]
    hi, lo = tree(pieces)
    hi, lo = jnp.transpose(hi), jnp.transpose(lo)
    total = rows_sum(hi)
    row = total[0] + (total[1] + rows_sum(lo)[0])
    row_ref[...] = jnp.broadcast_to(row[0:1], row_ref.shape)


def sums(q, north, south, faces, token):
    rows, wide = q.shape
    return pl.pallas_call(
        sums_kernel,
        out_shape=(shape(LANES, LANES), shape(9, rows + 16, wide)),
        in_specs=[VMEM] * 5,
        out_specs=(VMEM,) * 2,
        scratch_shapes=[pltpu.VMEM((8 * LANES, LANES), F32)],
        compiler_params=params(8),
        name="krylov_sums",
    )(q, north, south, faces, token)


def two_prod(a, b):
    p = a * b
    t = 4097.0 * a
    ah = t - (t - a)
    al = a - ah
    t = 4097.0 * b
    bh = t - (t - b)
    bl = b - bh
    return p, ((ah * bh - p) + (ah * bl + al * bh)) + al * bl


def quick(s, e):
    t = s + e
    return t, e - (t - s)


def pair_add(x, y):
    s, e = two_sum(x[0], y[0])
    return quick(s, e + (x[1] + y[1]))


def pair_neg(x):
    return -x[0], -x[1]


def pair_mul(x, y):
    p, e = two_prod(x[0], y[0])
    return quick(p, e + (x[0] * y[1] + x[1] * y[0]))


def pair_div(x, y):
    first = x[0] / y[0]
    p, e = two_prod(first, y[0])
    rest = ((x[0] - p) - e) + (x[1] - first * y[1])
    return quick(first, rest / y[0])


def minor(a, b, c, d):
    return pair_add(pair_mul(a, b), pair_neg(pair_mul(c, d)))


def pair_sum3(a, b, c):
    return pair_add(pair_add(a, b), c)


def small_solve(g, b):
    g00, g10, g11, g20, g21, g22 = g
    c00, c01, c02 = minor(g11, g22, g21, g21), minor(g20, g21, g10, g22), minor(g10, g21, g20, g11)
    c11, c12, c22 = minor(g00, g22, g20, g20), minor(g10, g20, g00, g21), minor(g00, g11, g10, g10)
    det = pair_sum3(pair_mul(g00, c00), pair_mul(g10, c01), pair_mul(g20, c02))
    three = det[0] > 1e-8 * (c22[0] * g22[0])
    two = c22[0] > 1e-8 * (g00[0] * g11[0])
    three = three & two
    rows = ((c00, c01, c02), (c01, c11, c12), (c02, c12, c22))
    full = [pair_div(pair_sum3(*[pair_mul(m, v) for m, v in zip(row, b)]), det)[0] for row in rows]
    half = [
        pair_div(minor(g11, b[0], g10, b[1]), c22)[0],
        pair_div(minor(g00, b[1], g10, b[0]), c22)[0],
        jnp.zeros_like(det[0]),
    ]
    alone = [b[0][0] / g00[0], half[2], half[2]]
    return [jnp.where(three, x, jnp.where(two, y, z)) for x, y, z in zip(full, half, alone)]


def coefficients(every_ref):
    total = quick(*rows_sum(every_ref[...]))

    def pick(x, at):
        return tuple(jnp.broadcast_to(v[:, at : at + 1], (8, LANES)) for v in x)

    def scaled(x, at):
        by = 1.0 / jnp.broadcast_to(x[0][:, at : at + 1], (8, LANES))
        p, e = two_prod(x[0], by)
        return quick(p, e + x[1] * by)

    first = scaled(total, 81)
    first = [pick(first, 81 + m) for m in range(9)]
    c = small_solve(first[:6], first[6:])
    terms = []
    for i in range(3):
        for j in range(3):
            shift = (LANES - 9 * (3 * i + j)) % LANES
            row = tuple(pltpu.roll(v, shift, 1) if shift else v for v in total)
            terms.append(pair_mul(row, two_prod(c[i], c[j])))
    while len(terms) > 1:
        odd = terms[len(terms) // 2 * 2 :]
        terms = [pair_add(terms[i], terms[i + 1]) for i in range(0, len(terms) - 1, 2)] + odd
    second = scaled(terms[0], 0)
    second = [pick(second, m) for m in range(9)]
    return c, small_solve(second[:6], second[6:])


def tracer_kernel(steric_ref, every_ref, field_ref, face_ref, far_ref, side_ref, mu_ref, rho_ref, tall_ref, sems):
    levels, rows, cols = mu_ref.shape

    def copy(level):
        return pltpu.make_async_copy(far_ref.at[level], tall_ref.at[level], sems.at[level])

    for level in range(levels):
        copy(level).start()
    high, wide = rows + 8, cols + LANES

    def trim(v):
        edge = jnp.where(iota((8, wide), 0) < 4, v[rows : rows + 8], v[rows + 8 :])
        return jnp.concatenate([v[:rows], edge], axis=0)

    c, e = coefficients(every_ref)
    c, e = [[jnp.broadcast_to(v[0:1, 0:1], (1, 1)) for v in part] for part in (c, e)]
    w = [trim(field_ref[i]) for i in range(3)]
    ocean = trim(face_ref[5])
    rho_1 = c[0] * w[0] + c[1] * w[1] + c[2] * w[2]
    rho_0 = e[0] * (ocean * rho_1)
    for k in (1, 2):
        v = [trim(field_ref[2 + k + 2 * i]) for i in range(3)]
        rho_0 = rho_0 + e[k] * (c[0] * v[0] + c[1] * v[1] + c[2] * v[2])
    rho_ref[...] = rho_0[:rows, :cols]

    def one_level(level):
        height = steric_ref[level]
        full = lambda at: jnp.concatenate([tall_ref[level, at], side_ref[at, level]], axis=1)
        g = ocean * (full(0) + height * rho_1)
        dx = g - pltpu.roll(g, wide - 1, 1)
        dy = g - pltpu.roll(g, high - 1, 0)
        mu = g - (
            full(1) * dx + pltpu.roll(full(2) * dx, 1, 1) + full(3) * dy + pltpu.roll(full(4) * dy, 1, 0)
        )
        g = ocean * (mu + height * rho_0)
        dx = (g - pltpu.roll(g, wide - 1, 1))[:rows]
        dy = (g - pltpu.roll(g, high - 1, 0))[:, :cols]
        back_x = pltpu.roll(full(5)[:rows] * dx, 1, 1)[:, :cols]
        back_y = pltpu.roll(tall_ref[level, 6] * dy, 1, 0)[:rows]
        mu_ref[level] = g[:rows, :cols] - (
            tall_ref[level, 7, 0:rows, :] * dx[:, :cols] + back_x + tall_ref[level, 8, 0:rows, :] * dy[:rows] + back_y
        )

    def some_levels(group, carry):
        for i in range(GROUP):
            copy(group * GROUP + i).wait()
        for i in range(GROUP):
            one_level(group * GROUP + i)
        return carry

    lax.fori_loop(0, levels // GROUP, some_levels, 0)


def tracers(steric, every, fields, faces, tall, side):
    levels, count, high, cols = tall.shape
    rows = high - 8
    return pl.pallas_call(
        tracer_kernel,
        out_shape=(shape(levels, rows, cols), shape(rows, cols)),
        in_specs=[SCALAR] + [VMEM] * 3 + [HBM, VMEM],
        out_specs=(VMEM, VMEM),
        scratch_shapes=[pltpu.VMEM((levels, count, high, cols), F32), pltpu.SemaphoreType.DMA((levels,))],
        compiler_params=params(20),
        name="tracer_steps",
    )(steric, every, fields, faces, *far((tall,)), side)


def beside(cells, axis, step):
    count = lax.axis_size(axis)
    return lax.ppermute(cells, axis, [((i + step) % count, i) for i in range(count)])


def tracer_fields(keep, lam, zonal_1, merid_1, zonal_0, merid_0, mix_x, mix_y):
    flow_x, flow_y = 0.5 * zonal_1, 0.5 * merid_1
    past_x, past_y = 0.5 * zonal_0, 0.5 * merid_0
    return (
        lam,
        flow_x + mix_x,
        flow_x - mix_x,
        keep * (flow_y + mix_y),
        keep * (flow_y - mix_y),
        past_x - mix_x,
        keep * (past_y - mix_y),
        past_x + mix_x,
        keep * (past_y + mix_y),
    )


def surface_fields(keep, diag_ref, east_ref, north_ref, land_ref, rows):
    return diag_ref[rows], east_ref[rows], keep * north_ref[rows], land_ref[rows].astype(F32)


UP = (0, 1, 2, 3)
DOWN = (0, 1, 2, 3, 4, 6)
SIDE = (0, 1, 2, 3, 4, 5)


def kept(token_ref, first, count, rows, cols):
    last = jnp.concatenate([token_ref[0:1, :]] * (cols // LANES), axis=1)
    return jnp.where((iota((count, cols), 0) + first == rows - 1) & (last == 1.0), 0.0, 1.0)


def opening_kernel(capacity, token_ref, lam_ref, zonal_ref, merid_ref, mix_x_ref, mix_y_ref, *refs):
    surface_refs, (sla_ref, weight_ref), marks = refs[:4], refs[4:6], refs[6:9]
    up_ref, down_ref, next_ref, data_ref, place_ref, meta_ref = refs[9:15]
    held_ref, flat_ref, land_ref, segment_ref, mark_ref, sems, flat_sems, segment_sems, mark_sems = refs[15:]
    levels, rows, cols = lam_ref.shape
    blocks = mark_ref.shape[1]

    def started(source, target, sem):
        copy = pltpu.make_async_copy(source, target, sem)
        copy.start()
        return copy

    mark_copies = [started(ref, mark_ref.at[i], mark_sems.at[i]) for i, ref in enumerate(marks)]
    segment_copies = []
    for k in range(2):
        block = pl.ds(k * blocks * LANES // 2, blocks * LANES // 2)
        for i, ref in enumerate((sla_ref, weight_ref)):
            segment_copies.append(started(ref.at[block, :], segment_ref.at[i, block, :], segment_sems.at[2 * k + i]))
    copies, flat_copies = [], []
    for part, (first, outer) in enumerate(((0, 0), (rows - 8, rows - 2))):
        block = pl.ds(outer, 2)
        for source in (
            lam_ref.at[:, block, :],
            zonal_ref.at[1, :, block, :],
            merid_ref.at[1, :, block, :],
            mix_x_ref.at[:, block, :],
            mix_y_ref.at[:, block, :],
            merid_ref.at[0, :, block, :],
        )[: 5 + part]:
            copies.append(started(source, held_ref.at[len(copies)], sems.at[len(copies)]))
        block = pl.ds(first, 8)
        for i, ref in enumerate(surface_refs[:3]):
            flat_copies.append(started(ref.at[block, :], flat_ref.at[part, i], flat_sems.at[len(flat_copies)]))
        ref = surface_refs[3]
        flat_copies.append(started(ref.at[block, :], land_ref.at[part], flat_sems.at[len(flat_copies)]))
    next_ref[...] = token_ref[...]

    for copy in mark_copies:
        copy.wait()
    col_t, count_t = ranks(capacity, mark_ref[0], mark_ref[1], mark_ref[2], place_ref, meta_ref)
    for copy in copies + flat_copies:
        copy.wait()
    for part, (out_ref, picks, first, take) in enumerate(((up_ref, UP, 0, 0), (down_ref, DOWN, rows - 8, 6))):
        keep = kept(token_ref, first, 8, rows, cols)
        base = 2 * len(picks) * levels
        diag, east, north = [flat_ref[part, i] for i in range(3)]
        ocean = land_ref[part].astype(F32)
        for at, field in enumerate((diag, east, keep * north, ocean)):
            out_ref[base + 8 * at : base + 8 * at + 8, :] = field
        for level in range(levels):
            lam, zonal_1, merid_1, mix_x, mix_y, merid_0 = [held_ref[5 * part + min(i, 4 + part), level] for i in range(6)]
            fields = tracer_fields(keep[take : take + 2], lam, zonal_1, merid_1, zonal_1, merid_0, mix_x, mix_y)
            for at, pick in enumerate(picks):
                base = 2 * (at * levels + level)
                out_ref[base : base + 2, :] = fields[pick]
    for copy in segment_copies:
        copy.wait()
    for k in range(blocks):
        here = slice(k * LANES, (k + 1) * LANES)
        turned_rows(
            data_ref, k, segment_ref[1, here, :], segment_ref[0, here, :], col_t[:, k : k + 1], count_t[:, k : k + 1]
        )


def edge_rows(n_ref, s_ref, pick, levels, level, cols):
    zero = lambda count: jnp.zeros((count, cols), F32)
    north = zero(2)
    if pick in UP:
        base = 2 * (UP.index(pick) * levels + level)
        north = n_ref[base : base + 2, :]
    south = zero(2)
    if pick in DOWN:
        base = 2 * (DOWN.index(pick) * levels + level)
        south = s_ref[base : base + 2, :]
    return jnp.concatenate([north, zero(4), south], axis=0)


def halves(tall):
    lane = iota((tall.shape[0], LANES), 1)
    return jnp.where(lane < LANES // 2, tall[:, :LANES], tall[:, -LANES:])


def gathered(talls, width):
    lane = iota((talls[0].shape[0], LANES), 1)
    mixed = jnp.zeros((talls[0].shape[0], LANES), F32)
    for at, tall in enumerate(talls):
        mixed = jnp.where(lane // (2 * width) == at, pltpu.roll(halves(tall), width + 2 * width * at, 1), mixed)
    return mixed


def scattered(mixed, at, width):
    return pltpu.roll(mixed, LANES - width - 2 * width * at, 1)


TRACER_WIDTH = 2
FACE_WIDTH = 8


GROUP = 4


def cols_kernel(token_ref, lam_ref, zonal_ref, merid_ref, mix_x_ref, mix_y_ref, *refs):
    surface_refs, height_refs, (n_ref, s_ref) = refs[:4], refs[4:6], refs[6:8]
    out_ref, far_ref, face_ref, height_ref, held_ref, flat_ref, tall_ref, sems, far_sems = refs[8:]
    levels, rows, cols = lam_ref.shape
    copies = []
    for group in range(levels // GROUP):
        block = pl.ds(group * GROUP, GROUP)
        for i, source in enumerate(
            (
                lam_ref.at[block],
                zonal_ref.at[1, block],
                merid_ref.at[1, block],
                zonal_ref.at[0, block],
                merid_ref.at[0, block],
                mix_x_ref.at[block],
                mix_y_ref.at[block],
            )
        ):
            copies.append(pltpu.make_async_copy(source, held_ref.at[i, block], sems.at[len(copies)]))
            copies[-1].start()
    keep = kept(token_ref, 0, rows, rows, cols)
    high = rows + 8
    used = 2 * TRACER_WIDTH * len(SIDE)
    blocks = levels * high // LANES
    base = blocks * used
    up, down = 2 * len(UP) * levels, 2 * len(DOWN) * levels
    talls = []
    for at, field in enumerate(surface_fields(keep, *surface_refs, slice(0, rows))):
        tall = jnp.concatenate(
            [field, n_ref[up + 8 * at : up + 8 * at + 8, :], s_ref[down + 8 * at : down + 8 * at + 8, :]], axis=0
        )
        face_ref[at] = tall
        talls.append(tall)
    for at, ref in enumerate(height_refs):
        height_ref[at] = ref[...]
        talls.append(jnp.concatenate([ref[...], jnp.zeros((16, cols), F32)], axis=0))
    out_ref[base : base + rows + 16, :] = gathered(talls, FACE_WIDTH)
    far = []
    for level in range(levels):
        if level % GROUP == 0:
            for copy in copies[7 * (level // GROUP) : 7 * (level // GROUP) + 7]:
                copy.wait()
        fields = tracer_fields(keep, *[held_ref[i, level] for i in range(7)])
        talls = []
        for pick, field in enumerate(fields):
            tall_ref[level, pick, 0:rows, :] = field
            edge = edge_rows(n_ref, s_ref, pick, levels, level, cols)
            tall_ref[level, pick, rows:high, :] = edge
            if pick in SIDE:
                talls.append(jnp.concatenate([field, edge], axis=0))
        flat_ref[level * high : (level + 1) * high, :] = gathered(talls, TRACER_WIDTH)
        far.append(pltpu.make_async_copy(tall_ref.at[level], far_ref.at[level], far_sems.at[level]))
        far[-1].start()
    for b in range(blocks):
        turned = jnp.transpose(flat_ref[b * LANES : (b + 1) * LANES, :])
        out_ref[b * used : (b + 1) * used, :] = turned[:used]
    for copy in far:
        copy.wait()


def side_kernel(strip_ref, token_ref, side_ref, next_ref, flat_ref):
    next_ref[...] = token_ref[...]
    levels, high = side_ref.shape[1:3]
    used = 2 * TRACER_WIDTH * len(SIDE)
    blocks = levels * high // LANES
    for b in range(blocks):
        both = strip_ref[b * used : (b + 1) * used, :]
        both = jnp.concatenate([both, jnp.zeros((LANES - used, LANES), F32)], axis=0)
        flat_ref[b * LANES : (b + 1) * LANES, :] = jnp.transpose(both)
    for level in range(levels):
        mixed = flat_ref[level * high : (level + 1) * high, :]
        for at in range(len(SIDE)):
            side_ref[at, level] = scattered(mixed, at, TRACER_WIDTH)


def face_halo_kernel(base, token_ref, tall_ref, height_ref, e_ref, w_ref, face_ref, full_ref, strip_ref):
    from_west = iota((base, LANES), 0) % (2 * TRACER_WIDTH) < TRACER_WIDTH
    strip_ref[...] = jnp.where(from_west, w_ref[0:base, :], e_ref[0:base, :])
    high = tall_ref.shape[1]
    rows = height_ref.shape[1]
    for at in range(2):
        full_ref[at, :, : -LANES] = height_ref[at]
    western = iota((high, LANES), 1) % (2 * FACE_WIDTH) < FACE_WIDTH
    here = slice(base, base + high)
    mixed = jnp.where(western, w_ref[here, :], e_ref[here, :])
    for at in range(2):
        full_ref[at, :, -LANES:] = scattered(mixed, 4 + at, FACE_WIDTH)[:rows]
    full = [jnp.concatenate([tall_ref[at], scattered(mixed, at, FACE_WIDTH)], axis=1) for at in range(4)]
    diag, east, north, ocean = full
    west, south = pltpu.roll(east, 1, 1), pltpu.roll(north, 1, 0)
    face_ref[0] = (1.0 + diag) + east + west + north + south
    for at, field in enumerate((east, west, north, south, ocean)):
        face_ref[1 + at] = field


def opening(token, tracer, surface, segments, marks, capacity):
    levels, rows, cols = tracer[0].shape
    up, down = 2 * len(UP) * levels + 32, 2 * len(DOWN) * levels + 32
    blocks = segments[0].shape[0] // LANES
    marks = tuple(mark.reshape(blocks, LANES) for mark in marks)
    return pl.pallas_call(
        functools.partial(opening_kernel, capacity),
        out_shape=(
            shape(up, cols),
            shape(down, cols),
            shape(*token.shape),
            jax.ShapeDtypeStruct((blocks * LANES, 4 * LANES), BF16),
            jax.ShapeDtypeStruct((blocks, LANES), jnp.int32),
            shape(LANES, LANES),
        ),
        in_specs=[VMEM] + [HBM] * 14,
        out_specs=(VMEM,) * 6,
        scratch_shapes=[
            pltpu.VMEM((11, levels, 2, cols), F32),
            pltpu.VMEM((2, 3, 8, cols), F32),
            pltpu.VMEM((2, 8, cols), jnp.int32),
            pltpu.VMEM((2, blocks * LANES, LANES), F32),
            pltpu.VMEM((3, blocks, LANES), jnp.int32),
            pltpu.SemaphoreType.DMA((11,)),
            pltpu.SemaphoreType.DMA((8,)),
            pltpu.SemaphoreType.DMA((4,)),
            pltpu.SemaphoreType.DMA((3,)),
        ],
        compiler_params=params(12),
        name="opening",
    )(token, *far(tracer), *far(surface), *far(segments), *far(marks))


def edges_to_tx(token, tracer, surface, heights, north, south):
    levels, rows, cols = tracer[0].shape
    high = rows + 8
    side_rows = 2 * TRACER_WIDTH * len(SIDE) * levels * high // LANES + rows + 16
    sides, tall, faces, heights = pl.pallas_call(
        cols_kernel,
        out_shape=(
            shape(side_rows, LANES),
            far_shape(levels, 9, high, cols),
            shape(4, rows + 16, cols),
            shape(2, rows, cols),
        ),
        in_specs=[VMEM] + [HBM] * 5 + [VMEM] * 8,
        out_specs=(VMEM, HBM, VMEM, VMEM),
        scratch_shapes=[
            pltpu.VMEM((7, levels, rows, cols), F32),
            pltpu.VMEM((levels * high, LANES), F32),
            pltpu.VMEM((levels, 9, high, cols), F32),
            pltpu.SemaphoreType.DMA((7 * levels // GROUP,)),
            pltpu.SemaphoreType.DMA((levels,)),
        ],
        compiler_params=params(24),
        name="edge_columns",
    )(token, *far(tracer), *far(surface), *far(heights), north, south)
    return (beside(sides, "tx", 1), beside(sides, "tx", -1)), tall, faces, heights


def faces_with_halo(token, tall, heights, east, west):
    count, high, cols = tall.shape
    base = east.shape[0] - high
    return pl.pallas_call(
        functools.partial(face_halo_kernel, base),
        out_shape=(shape(6, high, cols + LANES), shape(2, heights.shape[1], cols + LANES), shape(base, LANES)),
        in_specs=[VMEM] * 5,
        out_specs=(VMEM,) * 3,
        compiler_params=params(6),
        name="surface_halos",
    )(token, tall, heights, east, west)


def tracer_sides(token, strips, levels, rows):
    high = rows + 8
    return pl.pallas_call(
        side_kernel,
        out_shape=(shape(len(SIDE), levels, high, LANES), shape(*token.shape)),
        in_specs=[VMEM] * 2,
        out_specs=(VMEM, VMEM),
        scratch_shapes=[pltpu.VMEM((levels * high, LANES), F32)],
        compiler_params=params(8),
        name="tracer_halos",
    )(strips, token)


def on_device(
    lam_tracer,
    lam_eta,
    land,
    zonal_flow,
    merid_flow,
    zonal_mixing,
    merid_mixing,
    surface_east,
    surface_north,
    surface_diag,
    steric,
    eta_saved,
    obs_sla,
    obs_weight,
    obs_tile,
    obs_start,
    obs_count,
):
    levels, rows, cols = lam_tracer.shape
    n_rows = lax.axis_size("ty")
    devices = n_rows * lax.axis_size("tx")
    capacity = 2 * obs_sla.shape[0] // devices
    token = jnp.full((8, LANES), lax.axis_index("ty") == n_rows - 1, F32)
    tracer = (lam_tracer, zonal_flow, merid_flow, zonal_mixing, merid_mixing)
    surface = (surface_diag, surface_east, surface_north, land)
    to_south, to_north, token, *ranked = opening(
        token, tracer, surface, (obs_sla, obs_weight), (obs_tile, obs_start, obs_count), capacity
    )
    around_ty = beside(to_south, "ty", 1), beside(to_north, "ty", -1)
    sent, token = placed(*ranked, token, capacity, devices // n_rows)
    sent, *around_ty = lax.optimization_barrier((sent, *around_ty))
    got = lax.all_to_all(
        sent.reshape(devices, 1, -1), AXES, split_axis=0, concat_axis=0, tiled=True
    ).reshape(sent.shape)
    around_tx, tall, faces, heights = edges_to_tx(token, tracer, surface, (lam_eta, eta_saved), *around_ty)
    faces, heights, strips = faces_with_halo(token, faces, heights, *around_tx)
    rhs, token = unpack(got, heights, faces, token, capacity)
    north, south = beside(rhs[:8], "ty", 1), beside(rhs[-8:], "ty", -1)
    sides, token = tracer_sides(token, strips, levels, rows)
    mine, krylov_fields = sums(rhs, north, south, faces, token)
    every = lax.all_to_all(
        mine.reshape(devices, 1, LANES), AXES, split_axis=0, concat_axis=0, tiled=True
    ).reshape(devices, LANES)
    return tracers(steric, every, krylov_fields, faces, tall, sides)


def solution(mesh):
    in_specs = (
        P(None, "ty", "tx"),
        P("ty", "tx"),
        P("ty", "tx"),
        P(None, None, "ty", "tx"),
        P(None, None, "ty", "tx"),
        P(None, "ty", "tx"),
        P(None, "ty", "tx"),
        P("ty", "tx"),
        P("ty", "tx"),
        P("ty", "tx"),
        P(),
        P("ty", "tx"),
        P(AXES, None),
        P(AXES, None),
        P(AXES, None),
        P(AXES),
        P(AXES),
    )
    out_specs = (P(None, "ty", "tx"), P("ty", "tx"))
    return jax.shard_map(
        on_device, mesh=mesh, in_specs=in_specs, out_specs=out_specs, check_vma=False
    )
```

```python
import functools

import jax
import jax.numpy as jnp
from jax import lax
from jax.experimental import pallas as pl
from jax.experimental.pallas import tpu as pltpu
from jax.sharding import PartitionSpec as P

AXES = ("ty", "tx")
SHIFT_0 = 1.6
SHIFT_1 = 35.0
SCALE_0 = 1.0 / 32.0
SCALE_1 = 1.0 / 16.0
LANES = 128
VMEM = pl.BlockSpec(memory_space=pltpu.VMEM)
SCALAR = pl.BlockSpec(memory_space=pltpu.SMEM)
HBM = pl.BlockSpec(memory_space=pltpu.HBM)
F32 = jnp.float32
BF16 = jnp.bfloat16


def params(mib):
    return pltpu.CompilerParams(vmem_limit_bytes=mib * 1024 * 1024)


def iota(dims, axis):
    return lax.broadcasted_iota(jnp.int32, dims, axis)


def shape(*dims):
    return jax.ShapeDtypeStruct(dims, F32)


def far_shape(*dims):
    return pltpu.HBM(dims, F32)


def far(arrays):
    return tuple(pltpu.with_memory_space_constraint(x, pltpu.HBM) for x in arrays)


def split(x):
    hi = x.astype(BF16)
    return hi, (x - hi.astype(F32)).astype(BF16)


def ranks(capacity, tile, start, count, place_ref, meta_ref):
    blocks = tile.shape[0]
    square = (LANES, LANES)
    sub, lane = iota(square, 0), iota(square, 1)
    prefix = jnp.concatenate([(sub < lane).astype(BF16), jnp.ones(square, BF16)], axis=1)
    carry = jnp.zeros(square, F32)
    hits, firsts = [], []
    for k in range(blocks):
        target = tile[k : k + 1]
        hit = sub == target
        hits.append(hit.astype(F32).astype(BF16))
        both = jnp.dot(hits[-1], prefix, preferred_element_type=F32)
        slot = jnp.sum(jnp.where(hit, both[:, :LANES] + carry, 0.0), axis=0, keepdims=True)
        carry = carry + both[:, LANES:]
        slot = slot.astype(jnp.int32)
        place_ref[k : k + 1, :] = target * capacity + slot
        begin = start[k : k + 1]
        block_of = jnp.where(sub == slot, begin // LANES, 0)
        lane_of = jnp.where(sub == slot + 64, begin & (LANES - 1), 0)
        firsts.append((block_of + lane_of).astype(F32).astype(BF16))
    meta_ref[...] = lax.dot_general(
        jnp.concatenate(hits, axis=1),
        jnp.concatenate(firsts, axis=1),
        (((1,), (1,)), ((), ())),
        preferred_element_type=F32,
    )
    col_t = jnp.transpose((start & (LANES - 1)).astype(F32)).astype(jnp.int32)
    return col_t, jnp.transpose(count.astype(F32)).astype(jnp.int32)


def turned_rows(data_ref, k, weight, sla, col, count):
    lane = iota((LANES, LANES), 1)
    weight = jnp.where(lane < count, weight, 0.0)
    value = weight * sla
    index = (lane - col) & (LANES - 1)
    weight = jnp.take_along_axis(weight, index, axis=1)
    value = jnp.take_along_axis(value, index, axis=1)
    data_ref[k * LANES : (k + 1) * LANES, :] = jnp.concatenate([*split(weight), *split(value)], axis=1)


EDGE = 5
WIDE = 2 * EDGE
FIRST_SLOTS = 12


def edge_lanes(rows):
    slot, lane = iota((rows, LANES), 0) % 16, iota((rows, LANES), 1)
    rest = 16 - FIRST_SLOTS
    late = slot - FIRST_SLOTS
    is_first = (lane // WIDE == slot) & (late < 0)
    is_late = ((lane // WIDE) % rest == late) & (lane < 2 * rest * WIDE)
    first = (lane - WIDE * slot) & (LANES - 1)
    second = (first + WIDE) & (LANES - 1)
    third = jnp.where(lane < rest * WIDE, lane - WIDE * late, lane - WIDE * (late + rest - 1)) & (LANES - 1)
    return (first, is_first), (second, is_first), (third, is_late)


def folded(parts):
    sub = iota((8, LANES), 0)
    for step in (4, 2, 1):
        low = (sub & step) == 0
        half = len(parts) // 2
        pairs = []
        for a, b in zip(parts[:half], parts[half:]):
            other = jnp.where(low, b, a)
            moved = jnp.where(low, pltpu.roll(other, 8 - step, 0), pltpu.roll(other, step, 0))
            pairs.append(jnp.where(low, a, b) + moved)
        parts = pairs
    return parts[0]


def place_kernel(capacity, n_cols, data_ref, place_ref, meta_ref, token_ref, out_ref, next_ref, made_ref, sems):
    next_ref[...] = token_ref[...]
    blocks = place_ref.shape[0]
    chunk = 2 * capacity + 4
    place = jnp.concatenate([place_ref[k : k + 1, :] for k in range(blocks)], axis=1)
    height = n_cols * capacity
    slots = iota((height, blocks * LANES), 0)
    lane = iota((capacity, LANES), 1)
    ends = jnp.where(lane < WIDE, lane % EDGE, LANES - EDGE + lane % EDGE)
    in_value = (lane // EDGE) % 2 == 1
    lanes = edge_lanes(capacity)
    western = iota((n_cols, LANES), 1) < WIDE * (16 - FIRST_SLOTS)
    east_of = lambda x: pltpu.roll(x, n_cols - 1, 0)
    west_of = lambda x: pltpu.roll(x, 1, 0)
    copies = []
    for g in range(LANES // n_cols):
        pick = (slots == place - g * height).astype(F32).astype(BF16)
        moved = jnp.dot(pick, data_ref[...], preferred_element_type=F32)
        weight = moved[:, :LANES] + moved[:, LANES : 2 * LANES]
        value = moved[:, 2 * LANES : 3 * LANES] + moved[:, 3 * LANES :]
        first = g * n_cols * chunk
        parts = [[], [], []]
        for t in range(n_cols):
            base = first + t * chunk
            rows = slice(t * capacity, (t + 1) * capacity)
            made_ref[base : base + capacity, :] = weight[rows]
            made_ref[base + capacity : base + 2 * capacity, :] = value[rows]
            both = jnp.where(
                in_value,
                jnp.take_along_axis(value[rows], ends, axis=1),
                jnp.take_along_axis(weight[rows], ends, axis=1),
            )
            for part, (index, mine) in zip(parts[:2], lanes):
                spread = jnp.where(mine, jnp.take_along_axis(both, index, axis=1), 0.0)
                part.append(spread[:8] + spread[8:])
            index, mine = lanes[2]
            parts[2].append(jnp.where(mine[8:], jnp.take_along_axis(both[8:], index[8:], axis=1), 0.0))
        edges = [
            jnp.concatenate([folded(part[i : i + 8]) for i in range(0, n_cols, 8)], axis=0) for part in parts
        ]
        meta = meta_ref[g * n_cols : (g + 1) * n_cols, :]
        meta = (
            meta + pltpu.roll(east_of(meta), capacity, 1) + pltpu.roll(west_of(meta), 2 * capacity, 1)
        )
        extra = (
            meta,
            east_of(edges[0]),
            west_of(edges[1]),
            jnp.where(western, east_of(edges[2]), west_of(edges[2])),
        )
        for i, rows in enumerate(extra):
            made_ref[pl.ds(first + 2 * capacity + i, n_cols, stride=chunk), :] = rows
        ready = pl.ds(first, n_cols * chunk)
        copies.append(pltpu.make_async_copy(made_ref.at[ready, :], out_ref.at[ready, :], sems.at[g]))
        copies[-1].start()
    for copy in copies:
        copy.wait()


def placed(data, place, meta, token, capacity, n_cols):
    chunk = 2 * capacity + 4
    return pl.pallas_call(
        functools.partial(place_kernel, capacity, n_cols),
        out_shape=(far_shape(LANES * chunk, LANES), shape(*token.shape)),
        in_specs=[VMEM] * 4,
        out_specs=(HBM, VMEM),
        scratch_shapes=[
            pltpu.VMEM((LANES * chunk, LANES), F32),
            pltpu.SemaphoreType.DMA((LANES // n_cols,)),
        ],
        compiler_params=params(12),
        name="place_segments",
    )(data, place, meta, token)


def unpack_kernel(capacity, got_ref, height_ref, face_ref, token_ref, q_ref, next_ref, sum_ref):
    next_ref[...] = token_ref[...]
    chunk = 2 * capacity + 4
    square = (LANES, LANES)
    lane = iota(square, 1)
    meta = got_ref[pl.ds(2 * capacity, LANES, stride=chunk), :]
    meta_t = jnp.transpose(meta)
    rows, cols = q_ref.shape[0], q_ref.shape[1] - LANES
    cells = rows * cols // LANES
    blocks = iota((cells, LANES), 0).astype(F32)
    lane_f = lane.astype(F32)
    acc = jnp.zeros((cells, 4 * LANES), F32)
    for j in range(capacity):
        weight = got_ref[pl.ds(j, LANES, stride=chunk), :]
        value = got_ref[pl.ds(capacity + j, LANES, stride=chunk), :]
        here = lane_f >= meta[:, 64 + j : 65 + j]
        hit = (blocks == meta_t[j : j + 1]).astype(F32).astype(BF16)
        his, los = [], []
        for x in (weight, value):
            hi = x.astype(BF16).astype(F32)
            lo = x - hi
            for keep in (here, ~here):
                his.append(jnp.where(keep, hi, 0.0).astype(BF16))
                los.append(jnp.where(keep, lo, 0.0).astype(BF16))
        data = jnp.concatenate(
            [jnp.concatenate(his, axis=1), jnp.concatenate(los, axis=1)], axis=0
        )
        acc = acc + jnp.dot(
            jnp.concatenate([hit, hit], axis=1), data, preferred_element_type=F32
        )
    for i in range(2):
        here, after = acc[:, 2 * i * LANES : (2 * i + 1) * LANES], acc[:, (2 * i + 1) * LANES : (2 * i + 2) * LANES]
        sum_ref[i, :, :] = here + pltpu.roll(after, 1, 0)
    for half in range(2):
        at = slice(half * LANES, (half + 1) * LANES)
        weight = sum_ref[0, pl.ds(half, rows, stride=2), :]
        value = sum_ref[1, pl.ds(half, rows, stride=2), :]
        mu = height_ref[0, :, at] + (weight * height_ref[1, :, at] - value)
        q_ref[:, at] = face_ref[5, 0:rows, at] * mu

    row_of = iota((rows, LANES), 0).astype(F32)
    group = iota((rows, LANES), 1) // WIDE
    rest = capacity - FIRST_SLOTS
    at = lane % EDGE
    first = capacity + jnp.minimum(lane // WIDE, FIRST_SLOTS - 1)
    late = capacity + FIRST_SLOTS + (lane // WIDE) % rest
    western = lane < rest * WIDE
    edges = []
    for i, (index, is_west) in enumerate(
        ((first, True), (first + capacity, False), (jnp.where(western, late, late + capacity), western))
    ):
        block = jnp.take_along_axis(meta, index, axis=1)
        start = jnp.take_along_axis(meta, index + 64, axis=1).astype(jnp.int32)
        odd = block != 2.0 * jnp.floor(0.5 * block)
        has_west = ~odd & (at >= start)
        has_east = odd | (LANES - EDGE + at < start)
        if is_west is True:
            valid = has_west
        elif is_west is False:
            valid = has_east
        else:
            valid = (is_west & has_west) | (~is_west & has_east)
        edge = got_ref[pl.ds(2 * capacity + 1 + i, LANES, stride=chunk), :]
        edges.append(jnp.concatenate(split(jnp.where(valid, edge, 0.0)), axis=0))

    def edge_sum(base, row, first_group):
        hits = []
        for j in range(capacity):
            hits.append((row_of == jnp.floor(0.5 * meta_t[base + j : base + j + 1])).astype(F32).astype(BF16))

        def spread(picks, edge):
            hit = jnp.concatenate(picks, axis=0)
            return jnp.dot(jnp.concatenate([hit, hit], axis=1), edges[edge], preferred_element_type=F32)

        total = jnp.zeros((rows, LANES), F32)
        full = spread(hits[:FIRST_SLOTS], row)
        for j in range(FIRST_SLOTS):
            total = jnp.where(group == j, full[j * rows : (j + 1) * rows], total)
        tail = spread(hits[FIRST_SLOTS:], 2)
        late = jnp.zeros((rows, LANES), F32)
        for j in range(rest):
            late = jnp.where(group == first_group + j, tail[j * rows : (j + 1) * rows], late)
        if first_group:
            late = pltpu.roll(late, LANES - WIDE * first_group, 1)
        total = total + late
        total = total + pltpu.roll(total, LANES - 6 * WIDE, 1)
        total = total + pltpu.roll(total, LANES - 3 * WIDE, 1)
        total = total + pltpu.roll(total, LANES - WIDE, 1) + pltpu.roll(total, LANES - 2 * WIDE, 1)
        return total, pltpu.roll(total, LANES - EDGE, 1)

    side = slice(cols, cols + LANES)
    eastern = iota((rows, LANES), 1) < LANES // 2
    weight, value = [
        jnp.where(eastern, e, pltpu.roll(w, LANES - EDGE, 1))
        for e, w in zip(edge_sum(capacity, 0, 0), edge_sum(2 * capacity, 1, rest))
    ]
    mu = height_ref[0, :, side] + (weight * height_ref[1, :, side] - value)
    q_ref[:, side] = face_ref[5, 0:rows, side] * mu


def unpack(got, heights, faces, token, capacity):
    rows, wide = heights.shape[1:]
    return pl.pallas_call(
        functools.partial(unpack_kernel, capacity),
        out_shape=(shape(rows, wide), shape(*token.shape)),
        in_specs=[VMEM] * 4,
        out_specs=(VMEM, VMEM),
        scratch_shapes=[pltpu.VMEM((2, rows * (wide - LANES) // LANES, LANES), F32)],
        compiler_params=params(10),
        name="forcing",
    )(got, heights, faces, token)


def two_sum(a, b):
    s = a + b
    t = s - a
    return s, (a - (s - t)) + (b - t)


def pair_sum(x, y):
    s, e = two_sum(x[0], y[0])
    e = e + (x[1] + y[1])
    return s, e


def tree(parts):
    while len(parts) > 1:
        odd = parts[len(parts) // 2 * 2 :]
        parts = [pair_sum(parts[i], parts[i + 1]) for i in range(0, len(parts) - 1, 2)] + odd
    return parts[0]


def rows_sum(hi):
    zero = jnp.zeros((8, LANES), F32)
    total = tree([(hi[8 * i : 8 * i + 8], zero) for i in range(16)])
    for step in (4, 2, 1):
        total = pair_sum(total, (pltpu.roll(total[0], step, 0), pltpu.roll(total[1], step, 0)))
    return total


def krylov(apply, start):
    first = apply(start)
    one = SCALE_0 * (first - SHIFT_0 * start)
    second = apply(one)
    two = SCALE_1 * (second - SHIFT_1 * one)
    return (start, one, two), (first, second, apply(two))


def sums_kernel(q_ref, north_ref, south_ref, face_ref, token_ref, row_ref, field_ref, part_ref):
    rows, cols = q_ref.shape[0], q_ref.shape[1] - LANES
    high, wide = rows + 16, cols + LANES
    q = jnp.concatenate([q_ref[...], north_ref[...], south_ref[...]], axis=0)

    def apply(v):
        return (
            face_ref[0] * v
            - face_ref[1] * pltpu.roll(v, wide - 1, 1)
            - face_ref[2] * pltpu.roll(v, 1, 1)
            - face_ref[3] * pltpu.roll(v, high - 1, 0)
            - face_ref[4] * pltpu.roll(v, 1, 0)
        )

    def inner(at, a, b):
        p = a[:rows, :cols] * b[:rows, :cols]
        p = (p[0:8] + p[8:16]) + (p[16:24] + p[24:32])
        part_ref[8 * at : 8 * at + 8, :] = p[:, :LANES] + p[:, LANES:]

    w, aw = krylov(apply, q)
    y, ay = zip(*[krylov(apply, face_ref[5] * v) for v in w])
    for i in range(3):
        field_ref[i] = w[i]
        field_ref[3 + 2 * i] = y[i][1]
        field_ref[4 + 2 * i] = y[i][2]
    orders = [(k, l) for k in range(3) for l in range(k + 1)]
    at = 0
    for i in range(3):
        for j in range(3):
            for k, l in orders:
                inner(at, y[i][k], ay[j][l])
                at += 1
            for k in range(3):
                inner(at, y[i][k], y[j][0])
                at += 1
    for k, l in orders:
        inner(at, w[k], aw[l])
        at += 1
    for k in range(3):
        inner(at, w[k], q)
        at += 1
    part_ref[8 * at :, :] = jnp.zeros((8 * (LANES - at), LANES), F32)
    zero = jnp.zeros((LANES, LANES), F32)
    pieces = [(part_ref[pl.ds(s, LANES, stride=8), :], zero) for s in range(8)]
    hi, lo = tree(pieces)
    hi, lo = jnp.transpose(hi), jnp.transpose(lo)
    total = rows_sum(hi)
    row = total[0] + (total[1] + rows_sum(lo)[0])
    row_ref[...] = jnp.broadcast_to(row[0:1], row_ref.shape)


def sums(q, north, south, faces, token):
    rows, wide = q.shape
    return pl.pallas_call(
        sums_kernel,
        out_shape=(shape(LANES, LANES), shape(9, rows + 16, wide)),
        in_specs=[VMEM] * 5,
        out_specs=(VMEM,) * 2,
        scratch_shapes=[pltpu.VMEM((8 * LANES, LANES), F32)],
        compiler_params=params(8),
        name="krylov_sums",
    )(q, north, south, faces, token)


def two_prod(a, b):
    p = a * b
    t = 4097.0 * a
    ah = t - (t - a)
    al = a - ah
    t = 4097.0 * b
    bh = t - (t - b)
    bl = b - bh
    return p, ((ah * bh - p) + (ah * bl + al * bh)) + al * bl


def quick(s, e):
    t = s + e
    return t, e - (t - s)


def pair_add(x, y):
    s, e = two_sum(x[0], y[0])
    return quick(s, e + (x[1] + y[1]))


def pair_neg(x):
    return -x[0], -x[1]


def pair_mul(x, y):
    p, e = two_prod(x[0], y[0])
    return quick(p, e + (x[0] * y[1] + x[1] * y[0]))


def pair_div(x, y):
    first = x[0] / y[0]
    p, e = two_prod(first, y[0])
    rest = ((x[0] - p) - e) + (x[1] - first * y[1])
    return quick(first, rest / y[0])


def minor(a, b, c, d):
    return pair_add(pair_mul(a, b), pair_neg(pair_mul(c, d)))


def pair_sum3(a, b, c):
    return pair_add(pair_add(a, b), c)


def small_solve(g, b):
    g00, g10, g11, g20, g21, g22 = g
    c00, c01, c02 = minor(g11, g22, g21, g21), minor(g20, g21, g10, g22), minor(g10, g21, g20, g11)
    c11, c12, c22 = minor(g00, g22, g20, g20), minor(g10, g20, g00, g21), minor(g00, g11, g10, g10)
    det = pair_sum3(pair_mul(g00, c00), pair_mul(g10, c01), pair_mul(g20, c02))
    three = det[0] > 1e-8 * (c22[0] * g22[0])
    two = c22[0] > 1e-8 * (g00[0] * g11[0])
    three = three & two
    rows = ((c00, c01, c02), (c01, c11, c12), (c02, c12, c22))
    full = [pair_div(pair_sum3(*[pair_mul(m, v) for m, v in zip(row, b)]), det)[0] for row in rows]
    half = [
        pair_div(minor(g11, b[0], g10, b[1]), c22)[0],
        pair_div(minor(g00, b[1], g10, b[0]), c22)[0],
        jnp.zeros_like(det[0]),
    ]
    alone = [b[0][0] / g00[0], half[2], half[2]]
    return [jnp.where(three, x, jnp.where(two, y, z)) for x, y, z in zip(full, half, alone)]


def coefficients(every_ref):
    total = quick(*rows_sum(every_ref[...]))

    def pick(x, at):
        return tuple(jnp.broadcast_to(v[:, at : at + 1], (8, LANES)) for v in x)

    def scaled(x, at):
        by = 1.0 / jnp.broadcast_to(x[0][:, at : at + 1], (8, LANES))
        p, e = two_prod(x[0], by)
        return quick(p, e + x[1] * by)

    first = scaled(total, 81)
    first = [pick(first, 81 + m) for m in range(9)]
    c = small_solve(first[:6], first[6:])
    terms = []
    for i in range(3):
        for j in range(3):
            shift = (LANES - 9 * (3 * i + j)) % LANES
            row = tuple(pltpu.roll(v, shift, 1) if shift else v for v in total)
            terms.append(pair_mul(row, two_prod(c[i], c[j])))
    while len(terms) > 1:
        odd = terms[len(terms) // 2 * 2 :]
        terms = [pair_add(terms[i], terms[i + 1]) for i in range(0, len(terms) - 1, 2)] + odd
    second = scaled(terms[0], 0)
    second = [pick(second, m) for m in range(9)]
    return c, small_solve(second[:6], second[6:])


def tracer_kernel(steric_ref, every_ref, field_ref, face_ref, token_ref, *refs):
    tracer_refs, (fringe_ref, side_ref, mu_ref, rho_ref, held_ref, sems) = refs[:5], refs[5:]
    levels, rows, cols = mu_ref.shape
    for group in range(levels // GROUP):
        for copy in level_copies(group, tracer_refs, held_ref, sems):
            copy.start()
    keep = kept(token_ref, 0, rows, rows, cols)
    high, wide = rows + 8, cols + LANES

    def trim(v):
        edge = jnp.where(iota((8, wide), 0) < 4, v[rows : rows + 8], v[rows + 8 :])
        return jnp.concatenate([v[:rows], edge], axis=0)

    c, e = coefficients(every_ref)
    c, e = [[jnp.broadcast_to(v[0:1, 0:1], (1, 1)) for v in part] for part in (c, e)]
    w = [trim(field_ref[i]) for i in range(3)]
    ocean = trim(face_ref[5])
    rho_1 = c[0] * w[0] + c[1] * w[1] + c[2] * w[2]
    rho_0 = e[0] * (ocean * rho_1)
    for k in (1, 2):
        v = [trim(field_ref[2 + k + 2 * i]) for i in range(3)]
        rho_0 = rho_0 + e[k] * (c[0] * v[0] + c[1] * v[1] + c[2] * v[2])
    rho_ref[...] = rho_0[:rows, :cols]

    def one_level(level):
        height = steric_ref[level]
        fields = tracer_fields(keep, *[held_ref[i, level] for i in range(7)])
        tall = lambda at: jnp.concatenate([fields[at], fringe_ref[level, at]], axis=0)
        full = lambda at: jnp.concatenate([tall(at), side_ref[at, level]], axis=1)
        g = ocean * (full(0) + height * rho_1)
        dx = g - pltpu.roll(g, wide - 1, 1)
        dy = g - pltpu.roll(g, high - 1, 0)
        mu = g - (
            full(1) * dx + pltpu.roll(full(2) * dx, 1, 1) + full(3) * dy + pltpu.roll(full(4) * dy, 1, 0)
        )
        g = ocean * (mu + height * rho_0)
        dx = (g - pltpu.roll(g, wide - 1, 1))[:rows]
        dy = (g - pltpu.roll(g, high - 1, 0))[:, :cols]
        back_x = pltpu.roll(full(5)[:rows] * dx, 1, 1)[:, :cols]
        back_y = pltpu.roll(tall(6) * dy, 1, 0)[:rows]
        mu_ref[level] = g[:rows, :cols] - (
            fields[7] * dx[:, :cols] + back_x + fields[8] * dy[:rows] + back_y
        )

    def some_levels(group, carry):
        for copy in level_copies(group, tracer_refs, held_ref, sems):
            copy.wait()
        for i in range(GROUP):
            one_level(group * GROUP + i)
        return carry

    lax.fori_loop(0, levels // GROUP, some_levels, 0)


def tracers(steric, every, fields, faces, token, tracer, fringe, side):
    levels, rows, cols = tracer[0].shape
    return pl.pallas_call(
        tracer_kernel,
        out_shape=(shape(levels, rows, cols), shape(rows, cols)),
        in_specs=[SCALAR] + [VMEM] * 4 + [HBM] * 5 + [VMEM] * 2,
        out_specs=(VMEM, VMEM),
        scratch_shapes=[pltpu.VMEM((7, levels, rows, cols), F32), pltpu.SemaphoreType.DMA((7 * levels // GROUP,))],
        compiler_params=params(20),
        name="tracer_steps",
    )(steric, every, fields, faces, token, *far(tracer), fringe, side)


def beside(cells, axis, step):
    count = lax.axis_size(axis)
    return lax.ppermute(cells, axis, [((i + step) % count, i) for i in range(count)])


def tracer_fields(keep, lam, zonal_1, merid_1, zonal_0, merid_0, mix_x, mix_y):
    flow_x, flow_y = 0.5 * zonal_1, 0.5 * merid_1
    past_x, past_y = 0.5 * zonal_0, 0.5 * merid_0
    return (
        lam,
        flow_x + mix_x,
        flow_x - mix_x,
        keep * (flow_y + mix_y),
        keep * (flow_y - mix_y),
        past_x - mix_x,
        keep * (past_y - mix_y),
        past_x + mix_x,
        keep * (past_y + mix_y),
    )


def surface_fields(keep, diag_ref, east_ref, north_ref, land_ref, rows):
    return diag_ref[rows], east_ref[rows], keep * north_ref[rows], land_ref[rows].astype(F32)


UP = (0, 1, 2, 3)
DOWN = (0, 1, 2, 3, 4, 6)
SIDE = (0, 1, 2, 3, 4, 5)


def kept(token_ref, first, count, rows, cols):
    last = jnp.concatenate([token_ref[0:1, :]] * (cols // LANES), axis=1)
    return jnp.where((iota((count, cols), 0) + first == rows - 1) & (last == 1.0), 0.0, 1.0)


def opening_kernel(capacity, token_ref, lam_ref, zonal_ref, merid_ref, mix_x_ref, mix_y_ref, *refs):
    surface_refs, (sla_ref, weight_ref), marks = refs[:4], refs[4:6], refs[6:9]
    up_ref, down_ref, next_ref, data_ref, place_ref, meta_ref = refs[9:15]
    held_ref, flat_ref, land_ref, segment_ref, mark_ref, sems, flat_sems, segment_sems, mark_sems = refs[15:]
    levels, rows, cols = lam_ref.shape
    blocks = mark_ref.shape[1]

    def started(source, target, sem):
        copy = pltpu.make_async_copy(source, target, sem)
        copy.start()
        return copy

    mark_copies = [started(ref, mark_ref.at[i], mark_sems.at[i]) for i, ref in enumerate(marks)]
    segment_copies = []
    for k in range(2):
        block = pl.ds(k * blocks * LANES // 2, blocks * LANES // 2)
        for i, ref in enumerate((sla_ref, weight_ref)):
            segment_copies.append(started(ref.at[block, :], segment_ref.at[i, block, :], segment_sems.at[2 * k + i]))
    copies, flat_copies = [], []
    for part, (first, outer) in enumerate(((0, 0), (rows - 8, rows - 2))):
        block = pl.ds(outer, 2)
        for source in (
            lam_ref.at[:, block, :],
            zonal_ref.at[1, :, block, :],
            merid_ref.at[1, :, block, :],
            mix_x_ref.at[:, block, :],
            mix_y_ref.at[:, block, :],
            merid_ref.at[0, :, block, :],
        )[: 5 + part]:
            copies.append(started(source, held_ref.at[len(copies)], sems.at[len(copies)]))
        block = pl.ds(first, 8)
        for i, ref in enumerate(surface_refs[:3]):
            flat_copies.append(started(ref.at[block, :], flat_ref.at[part, i], flat_sems.at[len(flat_copies)]))
        ref = surface_refs[3]
        flat_copies.append(started(ref.at[block, :], land_ref.at[part], flat_sems.at[len(flat_copies)]))
    next_ref[...] = token_ref[...]

    for copy in mark_copies:
        copy.wait()
    col_t, count_t = ranks(capacity, mark_ref[0], mark_ref[1], mark_ref[2], place_ref, meta_ref)
    for copy in copies + flat_copies:
        copy.wait()
    for part, (out_ref, picks, first, take) in enumerate(((up_ref, UP, 0, 0), (down_ref, DOWN, rows - 8, 6))):
        keep = kept(token_ref, first, 8, rows, cols)
        base = 2 * len(picks) * levels
        diag, east, north = [flat_ref[part, i] for i in range(3)]
        ocean = land_ref[part].astype(F32)
        for at, field in enumerate((diag, east, keep * north, ocean)):
            out_ref[base + 8 * at : base + 8 * at + 8, :] = field
        for level in range(levels):
            lam, zonal_1, merid_1, mix_x, mix_y, merid_0 = [held_ref[5 * part + min(i, 4 + part), level] for i in range(6)]
            fields = tracer_fields(keep[take : take + 2], lam, zonal_1, merid_1, zonal_1, merid_0, mix_x, mix_y)
            for at, pick in enumerate(picks):
                base = 2 * (at * levels + level)
                out_ref[base : base + 2, :] = fields[pick]
    for copy in segment_copies:
        copy.wait()
    for k in range(blocks):
        here = slice(k * LANES, (k + 1) * LANES)
        turned_rows(
            data_ref, k, segment_ref[1, here, :], segment_ref[0, here, :], col_t[:, k : k + 1], count_t[:, k : k + 1]
        )


def edge_rows(n_ref, s_ref, pick, levels, level, cols):
    zero = lambda count: jnp.zeros((count, cols), F32)
    north = zero(2)
    if pick in UP:
        base = 2 * (UP.index(pick) * levels + level)
        north = n_ref[base : base + 2, :]
    south = zero(2)
    if pick in DOWN:
        base = 2 * (DOWN.index(pick) * levels + level)
        south = s_ref[base : base + 2, :]
    return jnp.concatenate([north, zero(4), south], axis=0)


def halves(tall):
    lane = iota((tall.shape[0], LANES), 1)
    return jnp.where(lane < LANES // 2, tall[:, :LANES], tall[:, -LANES:])


def gathered(talls, width):
    lane = iota((talls[0].shape[0], LANES), 1)
    mixed = jnp.zeros((talls[0].shape[0], LANES), F32)
    for at, tall in enumerate(talls):
        mixed = jnp.where(lane // (2 * width) == at, pltpu.roll(halves(tall), width + 2 * width * at, 1), mixed)
    return mixed


def scattered(mixed, at, width):
    return pltpu.roll(mixed, LANES - width - 2 * width * at, 1)


TRACER_WIDTH = 2
FACE_WIDTH = 8


GROUP = 4


def level_copies(group, refs, held_ref, sems):
    lam_ref, zonal_ref, merid_ref, mix_x_ref, mix_y_ref = refs
    block = pl.ds(group * GROUP, GROUP)
    sources = (
        lam_ref.at[block],
        zonal_ref.at[1, block],
        merid_ref.at[1, block],
        zonal_ref.at[0, block],
        merid_ref.at[0, block],
        mix_x_ref.at[block],
        mix_y_ref.at[block],
    )
    return [
        pltpu.make_async_copy(source, held_ref.at[i, block], sems.at[7 * group + i]) for i, source in enumerate(sources)
    ]


def cols_kernel(token_ref, lam_ref, zonal_ref, merid_ref, mix_x_ref, mix_y_ref, *refs):
    surface_refs, height_refs, (n_ref, s_ref) = refs[:4], refs[4:6], refs[6:8]
    out_ref, fringe_ref, face_ref, height_ref, held_ref, flat_ref, sems = refs[8:]
    levels, rows, cols = lam_ref.shape
    tracer_refs = (lam_ref, zonal_ref, merid_ref, mix_x_ref, mix_y_ref)
    copies = []
    for group in range(levels // GROUP):
        copies += level_copies(group, tracer_refs, held_ref, sems)
    for copy in copies:
        copy.start()
    keep = kept(token_ref, 0, rows, rows, cols)
    high = rows + 8
    used = 2 * TRACER_WIDTH * len(SIDE)
    blocks = levels * high // LANES
    base = blocks * used
    up, down = 2 * len(UP) * levels, 2 * len(DOWN) * levels
    talls = []
    for at, field in enumerate(surface_fields(keep, *surface_refs, slice(0, rows))):
        tall = jnp.concatenate(
            [field, n_ref[up + 8 * at : up + 8 * at + 8, :], s_ref[down + 8 * at : down + 8 * at + 8, :]], axis=0
        )
        face_ref[at] = tall
        talls.append(tall)
    for at, ref in enumerate(height_refs):
        height_ref[at] = ref[...]
        talls.append(jnp.concatenate([ref[...], jnp.zeros((16, cols), F32)], axis=0))
    out_ref[base : base + rows + 16, :] = gathered(talls, FACE_WIDTH)
    for level in range(levels):
        if level % GROUP == 0:
            for copy in copies[7 * (level // GROUP) : 7 * (level // GROUP) + 7]:
                copy.wait()
        fields = tracer_fields(keep, *[held_ref[i, level] for i in range(7)])
        talls = []
        for pick, field in enumerate(fields[:7]):
            edge = edge_rows(n_ref, s_ref, pick, levels, level, cols)
            fringe_ref[level, pick] = edge
            if pick in SIDE:
                talls.append(jnp.concatenate([field, edge], axis=0))
        flat_ref[level * high : (level + 1) * high, :] = gathered(talls, TRACER_WIDTH)
    for b in range(blocks):
        turned = jnp.transpose(flat_ref[b * LANES : (b + 1) * LANES, :])
        out_ref[b * used : (b + 1) * used, :] = turned[:used]


def side_kernel(strip_ref, token_ref, side_ref, next_ref, flat_ref):
    next_ref[...] = token_ref[...]
    levels, high = side_ref.shape[1:3]
    used = 2 * TRACER_WIDTH * len(SIDE)
    blocks = levels * high // LANES
    for b in range(blocks):
        both = strip_ref[b * used : (b + 1) * used, :]
        both = jnp.concatenate([both, jnp.zeros((LANES - used, LANES), F32)], axis=0)
        flat_ref[b * LANES : (b + 1) * LANES, :] = jnp.transpose(both)
    for level in range(levels):
        mixed = flat_ref[level * high : (level + 1) * high, :]
        for at in range(len(SIDE)):
            side_ref[at, level] = scattered(mixed, at, TRACER_WIDTH)


def face_halo_kernel(base, token_ref, tall_ref, height_ref, e_ref, w_ref, face_ref, full_ref, strip_ref):
    from_west = iota((base, LANES), 0) % (2 * TRACER_WIDTH) < TRACER_WIDTH
    strip_ref[...] = jnp.where(from_west, w_ref[0:base, :], e_ref[0:base, :])
    high = tall_ref.shape[1]
    rows = height_ref.shape[1]
    for at in range(2):
        full_ref[at, :, : -LANES] = height_ref[at]
    western = iota((high, LANES), 1) % (2 * FACE_WIDTH) < FACE_WIDTH
    here = slice(base, base + high)
    mixed = jnp.where(western, w_ref[here, :], e_ref[here, :])
    for at in range(2):
        full_ref[at, :, -LANES:] = scattered(mixed, 4 + at, FACE_WIDTH)[:rows]
    full = [jnp.concatenate([tall_ref[at], scattered(mixed, at, FACE_WIDTH)], axis=1) for at in range(4)]
    diag, east, north, ocean = full
    west, south = pltpu.roll(east, 1, 1), pltpu.roll(north, 1, 0)
    face_ref[0] = (1.0 + diag) + east + west + north + south
    for at, field in enumerate((east, west, north, south, ocean)):
        face_ref[1 + at] = field


def opening(token, tracer, surface, segments, marks, capacity):
    levels, rows, cols = tracer[0].shape
    up, down = 2 * len(UP) * levels + 32, 2 * len(DOWN) * levels + 32
    blocks = segments[0].shape[0] // LANES
    marks = tuple(mark.reshape(blocks, LANES) for mark in marks)
    return pl.pallas_call(
        functools.partial(opening_kernel, capacity),
        out_shape=(
            shape(up, cols),
            shape(down, cols),
            shape(*token.shape),
            jax.ShapeDtypeStruct((blocks * LANES, 4 * LANES), BF16),
            jax.ShapeDtypeStruct((blocks, LANES), jnp.int32),
            shape(LANES, LANES),
        ),
        in_specs=[VMEM] + [HBM] * 14,
        out_specs=(VMEM,) * 6,
        scratch_shapes=[
            pltpu.VMEM((11, levels, 2, cols), F32),
            pltpu.VMEM((2, 3, 8, cols), F32),
            pltpu.VMEM((2, 8, cols), jnp.int32),
            pltpu.VMEM((2, blocks * LANES, LANES), F32),
            pltpu.VMEM((3, blocks, LANES), jnp.int32),
            pltpu.SemaphoreType.DMA((11,)),
            pltpu.SemaphoreType.DMA((8,)),
            pltpu.SemaphoreType.DMA((4,)),
            pltpu.SemaphoreType.DMA((3,)),
        ],
        compiler_params=params(12),
        name="opening",
    )(token, *far(tracer), *far(surface), *far(segments), *far(marks))


def edges_to_tx(token, tracer, surface, heights, north, south):
    levels, rows, cols = tracer[0].shape
    high = rows + 8
    side_rows = 2 * TRACER_WIDTH * len(SIDE) * levels * high // LANES + rows + 16
    sides, fringe, faces, heights = pl.pallas_call(
        cols_kernel,
        out_shape=(
            shape(side_rows, LANES),
            shape(levels, 7, 8, cols),
            shape(4, rows + 16, cols),
            shape(2, rows, cols),
        ),
        in_specs=[VMEM] + [HBM] * 5 + [VMEM] * 8,
        out_specs=(VMEM,) * 4,
        scratch_shapes=[
            pltpu.VMEM((7, levels, rows, cols), F32),
            pltpu.VMEM((levels * high, LANES), F32),
            pltpu.SemaphoreType.DMA((7 * levels // GROUP,)),
        ],
        compiler_params=params(24),
        name="edge_columns",
    )(token, *far(tracer), *far(surface), *far(heights), north, south)
    return (beside(sides, "tx", 1), beside(sides, "tx", -1)), fringe, faces, heights


def faces_with_halo(token, tall, heights, east, west):
    count, high, cols = tall.shape
    base = east.shape[0] - high
    return pl.pallas_call(
        functools.partial(face_halo_kernel, base),
        out_shape=(shape(6, high, cols + LANES), shape(2, heights.shape[1], cols + LANES), shape(base, LANES)),
        in_specs=[VMEM] * 5,
        out_specs=(VMEM,) * 3,
        compiler_params=params(6),
        name="surface_halos",
    )(token, tall, heights, east, west)


def tracer_sides(token, strips, levels, rows):
    high = rows + 8
    return pl.pallas_call(
        side_kernel,
        out_shape=(shape(len(SIDE), levels, high, LANES), shape(*token.shape)),
        in_specs=[VMEM] * 2,
        out_specs=(VMEM, VMEM),
        scratch_shapes=[pltpu.VMEM((levels * high, LANES), F32)],
        compiler_params=params(8),
        name="tracer_halos",
    )(strips, token)


def on_device(
    lam_tracer,
    lam_eta,
    land,
    zonal_flow,
    merid_flow,
    zonal_mixing,
    merid_mixing,
    surface_east,
    surface_north,
    surface_diag,
    steric,
    eta_saved,
    obs_sla,
    obs_weight,
    obs_tile,
    obs_start,
    obs_count,
):
    levels, rows, cols = lam_tracer.shape
    n_rows = lax.axis_size("ty")
    devices = n_rows * lax.axis_size("tx")
    capacity = 2 * obs_sla.shape[0] // devices
    token = jnp.full((8, LANES), lax.axis_index("ty") == n_rows - 1, F32)
    tracer = (lam_tracer, zonal_flow, merid_flow, zonal_mixing, merid_mixing)
    surface = (surface_diag, surface_east, surface_north, land)
    to_south, to_north, token, *ranked = opening(
        token, tracer, surface, (obs_sla, obs_weight), (obs_tile, obs_start, obs_count), capacity
    )
    around_ty = beside(to_south, "ty", 1), beside(to_north, "ty", -1)
    sent, token = placed(*ranked, token, capacity, devices // n_rows)
    sent, *around_ty = lax.optimization_barrier((sent, *around_ty))
    got = lax.all_to_all(
        sent.reshape(devices, 1, -1), AXES, split_axis=0, concat_axis=0, tiled=True
    ).reshape(sent.shape)
    around_tx, fringe, faces, heights = edges_to_tx(token, tracer, surface, (lam_eta, eta_saved), *around_ty)
    faces, heights, strips = faces_with_halo(token, faces, heights, *around_tx)
    rhs, token = unpack(got, heights, faces, token, capacity)
    north, south = beside(rhs[:8], "ty", 1), beside(rhs[-8:], "ty", -1)
    sides, token = tracer_sides(token, strips, levels, rows)
    mine, krylov_fields = sums(rhs, north, south, faces, token)
    every = lax.all_to_all(
        mine.reshape(devices, 1, LANES), AXES, split_axis=0, concat_axis=0, tiled=True
    ).reshape(devices, LANES)
    return tracers(steric, every, krylov_fields, faces, token, tracer, fringe, sides)


def solution(mesh):
    in_specs = (
        P(None, "ty", "tx"),
        P("ty", "tx"),
        P("ty", "tx"),
        P(None, None, "ty", "tx"),
        P(None, None, "ty", "tx"),
        P(None, "ty", "tx"),
        P(None, "ty", "tx"),
        P("ty", "tx"),
        P("ty", "tx"),
        P("ty", "tx"),
        P(),
        P("ty", "tx"),
        P(AXES, None),
        P(AXES, None),
        P(AXES, None),
        P(AXES),
        P(AXES),
    )
    out_specs = (P(None, "ty", "tx"), P("ty", "tx"))
    return jax.shard_map(
        on_device, mesh=mesh, in_specs=in_specs, out_specs=out_specs, check_vma=False
    )
```
